32 devices in a mesh: fsdp: 4 (over y, x), ctx: 2 (over core), tp: 4 (over z).
Axes of the slice: x: 2, y: 2, z: 4, core: 2. Of those that a mesh axis runs over, the one named last changes fastest.
Arguments:
- inputs: bfloat16 [4, 1536, 768], P('fsdp', 'ctx'), may hold values from -6 to 6
- cotangent: bfloat16 [4, 1536, 768], P('fsdp', 'ctx'), may hold values from -6 to 6
- segments: int32 [4, 1536], P('fsdp', 'ctx'), may hold values from 0 to 15, never falling along the last dimension, each value on 1 to 768 neighbouring positions
- gains: float32 [3, 768], replicated, may hold values from 0.5 to 1.5
- last_gain: float32 [768], replicated, may hold values from 0.5 to 1.5
- in_weight: bfloat16 [2, 3, 768, 768], P(None, None, 'fsdp', 'tp'), may hold values from -0.21875 to 0.21875
- h3_out: bfloat16 [768, 768], P('tp', 'fsdp'), may hold values from -0.0546875 to 0.0546875
- attn_out: bfloat16 [768, 768], P('tp', 'fsdp'), may hold values from -0.875 to 0.875
- up_weight: bfloat16 [2, 768, 3072], P(None, 'fsdp', 'tp'), may hold values from -0.21875 to 0.21875
- down_weight: bfloat16 [2, 3072, 768], P(None, 'tp', 'fsdp'), may hold values from -0.109375 to 0.109375
- shift_taps: float32 [64, 768], P(None, 'tp'), may hold values from -1.5 to 1.5
- decay_rate: float32 [12, 64], P('tp'), may hold values from 3.2552085e-05 to 0.1
Outputs:
- output: bfloat16 [4, 1536, 768], P('fsdp', 'ctx')
- input_grad: float32 [4, 1536, 768], P('fsdp', 'ctx')
- gains_grad: float32 [3, 768], P(None, 'fsdp')
- last_gain_grad: float32 [768], P('fsdp')
- in_grad: float32 [2, 3, 768, 768], P(None, None, 'fsdp', 'tp')
- h3_out_grad: float32 [768, 768], P('tp', 'fsdp')
- attn_out_grad: float32 [768, 768], P('tp', 'fsdp')
- up_grad: float32 [2, 768, 3072], P(None, 'fsdp', 'tp')
- down_grad: float32 [2, 3072, 768], P(None, 'tp', 'fsdp')
- taps_grad: float32 [64, 768], P('fsdp', 'tp')
- rate_grad: float32 [12, 64], P('tp', 'fsdp')
The draws below stay inside these ranges and needn't reach their ends.
Inputs may be any that keep to these rules, and one draw needn't show every extreme that they name: `segments`: within a sequence the ids never fall along the positions, start at 0 and take every value up to 15; no document has more than 768 positions, and one has exactly that many.
All inputs are finite; a program needn't handle non-finite values.
Results may differ from the reference program's by a relative error of at most 0.03.
Values may be sent and summed in bfloat16 or wider, within the bound.
No kernel may reach another device: no remote copies, remote signals or barrier semaphores. Data moves between devices by JAX's collectives and lax.ppermute only.
A program may use at most 192 MiB of HBM per device.

```python
import math
import jax
import jax.numpy as jnp
import numpy as np
from jax import lax

D = 768
HEADS = 12
HEAD_DIM = 64
FF = 3072
SHIFT = 64
DOCS = 16
SEQS = 4
SEQ_LEN = 1536


def levels(stream_key, dims, cuts, low, largest):
    factor_of = 1.0
    for dim, shards_of in cuts:
        steps = jax.random.uniform(jax.random.fold_in(jax.random.fold_in(stream_key, 6), dim), (shards_of,), jnp.float32, low / len(cuts), largest / len(cuts))
        factor_of = factor_of * jnp.repeat(jnp.exp(steps), dims[dim] // shards_of).reshape((-1,) + (1,) * (len(dims) - 1 - dim))
    return factor_of


def profile(amount, total, reach, skew):
    portions = [(1 << 20) // math.isqrt(rank ** skew) + 1 for rank in range(2, amount + 1)]
    spare, holding = total - reach - (amount - 1), [1] * (amount - 1)
    while spare > 0:
        movable = [i for i in range(amount - 1) if holding[i] < reach]
        pool, budget = sum([portions[i] for i in movable]), spare
        for i in movable:
            addition = min(reach - holding[i], max(1, budget * portions[i] // pool), spare)
            holding[i] = holding[i] + addition
            spare = spare - addition
    return np.array([reach] + holding)


def uneven_parts(rng, number_of, total, reach, skew):
    if number_of == 2:
        one = jax.random.randint(rng, (), max(1, total - reach), min(reach, total - 1) + 1)
        return jnp.stack([one, total - one])
    lengths = jnp.asarray(profile(number_of, total, reach, skew), jnp.int32)
    twos = (number_of - 1) // 2
    source_of, taker = lengths[1:1 + 2 * twos:2], lengths[2:2 + 2 * twos:2]
    room = jnp.minimum(source_of - 1, reach - taker)
    passed = jax.random.randint(jax.random.fold_in(rng, 1), (twos,), 0, 1 << 20) % (room + 1)
    lengths = lengths.at[1:1 + 2 * twos:2].set(source_of - passed).at[2:2 + 2 * twos:2].set(taker + passed)
    return lengths[jax.random.permutation(jax.random.fold_in(rng, 2), number_of)]


def gaussian(own_key, dims, deviation, bound, cuts=(), kind=jnp.bfloat16):
    entries = jax.random.normal(own_key, dims, jnp.float32) * deviation
    if len(cuts) > 0:
        entries = levels(own_key, dims, cuts, -0.22, 0.18) * entries
    return jnp.clip(entries, min=-bound, max=bound).astype(kind)


def setup_inputs(seed: int = 0) -> dict:
    splits = jax.random.split(jax.random.key(seed), 13)
    return {
        "inputs": gaussian(splits[0], (SEQS, SEQ_LEN, D), 1.0, 6.0, ((0, 4), (1, 2))),
        "cotangent": gaussian(splits[1], (SEQS, SEQ_LEN, D), 1.0, 6.0, ((0, 4), (1, 2))),
        "segments": jax.vmap(lambda own: jnp.searchsorted(jnp.cumsum(uneven_parts(own, DOCS, SEQ_LEN, SEQ_LEN // 2, 2)), jnp.arange(SEQ_LEN), side="right"))(jax.random.split(splits[2], SEQS)).reshape((SEQS, SEQ_LEN)).astype(jnp.int32),
        "gains": jnp.clip(1.0 + 0.1 * jax.random.normal(splits[3], (3, D), jnp.float32), 0.5, 1.5),
        "last_gain": jnp.clip(1.0 + 0.1 * jax.random.normal(splits[4], (D,), jnp.float32), 0.5, 1.5),
        "in_weight": gaussian(splits[5], (2, 3, D, D), D ** -0.5, 0.21875, ((2, 4), (3, 4))),
        "h3_out": gaussian(splits[6], (D, D), (D * 16) ** -0.5, 0.0546875, ((0, 4), (1, 4))),
        "attn_out": gaussian(splits[7], (D, D), (D // 16) ** -0.5, 0.875, ((0, 4), (1, 4))),
        "up_weight": gaussian(splits[8], (2, D, FF), D ** -0.5, 0.21875, ((1, 4), (2, 4))),
        "down_weight": gaussian(splits[9], (2, FF, D), FF ** -0.5, 0.109375, ((1, 4), (2, 4))),
        "shift_taps": gaussian(splits[10], (SHIFT, D), (2 * SHIFT ** -0.5), 1.5, ((1, 4),), jnp.float32),
        "decay_rate": jnp.clip(jnp.exp(math.log(0.1) - 8.030084 * jax.random.uniform(splits[11], (HEADS, HEAD_DIM), jnp.float32) ** levels(splits[11], (HEADS, HEAD_DIM), ((0, 4),), -0.2, 0.2)), 3.255208503105678e-05, 0.1),
    }


highest_score = lax.Precision.HIGHEST
epsilon = 1e-05
masked_low = -1e+30

@jax.custom_vjp
def low(v):
    return lax.optimization_barrier(v.astype(jnp.bfloat16)).astype(jnp.float32)

@jax.custom_vjp
def low_back(v):
    return v

def low_keep(v):
    return (low(v), None)

def low_pass(kept, grad):
    return (grad,)

def back_keep(v):
    return (v, None)

def back_low(kept, grad):
    return (low(grad),)
low.defvjp(low_keep, low_pass)
low_back.defvjp(back_keep, back_low)

def low_both(values):
    return low_back(low(values))

def layer_norm(residual, gain_row):
    center = lax.optimization_barrier(jnp.mean(residual, axis=-1, keepdims=True))
    shifted = residual - center
    spread = lax.optimization_barrier(jnp.mean(shifted * shifted, axis=-1, keepdims=True))
    return shifted * lax.rsqrt(spread + epsilon) * gain_row

def shift_mix(key_ext, seg_ext, tap_weights):
    tap_count = tap_weights.shape[0]
    row_count = key_ext.shape[0] - tap_count + 1
    seg_now = seg_ext[tap_count - 1:]
    running = jnp.zeros((row_count, key_ext.shape[1]), jnp.float32)
    for tap_index in range(tap_count):
        begin = tap_count - 1 - tap_index
        moved_rows = key_ext[begin:begin + row_count]
        same_doc = (seg_ext[begin:begin + row_count] == seg_now).astype(jnp.float32)
        running = running + moved_rows * same_doc[:, None] * tap_weights[tap_index][None, :]
    return running

def decay_blocks(queries, shifted, values, decay_rate, seg_here, entry_seg):
    row_count, head_count, key_width = queries.shape
    block_rows = min(128, row_count)
    block_count = row_count // block_rows
    positions = jnp.arange(block_rows, dtype=jnp.float32)
    middle = 0.5 * block_rows
    log_keep = -decay_rate
    rise_amount = jnp.exp(log_keep[None] * (positions[:, None, None] + 1.0))
    query_fac = jnp.exp(log_keep[None] * (positions[:, None, None] - middle))
    key_fac = jnp.exp(log_keep[None] * (middle - positions[:, None, None]))
    tail_factor = jnp.exp(log_keep[None] * (block_rows - 1.0 - positions[:, None, None]))
    whole_fac = jnp.exp(log_keep * block_rows)
    causal = positions[:, None] >= positions[None, :]

    def one_block(carry, block_in):
        current_state, factor_now, seg_before = carry
        query_block_rows, key_block_rows, value_block_rows, seg_b = block_in
        carried_state = (seg_b == seg_before).astype(jnp.float32)
        block_result = jnp.einsum('qlm,lmp->qlp', query_block_rows * rise_amount * carried_state[:, None, None], current_state, precision=highest_score)
        scores = jnp.einsum('thk,shk->hts', query_block_rows * query_fac, key_block_rows * key_fac, precision=highest_score)
        allowed = causal & (seg_b[:, None] == seg_b[None, :])
        scores = jnp.where(allowed[None], scores, 0.0)
        block_result = block_result + jnp.einsum('hts,shv->thv', scores, value_block_rows, precision=highest_score)
        seg_last = seg_b[block_rows - 1]
        keep_on = (seg_last == seg_before).astype(jnp.float32)
        input_final = (seg_b == seg_last).astype(jnp.float32)
        added_term = jnp.einsum('zct,zcy->cty', key_block_rows * tail_factor * input_final[:, None, None], value_block_rows, precision=highest_score)
        current_state = (whole_fac * keep_on)[:, :, None] * current_state + added_term
        factor_now = factor_now * whole_fac * keep_on
        return ((current_state, factor_now, seg_last), block_result)
    start_carry = (jnp.zeros((head_count, key_width, values.shape[2]), jnp.float32), jnp.ones((head_count, key_width), jnp.float32), entry_seg)
    blocks_in = (queries.reshape(block_count, block_rows, head_count, key_width), shifted.reshape(block_count, block_rows, head_count, key_width), values.reshape(block_count, block_rows, head_count, -1), seg_here.reshape(block_count, block_rows))
    (state_end, factor_end, seg_final), outs = lax.scan(jax.checkpoint(one_block), start_carry, blocks_in)
    return (outs.reshape(row_count, head_count, -1), factor_end, state_end)

def h3_local(queries, key_ext, values, tap_weights, decay_rate, seg_ext, seg_here, entry_seg):
    shifted = shift_mix(key_ext, seg_ext, tap_weights)
    row_count = queries.shape[0]
    head_count = decay_rate.shape[0]
    scaled_values = queries * HEAD_DIM ** (-0.5)
    return decay_blocks(scaled_values.reshape(row_count, head_count, -1), shifted.reshape(row_count, head_count, -1), values.reshape(row_count, head_count, -1), decay_rate, seg_here, entry_seg)

def h3_mixer(normed, proj_in, tap_weights, decay_rate, seg_here):
    triple = low_both(jnp.einsum('td,jdc->jtc', normed, proj_in, precision=highest_score))
    tap_count = tap_weights.shape[0]
    seq_rows = normed.shape[0]
    key_ext = jnp.concatenate([jnp.zeros((tap_count - 1, triple.shape[2]), jnp.float32), triple[1]])
    seg_ext = jnp.concatenate([jnp.zeros((tap_count - 1,), jnp.int32), seg_here])
    mixer_out, factor_end, state_end = h3_local(triple[0], key_ext, triple[2], tap_weights, decay_rate, seg_ext, seg_here, jnp.int32(0))
    return low(mixer_out.reshape(seq_rows, -1))

def attend(normed, proj_in, seg_here):
    triple = low_both(jnp.einsum('td,jdc->jtc', normed, proj_in, precision=highest_score))
    seq_rows, channels = (normed.shape[0], triple.shape[2])
    head_count = channels // HEAD_DIM
    query_h = triple[0].reshape(seq_rows, head_count, HEAD_DIM)
    key_h = triple[1].reshape(seq_rows, head_count, HEAD_DIM)
    value_h = triple[2].reshape(seq_rows, head_count, HEAD_DIM)
    key_pos = jnp.arange(seq_rows, dtype=jnp.int32)
    block_rows = min(512, seq_rows)

    def one_block(start_row):
        query_block_rows = lax.dynamic_slice_in_dim(query_h, start_row, block_rows, 0)
        seg_b = lax.dynamic_slice_in_dim(seg_here, start_row, block_rows, 0)
        query_pos = start_row + jnp.arange(block_rows, dtype=jnp.int32)
        scores = low_back(jnp.einsum('thd,shd->hts', query_block_rows, key_h, precision=highest_score) * HEAD_DIM ** (-0.5))
        allowed = ((key_pos[None, :] <= query_pos[:, None]) & (seg_here[None, :] == seg_b[:, None]))[None]
        masked = jnp.where(allowed, scores, masked_low)
        row_top = lax.optimization_barrier(jnp.max(masked, axis=-1, keepdims=True))
        expo = jnp.exp(masked - row_top)
        row_total = lax.optimization_barrier(jnp.sum(expo, axis=-1))
        numer = low_back(jnp.einsum('hts,shd->thd', low(expo), value_h, precision=highest_score))
        return numer / row_total.T[:, :, None]
    starts = jnp.arange(0, seq_rows, block_rows, dtype=jnp.int32)
    outs = lax.map(jax.checkpoint(one_block), starts)
    return low_both(outs.reshape(seq_rows, channels))

def feed(residual, gain_row, proj_up, proj_down):
    normed = low(layer_norm(residual, gain_row))
    up_values = low_back(jnp.dot(normed, proj_up, precision=highest_score))
    hidden = low(jax.nn.gelu(up_values, approximate=True))
    return low_back(jnp.dot(hidden, proj_down, precision=highest_score))

def reference(inputs, cotangent, segments, gains, last_gain, in_weight, h3_out, attn_out, up_weight, down_weight, shift_taps, decay_rate):

    def forward(rows_all, gains_f, last_f, in_f, h3_f, attn_f, up_f, down_f, taps_f, rate_f):

        def one_sequence(pair_in):
            residual, seg_raw = pair_in
            seg_here = seg_raw + 1
            normed = low(layer_norm(residual, gains_f[0]))
            mixed = h3_mixer(normed, in_f[0], taps_f, rate_f, seg_here)
            residual = residual + low_back(jnp.dot(mixed, h3_f, precision=highest_score))
            residual = residual + feed(residual, gains_f[1], up_f[0], down_f[0])
            normed = low(layer_norm(residual, gains_f[2]))
            mixed = attend(normed, in_f[1], seg_here)
            residual = residual + low_back(jnp.dot(mixed, attn_f, precision=highest_score))
            return residual + feed(residual, last_f, up_f[1], down_f[1])
        return lax.map(one_sequence, (rows_all, segments))
    primals = (inputs.astype(jnp.float32), gains.astype(jnp.float32), last_gain.astype(jnp.float32), in_weight.astype(jnp.float32), h3_out.astype(jnp.float32), attn_out.astype(jnp.float32), up_weight.astype(jnp.float32), down_weight.astype(jnp.float32), shift_taps.astype(jnp.float32), decay_rate.astype(jnp.float32))
    result, pullback = jax.vjp(forward, *primals)
    grads = pullback(cotangent.astype(jnp.float32))
    return (result.astype(jnp.bfloat16), grads[0], grads[1], grads[2], grads[3], grads[4], grads[5], grads[6], grads[7], grads[8], grads[9])
```

```python
import functools

import jax
import jax.numpy as jnp
from jax import lax
from jax.experimental import pallas as pl
from jax.experimental.pallas import tpu as pltpu
from jax.sharding import PartitionSpec as P

HEAD_DIM = 64
epsilon = 1e-05
masked_low = -1e30
bf16 = jnp.bfloat16
f32 = jnp.float32
scale = HEAD_DIM ** (-0.5)
CHUNK = 256
LIMIT = 56 * 1024 * 1024


def nn(a, b):
    return lax.dot_general(a, b, (((1,), (0,)), ((), ())), preferred_element_type=f32)


def nt(a, b):
    return lax.dot_general(a, b, (((1,), (1,)), ((), ())), preferred_element_type=f32)


def tn(a, b):
    return lax.dot_general(a, b, (((0,), (0,)), ((), ())), preferred_element_type=f32)


def head_masks(rows, channels):
    lane = lax.broadcasted_iota(jnp.int32, (rows, channels), 1)
    return [(lane >= HEAD_DIM * h) & (lane < HEAD_DIM * (h + 1)) for h in range(channels // HEAD_DIM)]


def same_head(channels):
    row = lax.broadcasted_iota(jnp.int32, (channels, channels), 0) // HEAD_DIM
    lane = lax.broadcasted_iota(jnp.int32, (channels, channels), 1) // HEAD_DIM
    return row == lane


def call(kernel, outs, scratch=(), smem=0, n_in=0, flops=0, nbytes=0):
    vm = pl.BlockSpec(memory_space=pltpu.VMEM)
    sm = pl.BlockSpec(memory_space=pltpu.SMEM)
    return pl.pallas_call(
        kernel,
        out_shape=[jax.ShapeDtypeStruct(s, d) for s, d in outs],
        in_specs=[sm] * smem + [vm] * n_in,
        out_specs=[vm] * len(outs),
        scratch_shapes=list(scratch),
        compiler_params=pltpu.CompilerParams(vmem_limit_bytes=LIMIT),
        cost_estimate=pl.CostEstimate(flops=int(flops), bytes_accessed=int(nbytes), transcendentals=0),
    )


def rolled_down(ext_ref, copies, rows):
    for r in range(8):
        copies[r, 8:rows, :] = ext_ref[8 - r : rows - r, :]


def shift_kernel(taps_n, key_ref, halo_ref, taps_ref, age_ref, tail_ref, value_ref, ks_ref, st_ref, ext, copies):
    rows, channels = key_ref.shape
    ext[0:taps_n, :] = halo_ref[...].astype(f32)
    ext[taps_n : taps_n + rows, :] = key_ref[...].astype(f32)
    rolled_down(ext, copies, rows + taps_n)

    def block(b, carry):
        start = pl.multiple_of(b * 64, 64)
        age = age_ref[pl.ds(start, 64), :]
        acc = jnp.zeros((64, channels), f32)
        for m in range(taps_n // 8):
            for r in range(8):
                j = 8 * m + r
                moved = copies[r, pl.ds(start + taps_n - 8 * m, 64), :]
                acc = acc + jnp.where(age >= j, moved, 0.0) * taps_ref[j : j + 1, :]
        ks_ref[pl.ds(start, 64), :] = acc
        return carry

    lax.fori_loop(0, rows // 64, block, 0)
    kt = (ks_ref[...] * tail_ref[...]).astype(bf16)
    st_ref[...] = jnp.where(same_head(channels), tn(value_ref[...], kt), 0.0)


def shift_forward(key, halo, taps, age, tail, value):
    rows, channels = key.shape
    taps_n = taps.shape[0]
    return call(
        functools.partial(shift_kernel, taps_n),
        [((rows, channels), f32), ((channels, channels), f32)],
        [pltpu.VMEM((rows + taps_n, channels), f32), pltpu.VMEM((8, rows + taps_n, channels), f32)],
        n_in=6,
        flops=4 * rows * channels * taps_n * 20,
        nbytes=4e6,
    )(key, halo, taps, age, tail, value)


def decay_factors(rate_row, rows):
    pos = lax.broadcasted_iota(jnp.int32, (rows, rate_row.shape[1]), 0).astype(f32)
    mid = 0.5 * rows
    q_fac = jnp.exp(-rate_row * (pos - mid))
    k_fac = jnp.exp(rate_row * (pos - mid))
    rise = jnp.exp(-rate_row * (pos + 1.0))
    tail = jnp.exp(-rate_row * (rows - 1.0 - pos))
    whole = jnp.exp(-rate_row * rows)
    return pos, mid, q_fac, k_fac, rise, tail, whole


def h3_kernel(q_ref, ks_ref, v_ref, sin_ref, rate_ref, segc_ref, segr_ref, entry_ref, y_ref, save_ref):
    rows, channels = q_ref.shape
    blocks = rows // CHUNK
    _, _, q_fac, k_fac, rise, tail, whole = decay_factors(rate_ref[...], CHUNK)
    heads = head_masks(CHUNK, channels)
    block_diag = same_head(channels)
    causal = lax.broadcasted_iota(jnp.int32, (CHUNK, CHUNK), 0) >= lax.broadcasted_iota(
        jnp.int32, (CHUNK, CHUNK), 1
    )
    state = sin_ref[...]
    for b in range(blocks):
        sl = slice(b * CHUNK, (b + 1) * CHUNK)
        seg_c = segc_ref[sl, :]
        seg_r = segr_ref[:, sl]
        before = entry_ref[...] if b == 0 else segc_ref[b * CHUNK - 1 : b * CHUNK, :]
        last = segc_ref[(b + 1) * CHUNK - 1 : (b + 1) * CHUNK, :]
        carried = (seg_c == before).astype(f32)
        final = (seg_c == last).astype(f32)
        keep = (last == before).astype(f32)
        q = q_ref[sl, :].astype(f32) * scale
        k = ks_ref[sl, :]
        v = v_ref[sl, :]
        qf = (q * q_fac).astype(bf16)
        kf = (k * k_fac).astype(bf16)
        qr = (q * (rise * carried)).astype(bf16)
        kt = (k * (tail * final)).astype(bf16)
        allowed = causal & (seg_c == seg_r)
        save_ref[b, :, :] = state
        y = nt(qr, state.astype(bf16))
        for hm in heads:
            scores = nt(jnp.where(hm, qf, jnp.zeros_like(qf)), kf)
            scores = jnp.where(allowed, scores, 0.0).astype(bf16)
            y = y + jnp.where(hm, nn(scores, v), 0.0)
        y_ref[sl, :] = y.astype(bf16)
        state = state * (whole * keep) + jnp.where(block_diag, tn(v, kt), 0.0)


def h3_forward_call(q, ks, v, state_in, rate_row, seg_col, seg_row, entry):
    rows, channels = q.shape
    return call(
        h3_kernel,
        [((rows, channels), bf16), ((rows // CHUNK, channels, channels), f32)],
        n_in=8,
        flops=3e9,
        nbytes=3e6,
    )(q, ks, v, state_in, rate_row, seg_col, seg_row, entry)


def h3_back_kernel(
    taps_n,
    q_ref,
    ks_ref,
    v_ref,
    dy_ref,
    save_ref,
    dst_ref,
    rate_ref,
    segc_ref,
    segr_ref,
    entry_ref,
    key_ref,
    halo_ref,
    taps_ref,
    age_ref,
    rem_ref,
    dq_ref,
    dk_ref,
    dv_ref,
    dtaps_ref,
    drate_ref,
    ext,
    copies,
    dext,
    dcopies,
    tap_acc,
):
    rows, channels = q_ref.shape
    blocks = rows // CHUNK
    pos, mid, q_fac, k_fac, rise, tail, whole = decay_factors(rate_ref[...], CHUNK)
    heads = head_masks(CHUNK, channels)
    block_diag = same_head(channels)
    row = lax.broadcasted_iota(jnp.int32, (CHUNK, CHUNK), 0)
    lane = lax.broadcasted_iota(jnp.int32, (CHUNK, CHUNK), 1)
    dstate = dst_ref[...]
    drate = jnp.zeros((1, channels), f32)
    dext[0:taps_n, :] = jnp.zeros((taps_n, channels), f32)
    dext[rows + taps_n : rows + 2 * taps_n, :] = jnp.zeros((taps_n, channels), f32)
    for b in reversed(range(blocks)):
        sl = slice(b * CHUNK, (b + 1) * CHUNK)
        seg_c = segc_ref[sl, :]
        seg_r = segr_ref[:, sl]
        before = entry_ref[...] if b == 0 else segc_ref[b * CHUNK - 1 : b * CHUNK, :]
        last = segc_ref[(b + 1) * CHUNK - 1 : (b + 1) * CHUNK, :]
        carried = (seg_c == before).astype(f32)
        final = (seg_c == last).astype(f32)
        keep = (last == before).astype(f32)
        q = q_ref[sl, :].astype(f32) * scale
        k = ks_ref[sl, :]
        v = v_ref[sl, :]
        dy = dy_ref[sl, :].astype(bf16)
        qf = (q * q_fac).astype(bf16)
        kf = (k * k_fac).astype(bf16)
        rise_c = rise * carried
        tail_c = tail * final
        qr = (q * rise_c).astype(bf16)
        kt = (k * tail_c).astype(bf16)
        same = seg_c == seg_r
        low_mask = (row >= lane) & same
        up_mask = (row <= lane) & same
        state = save_ref[b, :, :]
        dstate_b = dstate.astype(bf16)
        dqf = jnp.zeros((CHUNK, channels), f32)
        dkf = jnp.zeros((CHUNK, channels), f32)
        dv = nt(kt, dstate_b)
        zero = jnp.zeros_like(qf)
        for hm in heads:
            kh = jnp.where(hm, kf, zero)
            vh = jnp.where(hm, v, zero)
            scores_t = jnp.where(up_mask, nt(kh, qf), 0.0).astype(bf16)
            dv = dv + jnp.where(hm, nn(scores_t, dy), 0.0)
            dsc = jnp.where(low_mask, nt(dy, vh), 0.0).astype(bf16)
            dsc_t = jnp.where(up_mask, nt(vh, dy), 0.0).astype(bf16)
            dqf = dqf + nn(dsc, kh)
            dkf = dkf + jnp.where(hm, nn(dsc_t, qf), 0.0)
        dqr = nn(dy, state.astype(bf16))
        dkt = nn(v, dstate_b)
        dq_ref[sl, :] = ((dqf * q_fac + dqr * rise_c) * scale).astype(bf16)
        dv_ref[sl, :] = dv.astype(bf16)
        dext[taps_n + b * CHUNK : taps_n + (b + 1) * CHUNK, :] = dkf * k_fac + dkt * tail_c
        part = (pos - mid) * (qf.astype(f32) * dqf - kf.astype(f32) * dkf)
        part = part + (pos + 1.0) * (qr.astype(f32) * dqr)
        part = part + (CHUNK - 1.0 - pos) * (kt.astype(f32) * dkt)
        drate = drate + jnp.sum(part, axis=0, keepdims=True)
        held = dstate * (whole * keep)
        drate = drate + CHUNK * jnp.sum(state * held, axis=0, keepdims=True)
        dstate = held + jnp.where(block_diag, tn(dy, qr), 0.0)
    drate_ref[...] = -drate

    total = rows + taps_n
    ext[0:taps_n, :] = halo_ref[...].astype(f32)
    ext[taps_n:total, :] = key_ref[...].astype(f32)
    rolled_down(ext, copies, total)
    for r in range(8):
        dcopies[r, 0 : total + taps_n - 8, :] = dext[r : total + taps_n - 8 + r, :]
    tap_acc[...] = jnp.zeros(tap_acc.shape, f32)

    def block(b, carry):
        start = pl.multiple_of(b * 64, 64)
        rem = rem_ref[pl.ds(start, 64), :]
        acc = jnp.zeros((64, channels), f32)
        for m in range(taps_n // 8):
            for r in range(8):
                j = 8 * m + r
                moved = dcopies[r, pl.ds(start + 8 * m, 64), :]
                acc = acc + jnp.where(rem >= j, moved, 0.0) * taps_ref[j : j + 1, :]
        dk_ref[pl.ds(start, 64), :] = acc
        return carry

    lax.fori_loop(0, total // 64, block, 0)

    def tap_block(b, carry):
        start = pl.multiple_of(b * 64, 64)
        age = age_ref[pl.ds(start, 64), :]
        grad = dext[pl.ds(start + taps_n, 64), :]
        for m in range(taps_n // 8):
            for r in range(8):
                j = 8 * m + r
                moved = copies[r, pl.ds(start + taps_n - 8 * m, 64), :]
                term = jnp.where(age >= j, moved, 0.0) * grad
                tap_acc[j, :, :] += jnp.sum(term.reshape(8, 8, channels), axis=0)
        return carry

    lax.fori_loop(0, rows // 64, tap_block, 0)
    dtaps_ref[...] = jnp.sum(tap_acc[...], axis=1)


def h3_back_call(q, ks, v, dy, save, dstate, rate_row, seg_col, seg_row, entry, key, halo, taps, age, rem):
    rows, channels = q.shape
    taps_n = taps.shape[0]
    total = rows + taps_n
    return call(
        functools.partial(h3_back_kernel, taps_n),
        [
            ((rows, channels), bf16),
            ((total, channels), f32),
            ((rows, channels), bf16),
            ((taps_n, channels), f32),
            ((1, channels), f32),
        ],
        [
            pltpu.VMEM((total, channels), f32),
            pltpu.VMEM((8, total, channels), f32),
            pltpu.VMEM((total + taps_n, channels), f32),
            pltpu.VMEM((8, total + taps_n, channels), f32),
            pltpu.VMEM((taps_n, 8, channels), f32),
        ],
        n_in=15,
        flops=20e9,
        nbytes=6e6,
    )(q, ks, v, dy, save, dstate, rate_row, seg_col, seg_row, entry, key, halo, taps, age, rem)


def attend_kernel(lim_ref, q_ref, k_ref, v_ref, segc_ref, segr_ref, o_ref, stat_ref):
    rows, channels = q_ref.shape
    n_heads = channels // HEAD_DIM
    heads = head_masks(CHUNK, channels)
    row = lax.broadcasted_iota(jnp.int32, (CHUNK, CHUNK), 0)
    lane = lax.broadcasted_iota(jnp.int32, (CHUNK, CHUNK), 1)
    stat_lane = lax.broadcasted_iota(jnp.int32, (CHUNK, 128), 1)
    for b in range(rows // CHUNK):
        sl = slice(b * CHUNK, (b + 1) * CHUNK)
        low, high = lim_ref[0, b], lim_ref[1, b]
        q = q_ref[sl, :]
        seg_c = segc_ref[sl, :]
        qh = [jnp.where(hm, q, jnp.zeros_like(q)) for hm in heads]

        def step(t, carry):
            at = pl.multiple_of(t * CHUNK, CHUNK)
            keys = k_ref[pl.ds(at, CHUNK), :]
            values = v_ref[pl.ds(at, CHUNK), :]
            seg_r = segr_ref[t]
            allowed = (row >= lane + (t - high) * CHUNK) & (seg_c == seg_r)
            new = []
            for h in range(n_heads):
                top, total, acc = carry[h]
                z = jnp.where(allowed, nt(qh[h], keys) * scale, masked_low)
                new_top = jnp.maximum(top, jnp.max(z, axis=1, keepdims=True))
                shrink = jnp.exp(top - new_top)
                e = jnp.where(allowed, jnp.exp(z - new_top), 0.0)
                total = total * shrink + jnp.sum(e, axis=1, keepdims=True)
                acc = acc * shrink + nn(e.astype(bf16), values)
                new.append((new_top, total, acc))
            return tuple(new)

        start = tuple(
            (
                jnp.full((CHUNK, 1), masked_low, f32),
                jnp.zeros((CHUNK, 1), f32),
                jnp.zeros((CHUNK, channels), f32),
            )
            for _ in range(n_heads)
        )
        state = lax.fori_loop(low, high + 1, step, start)
        out = jnp.zeros((CHUNK, channels), f32)
        stats = jnp.zeros((CHUNK, 128), f32)
        for h in range(n_heads):
            top, total, acc = state[h]
            out = out + jnp.where(heads[h], acc / total, 0.0)
            stats = jnp.where(stat_lane == h, top, stats)
            stats = jnp.where(stat_lane == 8 + h, total, stats)
        o_ref[sl, :] = out
        stat_ref[b, :, :] = stats.T[0:16, :]


def attend_call(lim, q, k, v, seg_col, seg_tiles):
    rows, channels = q.shape
    return call(
        attend_kernel,
        [((rows, channels), f32), ((rows // CHUNK, 16, CHUNK), f32)],
        smem=1,
        n_in=5,
        flops=10e9,
        nbytes=4e6,
    )(lim, q, k, v, seg_col, seg_tiles)


def attend_back_kernel(
    lim_ref, q_ref, k_ref, v_ref, do_ref, o_ref, stat_ref, segc_ref, segr_ref, dq_ref, dkv_ref
):
    rows, channels = q_ref.shape
    n_heads = channels // HEAD_DIM
    heads = head_masks(CHUNK, channels)
    row = lax.broadcasted_iota(jnp.int32, (CHUNK, CHUNK), 0)
    lane = lax.broadcasted_iota(jnp.int32, (CHUNK, CHUNK), 1)
    stat_lane = lax.broadcasted_iota(jnp.int32, (CHUNK, 128), 1)
    dkv_ref[...] = jnp.zeros(dkv_ref.shape, f32)
    for b in range(rows // CHUNK):
        sl = slice(b * CHUNK, (b + 1) * CHUNK)
        low, high = lim_ref[0, b], lim_ref[1, b]
        q = q_ref[sl, :]
        do = do_ref[sl, :].astype(f32)
        o = o_ref[sl, :]
        seg_q = segr_ref[high]
        zero = jnp.zeros_like(q)
        qh = [jnp.where(hm, q, zero) for hm in heads]
        cols = jnp.zeros((CHUNK, 128), f32)
        for h in range(n_heads):
            inner = jnp.sum(jnp.where(heads[h], do * o, 0.0), axis=1, keepdims=True)
            cols = jnp.where(stat_lane == h, inner, cols)
        inner_rows = cols.T
        totals = stat_ref[b, 8:16, :]
        inv_cols = jnp.concatenate([1.0 / jnp.maximum(totals, 1e-30), jnp.zeros((120, CHUNK), f32)]).T
        wh = []
        for h in range(n_heads):
            inv = inv_cols[:, h : h + 1]
            wh.append(jnp.where(heads[h], do * inv, 0.0).astype(bf16))

        def step(t, dq):
            at = pl.multiple_of(t * CHUNK, CHUNK)
            keys = k_ref[pl.ds(at, CHUNK), :]
            values = v_ref[pl.ds(at, CHUNK), :]
            seg_k = segc_ref[pl.ds(at, CHUNK), :]
            allowed = (lane >= row + (t - high) * CHUNK) & (seg_k == seg_q)
            dk = jnp.zeros((CHUNK, channels), f32)
            dv = jnp.zeros((CHUNK, channels), f32)
            for h in range(n_heads):
                top = stat_ref[b, h : h + 1, :]
                total = stat_ref[b, 8 + h : 9 + h, :]
                z = jnp.where(allowed, nt(keys, qh[h]) * scale, masked_low)
                e = jnp.where(allowed, jnp.exp(z - top), 0.0)
                dp = nt(values, wh[h])
                dz = (e * (dp - inner_rows[h : h + 1, :] / total)).astype(bf16)
                dk = dk + nn(dz, qh[h])
                dv = dv + nn(e.astype(bf16), wh[h])
                dq = dq + jnp.where(heads[h], tn(dz, keys), 0.0)
            dkv_ref[pl.ds(at, CHUNK), 0:channels] += dk * scale
            dkv_ref[pl.ds(at, CHUNK), channels : 2 * channels] += dv
            return dq

        dq = lax.fori_loop(low, high + 1, step, jnp.zeros((CHUNK, channels), f32))
        dq_ref[sl, :] = (dq * scale).astype(bf16)


def attend_back_call(lim, q, k, v, do, o, stats, seg_keys_col, seg_tiles):
    rows, channels = q.shape
    return call(
        attend_back_kernel,
        [((rows, channels), bf16), ((k.shape[0], 2 * channels), f32)],
        smem=1,
        n_in=8,
        flops=20e9,
        nbytes=8e6,
    )(lim, q, k, v, do, o, stats, seg_keys_col, seg_tiles)


def at_rows(value, start, count):
    return lax.dynamic_slice_in_dim(value, start, count, 0)


def chain_join(earlier, later):
    return (later[0] * earlier[0], later[1] + later[0] * earlier[1])


class Rows:
    def __init__(self):
        self.blocks = lax.axis_size("ctx")
        self.place = lax.axis_index("ctx")

    def enter(self, rows):
        return rows

    def enter_ids(self, ids):
        return ids

    def leave(self, rows):
        return rows

    def leave_grad(self, rows):
        return rows

    def spread(self, rows, ordered):
        return rows

    def total(self, partial, ordered):
        return lax.psum(partial.astype(bf16), "tp").astype(f32)

    def local(self, value):
        return value

    def weights(self, proj_in, proj_out, proj_up, proj_down):
        return (
            lax.all_gather(proj_in, "fsdp", axis=1, tiled=True),
            lax.all_gather(proj_out, "fsdp", axis=1, tiled=True),
            lax.all_gather(proj_up, "fsdp", axis=0, tiled=True),
            lax.all_gather(proj_down, "fsdp", axis=1, tiled=True),
        )

    def from_previous(self, value):
        n = self.blocks
        return lax.ppermute(value, "ctx", [(i, i + 1) for i in range(n - 1)])

    def to_previous(self, value):
        n = self.blocks
        return lax.ppermute(value, "ctx", [(i + 1, i) for i in range(n - 1)])

    def state_before(self, factor, state):
        if self.blocks == 2:
            return self.from_previous(state.astype(bf16)).astype(f32)
        factors = lax.all_gather(factor.astype(bf16), "ctx").astype(f32)
        states = lax.all_gather(state.astype(bf16), "ctx")

        def one(hop, held):
            return states[hop].astype(f32) + factors[hop] * held

        return lax.fori_loop(0, self.place, one, jnp.zeros_like(state))

    def grad_after(self, factor, dstate):
        if self.blocks == 2:
            return self.to_previous(dstate.astype(bf16)).astype(f32)
        factors = lax.all_gather(factor.astype(bf16), "ctx").astype(f32)
        states = lax.all_gather(dstate.astype(bf16), "ctx")

        def one(hop, held):
            at = self.blocks - 1 - hop
            return states[at].astype(f32) + factors[at] * held

        return lax.fori_loop(0, self.blocks - 1 - self.place, one, jnp.zeros_like(dstate))

    def keys(self, key, value, ids):
        if self.blocks == 2:
            before = self.from_previous(jnp.concatenate([key, value], axis=1))
            ids_before = self.from_previous(ids.astype(bf16)).astype(jnp.int32)
            channels = key.shape[1]
            return (
                jnp.concatenate([before[:, :channels], key]),
                jnp.concatenate([before[:, channels:], value]),
                jnp.concatenate([ids_before, ids]),
                jnp.int32(key.shape[0]),
            )
        return (
            lax.all_gather(key, "ctx", axis=0, tiled=True),
            lax.all_gather(value, "ctx", axis=0, tiled=True),
            lax.all_gather(ids.astype(bf16), "ctx", axis=0, tiled=True).astype(jnp.int32),
            self.place * key.shape[0],
        )

    def key_grads(self, grads):
        if self.blocks == 2:
            rows = grads.shape[0] // 2
            return grads[rows:] + self.to_previous(grads[:rows].astype(bf16)).astype(f32)
        return lax.psum_scatter(
            grads.astype(bf16), "ctx", scatter_dimension=0, tiled=True
        ).astype(f32)

    def reduce(self, value, dim):
        value = lax.psum_scatter(value.astype(bf16), "fsdp", scatter_dimension=dim, tiled=True)
        return lax.psum(value, "ctx").astype(f32)

    def weight_grads(self, proj_in, proj_out, proj_up, proj_down):
        return (
            self.reduce(proj_in, 1),
            self.reduce(proj_out, 1),
            self.reduce(proj_up, 0),
            self.reduce(proj_down, 1),
        )

    def mixer_grads(self, taps, rate):
        return self.reduce(taps, 0), self.reduce(rate, 1)

    def gain_grads(self, rows):
        return self.reduce(rows, 1)


def norm_parts(rows):
    center = jnp.mean(rows, axis=-1, keepdims=True)
    shifted = rows - center
    spread = jnp.mean(shifted * shifted, axis=-1, keepdims=True)
    return center, lax.rsqrt(spread + epsilon)


def norm(rows, gain):
    center, inv = norm_parts(rows)
    return ((rows - center) * inv * gain).astype(bf16), (center, inv)


def norm_back(rows, kept, gain, grad):
    center, inv = kept
    unit = (rows - center) * inv
    dunit = grad * gain
    mean_d = jnp.mean(dunit, axis=-1, keepdims=True)
    mean_du = jnp.mean(dunit * unit, axis=-1, keepdims=True)
    return inv * (dunit - mean_d - unit * mean_du), jnp.sum(grad * unit, axis=0)


def gelu_tanh(values):
    return jax.nn.gelu(values, approximate=True)


def dot_nn(a, b):
    return jnp.dot(a, b, preferred_element_type=f32)


def dot_nt(a, b):
    return jnp.einsum("tf,df->td", a, b, preferred_element_type=f32)


def dot_tn(a, b):
    return jnp.einsum("tf,td->fd", a, b, preferred_element_type=f32)


def feed_forward(normed, proj_up, proj_down):
    up = dot_nn(normed, proj_up)
    hidden = gelu_tanh(up).astype(bf16)
    return dot_nn(hidden, proj_down), up, hidden


def feed_back(normed, up, hidden, grad_bf, proj_up, proj_down):
    down_grad = dot_tn(hidden, grad_bf)
    dhidden = dot_nt(grad_bf, proj_down)
    dup = jax.vjp(gelu_tanh, up)[1](dhidden)[0].astype(bf16)
    return dot_nt(dup, proj_up), dot_tn(normed, dup), down_grad


def project(normed, proj_in):
    return [dot_nn(normed, proj_in[j]).astype(bf16) for j in range(3)]


def project_back(normed, grads, proj_in):
    dnormed = sum(dot_nt(grads[j], proj_in[j]) for j in range(3))
    return dnormed, jnp.stack([dot_tn(normed, grads[j]) for j in range(3)])


def expand_state(small):
    channels = small.shape[1]
    return jnp.where(same_head(channels), jnp.tile(small, (channels // HEAD_DIM, 1)), 0.0)


def compact_state(state):
    channels = state.shape[1]
    return jnp.sum(state.reshape(channels // HEAD_DIM, HEAD_DIM, channels), axis=0)


def mixer_setup(ids, halo_ids, taps_n, rate_row):
    rows, channels = ids.shape[0], rate_row.shape[1]
    ext = jnp.concatenate([halo_ids, ids])
    at = jnp.arange(rows + taps_n, dtype=jnp.int32)
    same = ext[:, None] == ext[None, :]
    age = jnp.sum((same & (at[None, :] < at[:, None])).astype(jnp.int32), axis=1)[taps_n:]
    rem = jnp.sum((same & (at[None, :] > at[:, None])).astype(jnp.int32), axis=1)
    entry, last = halo_ids[taps_n - 1], ids[rows - 1]
    pos = jnp.arange(rows, dtype=f32)[:, None]
    tail = jnp.exp(-rate_row * (rows - 1.0 - pos)) * (ids == last).astype(f32)[:, None]
    rise = jnp.exp(-rate_row * (pos + 1.0)) * (ids == entry).astype(f32)[:, None]
    factor = jnp.exp(-rate_row * rows) * (entry == last).astype(f32)
    return (
        jnp.broadcast_to(age[:, None], (rows, channels)),
        jnp.broadcast_to(rem[:, None], (rows + taps_n, channels)),
        tail,
        rise,
        factor,
        entry.reshape(1, 1),
    )


def run(plan, inputs, cotangent, segments, gains, last_gain, in_weight, h3_out, attn_out, up_weight, down_weight, shift_taps, decay_rate):
    x0 = plan.enter(inputs[0]).astype(f32)
    grad = plan.enter(cotangent[0]).astype(f32)
    ids = plan.enter_ids(segments[0] + 1)
    taps, rate = plan.local(shift_taps), plan.local(decay_rate)
    in0, out0, up0, down0 = plan.weights(in_weight[0], h3_out, up_weight[0], down_weight[0])
    in1, out1, up1, down1 = plan.weights(in_weight[1], attn_out, up_weight[1], down_weight[1])
    taps_n = taps.shape[0]
    rows = ids.shape[0]
    rate_row = rate.reshape(1, -1)
    halo_ids = plan.from_previous(ids[rows - taps_n :].astype(bf16)).astype(jnp.int32)
    age, rem, tail, rise, factor, entry = mixer_setup(ids, halo_ids, taps_n, rate_row)
    seg_col, seg_row = ids[:, None], ids[None, :]

    n0, kept0 = norm(x0, gains[0])
    n0 = plan.spread(n0, True)
    q0, k0, v0 = project(n0, in0)
    halo = plan.from_previous(k0[rows - taps_n :])
    ks, state_end = shift_forward(k0, halo, taps, age, tail, v0)
    state_in = expand_state(plan.state_before(factor, compact_state(state_end)))
    y0, saved = h3_forward_call(q0, ks, v0, state_in, rate_row, seg_col, seg_row, entry)
    x1 = x0 + plan.total(dot_nn(y0, out0), True)
    m0, kept1 = norm(x1, gains[1])
    m0 = plan.spread(m0, False)
    part, u0, r0 = feed_forward(m0, up0, down0)
    x2 = x1 + plan.total(part, False)

    n2, kept2 = norm(x2, gains[2])
    n2 = plan.spread(n2, True)
    q2, k2, v2 = project(n2, in1)
    keys, values, key_ids, offset = plan.keys(k2, v2, ids)
    tiles = jnp.arange(rows // CHUNK, dtype=jnp.int32)
    firsts = ids[:: CHUNK]
    limits = jnp.stack(
        [
            jnp.sum((key_ids[None, :] < firsts[:, None]).astype(jnp.int32), axis=1) // CHUNK,
            offset // CHUNK + tiles,
        ]
    )
    seg_tiles = key_ids.reshape(-1, 1, CHUNK)
    mixed, stats = attend_call(limits, q2, keys, values, seg_col, seg_tiles)
    mixed_bf = mixed.astype(bf16)
    x3 = x2 + plan.total(dot_nn(mixed_bf, out1), True)
    m1, kept3 = norm(x3, last_gain)
    m1 = plan.spread(m1, False)
    part, u1, r1 = feed_forward(m1, up1, down1)
    x4 = x3 + plan.total(part, False)
    output = plan.leave(x4.astype(bf16))

    grad_bf = plan.spread(grad.astype(bf16), False)
    part, up1_grad, down1_grad = feed_back(m1, u1, r1, grad_bf, up1, down1)
    dres, gain3 = norm_back(x3, kept3, last_gain, plan.total(part, False))
    grad = grad + dres
    grad_bf = plan.spread(grad.astype(bf16), True)
    out1_grad = dot_tn(mixed_bf, grad_bf)
    dmixed = dot_nt(grad_bf, out1).astype(bf16)
    dq, dkv = attend_back_call(
        limits, q2, keys, values, dmixed, mixed, stats, key_ids[:, None], seg_tiles
    )
    dkv = plan.key_grads(dkv).astype(bf16)
    channels = dq.shape[1]
    part, in1_grad = project_back(n2, (dq, dkv[:, :channels], dkv[:, channels:]), in1)
    dres, gain2 = norm_back(x2, kept2, gains[2], plan.total(part, True))
    grad = grad + dres
    second = plan.weight_grads(in1_grad, out1_grad, up1_grad, down1_grad)

    grad_bf = plan.spread(grad.astype(bf16), False)
    part, up0_grad, down0_grad = feed_back(m0, u0, r0, grad_bf, up0, down0)
    dres, gain1 = norm_back(x1, kept1, gains[1], plan.total(part, False))
    grad = grad + dres
    grad_bf = plan.spread(grad.astype(bf16), True)
    out0_grad = dot_tn(y0, grad_bf)
    dy = dot_nt(grad_bf, out0)
    dstate_in = compact_state(
        jnp.where(
            same_head(channels),
            dot_tn(dy.astype(bf16), (q0.astype(f32) * (rise * scale)).astype(bf16)),
            0.0,
        )
    )
    dstate_end = expand_state(plan.grad_after(factor, dstate_in))
    dq, dk, dv, dtaps, drate = h3_back_call(
        q0, ks, v0, dy, saved, dstate_end, rate_row, seg_col, seg_row, entry, k0, halo, taps, age, rem
    )
    halo_grad = plan.to_previous(dk[:taps_n].astype(bf16)).astype(f32)
    dk = jnp.concatenate([dk[taps_n:rows], dk[rows:] + halo_grad]).astype(bf16)
    part, in0_grad = project_back(n0, (dq, dk, dv), in0)
    dres, gain0 = norm_back(x0, kept0, gains[0], plan.total(part, True))
    input_grad = plan.leave_grad(grad + dres)
    first = plan.weight_grads(in0_grad, out0_grad, up0_grad, down0_grad)
    dtaps, drate = plan.mixer_grads(dtaps, drate.reshape(rate.shape))
    gain_rows = plan.gain_grads(jnp.stack([gain0, gain1, gain2, gain3]))
    return (
        output[None],
        input_grad[None],
        gain_rows[:3],
        gain_rows[3],
        jnp.stack([first[0], second[0]]),
        first[1],
        second[1],
        jnp.stack([first[2], second[2]]),
        jnp.stack([first[3], second[3]]),
        dtaps,
        drate,
    )


def shards(*arguments):
    return run(Rows(), *arguments)


def solution(mesh):
    placed = (
        P("fsdp", "ctx", None),
        P("fsdp", "ctx", None),
        P("fsdp", "ctx"),
        P(),
        P(),
        P(None, None, "fsdp", "tp"),
        P("tp", "fsdp"),
        P("tp", "fsdp"),
        P(None, "fsdp", "tp"),
        P(None, "tp", "fsdp"),
        P(None, "tp"),
        P("tp", None),
    )
    return jax.shard_map(
        shards,
        mesh=mesh,
        in_specs=placed,
        out_specs=(
            P("fsdp", "ctx", None),
            P("fsdp", "ctx", None),
            P(None, "fsdp"),
            P("fsdp"),
            P(None, None, "fsdp", "tp"),
            P("tp", "fsdp"),
            P("tp", "fsdp"),
            P(None, "fsdp", "tp"),
            P(None, "tp", "fsdp"),
            P("fsdp", "tp"),
            P("tp", "fsdp"),
        ),
        check_vma=False,
    )
```

```python
import functools

import jax
import jax.numpy as jnp
from jax import lax
from jax.experimental import pallas as pl
from jax.experimental.pallas import tpu as pltpu
from jax.sharding import PartitionSpec as P

HEAD_DIM = 64
epsilon = 1e-05
masked_low = -1e30
bf16 = jnp.bfloat16
f32 = jnp.float32
scale = HEAD_DIM ** (-0.5)
CHUNK = 256


def nn(a, b):
    return lax.dot_general(a, b, (((1,), (0,)), ((), ())), preferred_element_type=f32)


def nt(a, b):
    return lax.dot_general(a, b, (((1,), (1,)), ((), ())), preferred_element_type=f32)


def tn(a, b):
    return lax.dot_general(a, b, (((0,), (0,)), ((), ())), preferred_element_type=f32)


def head_masks(rows, channels):
    lane = lax.broadcasted_iota(jnp.int32, (rows, channels), 1)
    return [(lane >= HEAD_DIM * h) & (lane < HEAD_DIM * (h + 1)) for h in range(channels // HEAD_DIM)]


def same_head(channels):
    row = lax.broadcasted_iota(jnp.int32, (channels, channels), 0) // HEAD_DIM
    lane = lax.broadcasted_iota(jnp.int32, (channels, channels), 1) // HEAD_DIM
    return row == lane


def compact(state):
    channels = state.shape[1]
    state = jnp.where(same_head(channels), state, 0.0)
    parts = [state[HEAD_DIM * h : HEAD_DIM * (h + 1), :] for h in range(channels // HEAD_DIM)]
    return sum(parts[1:], parts[0]).astype(bf16)


def expand(small):
    channels = small.shape[1]
    tall = jnp.concatenate([small.astype(f32)] * (channels // HEAD_DIM), axis=0)
    return jnp.where(same_head(channels), tall, 0.0)


def params(mib):
    return pltpu.CompilerParams(vmem_limit_bytes=mib * 1024 * 1024)


def kernel_call(kernel, outs, arrays, scalars=(), scratch=(), mib=32, us=2.0):
    vm = pl.BlockSpec(memory_space=pltpu.VMEM)
    sm = pl.BlockSpec(memory_space=pltpu.SMEM)
    return pl.pallas_call(
        kernel,
        out_shape=[jax.ShapeDtypeStruct(s, d) for s, d in outs],
        in_specs=[sm] * len(scalars) + [vm] * len(arrays),
        out_specs=[vm] * len(outs),
        scratch_shapes=list(scratch),
        compiler_params=params(mib),
        cost_estimate=pl.CostEstimate(flops=int(us * 1e9), bytes_accessed=1000, transcendentals=0),
    )(*scalars, *arrays)


def rolled_down(ext_ref, copies, rows):
    for r in range(8):
        copies[r, 8:rows, :] = ext_ref[8 - r : rows - r, :]


def shift_kernel(taps_n, key_ref, halo_ref, taps_ref, age_ref, tail_ref, value_ref, ks_ref, st_ref, ext, copies):
    rows, channels = key_ref.shape
    ext[0:taps_n, :] = halo_ref[...].astype(f32)
    ext[taps_n : taps_n + rows, :] = key_ref[...].astype(f32)
    rolled_down(ext, copies, rows + taps_n)

    def block(b, carry):
        start = pl.multiple_of(b * 64, 64)
        age = age_ref[pl.ds(start, 64), :]
        acc = jnp.zeros((64, channels), f32)
        for m in range(taps_n // 8):
            for r in range(8):
                j = 8 * m + r
                moved = copies[r, pl.ds(start + taps_n - 8 * m, 64), :]
                acc = acc + jnp.where(age >= j, moved, 0.0) * taps_ref[j : j + 1, :]
        ks_ref[pl.ds(start, 64), :] = acc
        return carry

    lax.fori_loop(0, rows // 64, block, 0)
    kt = (ks_ref[...] * tail_ref[...]).astype(bf16)
    st_ref[...] = compact(tn(value_ref[...], kt))


def shift_forward(key, halo, taps, age, tail, value):
    rows, channels = key.shape
    taps_n = taps.shape[0]
    return kernel_call(
        functools.partial(shift_kernel, taps_n),
        [((rows, channels), f32), ((HEAD_DIM, channels), bf16)],
        (key, halo, taps, age, tail, value),
        scratch=        [pltpu.VMEM((rows + taps_n, channels), f32), pltpu.VMEM((8, rows + taps_n, channels), f32)],
        us=10.0,
    )


def decay_factors(rate_row, rows):
    pos = lax.broadcasted_iota(jnp.int32, (rows, rate_row.shape[1]), 0).astype(f32)
    mid = 0.5 * rows
    q_fac = jnp.exp(-rate_row * (pos - mid))
    k_fac = jnp.exp(rate_row * (pos - mid))
    rise = jnp.exp(-rate_row * (pos + 1.0))
    tail = jnp.exp(-rate_row * (rows - 1.0 - pos))
    whole = jnp.exp(-rate_row * rows)
    return pos, mid, q_fac, k_fac, rise, tail, whole


def h3_kernel(q_ref, ks_ref, v_ref, sin_ref, rate_ref, segc_ref, segr_ref, entry_ref, y_ref, save_ref):
    rows, channels = q_ref.shape
    blocks = rows // CHUNK
    _, _, q_fac, k_fac, rise, tail, whole = decay_factors(rate_ref[...], CHUNK)
    heads = head_masks(CHUNK, channels)
    block_diag = same_head(channels)
    causal = lax.broadcasted_iota(jnp.int32, (CHUNK, CHUNK), 0) >= lax.broadcasted_iota(
        jnp.int32, (CHUNK, CHUNK), 1
    )
    state = expand(sin_ref[...])
    for b in range(blocks):
        sl = slice(b * CHUNK, (b + 1) * CHUNK)
        seg_c = segc_ref[sl, :]
        seg_r = segr_ref[:, sl]
        before = entry_ref[...] if b == 0 else segc_ref[b * CHUNK - 1 : b * CHUNK, :]
        last = segc_ref[(b + 1) * CHUNK - 1 : (b + 1) * CHUNK, :]
        carried = (seg_c == before).astype(f32)
        final = (seg_c == last).astype(f32)
        keep = (last == before).astype(f32)
        q = q_ref[sl, :].astype(f32) * scale
        k = ks_ref[sl, :]
        v = v_ref[sl, :]
        qf = (q * q_fac).astype(bf16)
        kf = (k * k_fac).astype(bf16)
        qr = (q * (rise * carried)).astype(bf16)
        kt = (k * (tail * final)).astype(bf16)
        allowed = causal & (seg_c == seg_r)
        save_ref[b, :, :] = state
        y = nt(qr, state.astype(bf16))
        for hm in heads:
            scores = nt(jnp.where(hm, qf, jnp.zeros_like(qf)), kf)
            scores = jnp.where(allowed, scores, 0.0).astype(bf16)
            y = y + jnp.where(hm, nn(scores, v), 0.0)
        y_ref[sl, :] = y.astype(bf16)
        state = state * (whole * keep) + jnp.where(block_diag, tn(v, kt), 0.0)


def h3_forward_call(q, ks, v, state_in, rate_row, seg_col, seg_row, entry):
    rows, channels = q.shape
    return kernel_call(
        h3_kernel,
        [((rows, channels), bf16), ((rows // CHUNK, channels, channels), f32)],
        (q, ks, v, state_in, rate_row, seg_col, seg_row, entry),
        us=5.0,
    )


def h3_back_kernel(
    taps_n,
    q_ref,
    ks_ref,
    v_ref,
    dy_ref,
    save_ref,
    dst_ref,
    rate_ref,
    segc_ref,
    segr_ref,
    entry_ref,
    key_ref,
    halo_ref,
    taps_ref,
    age_ref,
    rem_ref,
    dq_ref,
    dk_ref,
    dhalo_ref,
    dv_ref,
    dtaps_ref,
    drate_ref,
    ext,
    copies,
    dext,
    dcopies,
    tap_acc,
):
    rows, channels = q_ref.shape
    blocks = rows // CHUNK
    pos, mid, q_fac, k_fac, rise, tail, whole = decay_factors(rate_ref[...], CHUNK)
    heads = head_masks(CHUNK, channels)
    block_diag = same_head(channels)
    row = lax.broadcasted_iota(jnp.int32, (CHUNK, CHUNK), 0)
    lane = lax.broadcasted_iota(jnp.int32, (CHUNK, CHUNK), 1)
    dstate = expand(dst_ref[...])
    drate = jnp.zeros((1, channels), f32)
    dext[0:taps_n, :] = jnp.zeros((taps_n, channels), f32)
    dext[rows + taps_n : rows + 2 * taps_n, :] = jnp.zeros((taps_n, channels), f32)
    for b in reversed(range(blocks)):
        sl = slice(b * CHUNK, (b + 1) * CHUNK)
        seg_c = segc_ref[sl, :]
        seg_r = segr_ref[:, sl]
        before = entry_ref[...] if b == 0 else segc_ref[b * CHUNK - 1 : b * CHUNK, :]
        last = segc_ref[(b + 1) * CHUNK - 1 : (b + 1) * CHUNK, :]
        carried = (seg_c == before).astype(f32)
        final = (seg_c == last).astype(f32)
        keep = (last == before).astype(f32)
        q = q_ref[sl, :].astype(f32) * scale
        k = ks_ref[sl, :]
        v = v_ref[sl, :]
        dy = dy_ref[sl, :]
        qf = (q * q_fac).astype(bf16)
        kf = (k * k_fac).astype(bf16)
        rise_c = rise * carried
        tail_c = tail * final
        qr = (q * rise_c).astype(bf16)
        kt = (k * tail_c).astype(bf16)
        same = seg_c == seg_r
        low_mask = (row >= lane) & same
        up_mask = (row <= lane) & same
        state = save_ref[b, :, :]
        dstate_b = dstate.astype(bf16)
        dqf = jnp.zeros((CHUNK, channels), f32)
        dkf = jnp.zeros((CHUNK, channels), f32)
        dv = nt(kt, dstate_b)
        zero = jnp.zeros_like(qf)
        for hm in heads:
            kh = jnp.where(hm, kf, zero)
            vh = jnp.where(hm, v, zero)
            scores_t = jnp.where(up_mask, nt(kh, qf), 0.0).astype(bf16)
            dv = dv + jnp.where(hm, nn(scores_t, dy), 0.0)
            dsc = jnp.where(low_mask, nt(dy, vh), 0.0).astype(bf16)
            dsc_t = jnp.where(up_mask, nt(vh, dy), 0.0).astype(bf16)
            dqf = dqf + nn(dsc, kh)
            dkf = dkf + jnp.where(hm, nn(dsc_t, qf), 0.0)
        dqr = nn(dy, state.astype(bf16))
        dkt = nn(v, dstate_b)
        dq_ref[sl, :] = ((dqf * q_fac + dqr * rise_c) * scale).astype(bf16)
        dv_ref[sl, :] = dv.astype(bf16)
        dext[taps_n + b * CHUNK : taps_n + (b + 1) * CHUNK, :] = dkf * k_fac + dkt * tail_c
        part = (pos - mid) * (qf.astype(f32) * dqf - kf.astype(f32) * dkf)
        part = part + (pos + 1.0) * (qr.astype(f32) * dqr)
        part = part + (CHUNK - 1.0 - pos) * (kt.astype(f32) * dkt)
        drate = drate + jnp.sum(part, axis=0, keepdims=True)
        held = dstate * (whole * keep)
        drate = drate + CHUNK * jnp.sum(state * held, axis=0, keepdims=True)
        dstate = held + jnp.where(block_diag, tn(dy, qr), 0.0)
    drate_ref[...] = -drate

    total = rows + taps_n
    ext[0:taps_n, :] = halo_ref[...].astype(f32)
    ext[taps_n:total, :] = key_ref[...].astype(f32)
    rolled_down(ext, copies, total)
    for r in range(8):
        dcopies[r, 0 : total + taps_n - 8, :] = dext[r : total + taps_n - 8 + r, :]
    tap_acc[...] = jnp.zeros(tap_acc.shape, f32)

    def gathered(start):
        rem = rem_ref[pl.ds(start, 64), :]
        acc = jnp.zeros((64, channels), f32)
        for m in range(taps_n // 8):
            for r in range(8):
                j = 8 * m + r
                moved = dcopies[r, pl.ds(start + 8 * m, 64), :]
                acc = acc + jnp.where(rem >= j, moved, 0.0) * taps_ref[j : j + 1, :]
        return acc

    def block(b, carry):
        start = pl.multiple_of(b * 64, 64)
        dk_ref[pl.ds(start, 64), :] = gathered(start + taps_n)
        return carry

    lax.fori_loop(0, rows // 64, block, 0)
    dhalo_ref[...] = gathered(0).astype(bf16)

    def tap_block(b, carry):
        start = pl.multiple_of(b * 64, 64)
        age = age_ref[pl.ds(start, 64), :]
        grad = dext[pl.ds(start + taps_n, 64), :]
        for m in range(taps_n // 8):
            for r in range(8):
                j = 8 * m + r
                moved = copies[r, pl.ds(start + taps_n - 8 * m, 64), :]
                term = jnp.where(age >= j, moved, 0.0) * grad
                tap_acc[j, :, :] += jnp.sum(term.reshape(8, 8, channels), axis=0)
        return carry

    lax.fori_loop(0, rows // 64, tap_block, 0)
    dtaps_ref[...] = jnp.sum(tap_acc[...], axis=1)


def h3_back_call(q, ks, v, dy, save, dstate, rate_row, seg_col, seg_row, entry, key, halo, taps, age, rem):
    rows, channels = q.shape
    taps_n = taps.shape[0]
    total = rows + taps_n
    return kernel_call(
        functools.partial(h3_back_kernel, taps_n),
        [
            ((rows, channels), bf16),
            ((rows, channels), f32),
            ((taps_n, channels), bf16),
            ((rows, channels), bf16),
            ((taps_n, channels), f32),
            ((1, channels), f32),
        ],
        (q, ks, v, dy, save, dstate, rate_row, seg_col, seg_row, entry, key, halo, taps, age, rem),
        scratch=[
            pltpu.VMEM((total, channels), f32),
            pltpu.VMEM((8, total, channels), f32),
            pltpu.VMEM((total + taps_n, channels), f32),
            pltpu.VMEM((8, total + taps_n, channels), f32),
            pltpu.VMEM((taps_n, 8, channels), f32),
        ],
        mib=48,
        us=26.0,
    )


def attend_kernel(resume, finish, lim_ref, q_ref, k_ref, v_ref, segc_ref, segr_ref, *refs):
    if resume:
        acc_in, col_in = refs[:2]
        refs = refs[2:]
    rows, channels = q_ref.shape
    n_heads = channels // HEAD_DIM
    heads = head_masks(CHUNK, channels)
    row = lax.broadcasted_iota(jnp.int32, (CHUNK, CHUNK), 0)
    lane = lax.broadcasted_iota(jnp.int32, (CHUNK, CHUNK), 1)
    stat_lane = lax.broadcasted_iota(jnp.int32, (CHUNK, 128), 1)
    for b in range(rows // CHUNK):
        sl = slice(b * CHUNK, (b + 1) * CHUNK)
        low, high, diagonal = lim_ref[0, b], lim_ref[1, b], lim_ref[2, b]
        q = q_ref[sl, :]
        seg_c = segc_ref[sl, :]
        qh = [jnp.where(hm, q, jnp.zeros_like(q)) for hm in heads]

        def step(t, carry):
            at = pl.multiple_of(t * CHUNK, CHUNK)
            keys = k_ref[pl.ds(at, CHUNK), :]
            values = v_ref[pl.ds(at, CHUNK), :]
            seg_r = segr_ref[t]
            allowed = (row >= lane + (t - diagonal) * CHUNK) & (seg_c == seg_r)
            new = []
            for h in range(n_heads):
                top, total, acc = carry[h]
                z = jnp.where(allowed, nt(qh[h], keys) * scale, masked_low)
                new_top = jnp.maximum(top, jnp.max(z, axis=1, keepdims=True))
                shrink = jnp.exp(top - new_top)
                e = jnp.where(allowed, jnp.exp(z - new_top), 0.0)
                total = total * shrink + jnp.sum(e, axis=1, keepdims=True)
                acc = acc * shrink + nn(e.astype(bf16), values)
                new.append((new_top, total, acc))
            return tuple(new)

        if resume:
            col = col_in[sl, :]
            held = acc_in[sl, :]
            start = tuple((col[:, h : h + 1], col[:, 8 + h : 9 + h], held) for h in range(n_heads))
        else:
            start = tuple(
                (
                    jnp.full((CHUNK, 1), masked_low, f32),
                    jnp.zeros((CHUNK, 1), f32),
                    jnp.zeros((CHUNK, channels), f32),
                )
                for _ in range(n_heads)
            )
        state = lax.fori_loop(low, high + 1, step, start)
        out = jnp.zeros((CHUNK, channels), f32)
        stats = jnp.zeros((CHUNK, 128), f32)
        for h in range(n_heads):
            top, total, acc = state[h]
            out = jnp.where(heads[h], acc / total if finish else acc, out)
            stats = jnp.where(stat_lane == h, top, stats)
            stats = jnp.where(stat_lane == 8 + h, total, stats)
        refs[0][sl, :] = out
        if finish:
            refs[1][b, :, :] = stats.T[0:16, :]
            refs[2][sl, :] = out.astype(bf16)
        else:
            refs[1][sl, :] = stats


def attend(lim, q, k, v, seg_col, seg_tiles, held=(), finish=True):
    rows, channels = q.shape
    if finish:
        outs = [((rows, channels), f32), ((rows // CHUNK, 16, CHUNK), f32), ((rows, channels), bf16)]
    else:
        outs = [((rows, channels), f32), ((rows, 128), f32)]
    return kernel_call(
        functools.partial(attend_kernel, bool(held), finish),
        outs,
        (q, k, v, seg_col, seg_tiles, *held),
        scalars=(lim,),
        mib=48,
        us=5.0,
    )


def attend_back_kernel(
    lim_ref, q_ref, k_ref, v_ref, do_ref, o_ref, stat_ref, qseg_ref, kseg_ref, dqin_ref, dq_ref, dkv_ref, acc
):
    rows, channels = q_ref.shape
    n_heads = channels // HEAD_DIM
    heads = head_masks(CHUNK, channels)
    row = lax.broadcasted_iota(jnp.int32, (CHUNK, CHUNK), 0)
    lane = lax.broadcasted_iota(jnp.int32, (CHUNK, CHUNK), 1)
    stat_lane = lax.broadcasted_iota(jnp.int32, (CHUNK, 128), 1)
    acc[...] = jnp.zeros(acc.shape, f32)
    for b in range(rows // CHUNK):
        sl = slice(b * CHUNK, (b + 1) * CHUNK)
        low, high, diagonal = lim_ref[0, b], lim_ref[1, b], lim_ref[2, b]
        q = q_ref[sl, :]
        do = do_ref[sl, :].astype(f32)
        o = o_ref[sl, :]
        seg_q = qseg_ref[b]
        zero = jnp.zeros_like(q)
        qh = [jnp.where(hm, q, zero) for hm in heads]
        cols = jnp.zeros((CHUNK, 128), f32)
        for h in range(n_heads):
            inner = jnp.sum(jnp.where(heads[h], do * o, 0.0), axis=1, keepdims=True)
            cols = jnp.where(stat_lane == h, inner, cols)
        inner_rows = cols.T
        totals = stat_ref[b, 8:16, :]
        inv_cols = jnp.concatenate([1.0 / jnp.maximum(totals, 1e-30), jnp.zeros((120, CHUNK), f32)]).T
        wh = []
        for h in range(n_heads):
            inv = inv_cols[:, h : h + 1]
            wh.append(jnp.where(heads[h], do * inv, 0.0).astype(bf16))

        def step(t, dq):
            at = pl.multiple_of(t * CHUNK, CHUNK)
            keys = k_ref[pl.ds(at, CHUNK), :]
            values = v_ref[pl.ds(at, CHUNK), :]
            seg_k = kseg_ref[pl.ds(at, CHUNK), :]
            allowed = (lane >= row + (t - diagonal) * CHUNK) & (seg_k == seg_q)
            dk = jnp.zeros((CHUNK, channels), f32)
            dv = jnp.zeros((CHUNK, channels), f32)
            for h in range(n_heads):
                top = stat_ref[b, h : h + 1, :]
                total = stat_ref[b, 8 + h : 9 + h, :]
                z = jnp.where(allowed, nt(keys, qh[h]) * scale, masked_low)
                e = jnp.where(allowed, jnp.exp(z - top), 0.0)
                dp = nt(values, wh[h])
                dz = (e * (dp - inner_rows[h : h + 1, :] / total)).astype(bf16)
                dk = dk + nn(dz, qh[h])
                dv = dv + nn(e.astype(bf16), wh[h])
                dq = dq + jnp.where(heads[h], tn(dz, keys), 0.0)
            acc[0, pl.ds(at, CHUNK), :] += dk
            acc[1, pl.ds(at, CHUNK), :] += dv
            return dq

        dq = lax.fori_loop(low, high + 1, step, jnp.zeros((CHUNK, channels), f32))
        dq_ref[sl, :] = (dq * scale + dqin_ref[sl, :].astype(f32)).astype(dq_ref.dtype)
    dkv_ref[:, 0:channels] = (acc[0] * scale).astype(dkv_ref.dtype)
    dkv_ref[:, channels : 2 * channels] = acc[1].astype(dkv_ref.dtype)


def attend_back(lim, q, k, v, do, o, stats, q_tiles, key_col, dq_in, dq_type, dkv_type):
    rows, channels = q.shape
    return kernel_call(
        attend_back_kernel,
        [((rows, channels), dq_type), ((k.shape[0], 2 * channels), dkv_type)],
        (q, k, v, do, o, stats, q_tiles, key_col, dq_in),
        scalars=(lim,),
        scratch=[pltpu.VMEM((2, k.shape[0], channels), f32)],
        mib=56,
        us=7.0,
    )


def by_rows(rows, step, body):
    def one(i, carry):
        body(pl.ds(pl.multiple_of(i * step, step), step))
        return carry

    lax.fori_loop(0, rows // step, one, 0)


def norm_kernel(n_add, x_ref, *refs):
    adds, gain_ref, outs = refs[:n_add], refs[n_add], refs[n_add + 1 :]

    def body(at):
        x = x_ref[at, :].astype(f32)
        for a in adds:
            x = x + a[at, :].astype(f32)
        center = jnp.mean(x, axis=1, keepdims=True)
        moved = x - center
        inv = lax.rsqrt(jnp.mean(moved * moved, axis=1, keepdims=True) + epsilon)
        outs[0][at, :] = x
        outs[1][at, :] = (moved * inv * gain_ref[...]).astype(bf16)

    by_rows(x_ref.shape[0], 32, body)


def norm(x, adds, gain):
    shape = x.shape
    return kernel_call(
        functools.partial(norm_kernel, len(adds)),
        [(shape, f32), (shape, bf16)],
        (x, *adds, gain.reshape(1, -1)),
        us=2.0,
    )


def norm_back_kernel(n_add, x_ref, grad_ref, *refs):
    adds, gain_ref, outs = refs[:n_add], refs[n_add], refs[n_add + 1 :]

    def body(at):
        x = x_ref[at, :]
        center = jnp.mean(x, axis=1, keepdims=True)
        moved = x - center
        inv = lax.rsqrt(jnp.mean(moved * moved, axis=1, keepdims=True) + epsilon)
        unit = moved * inv
        d = adds[0][at, :].astype(f32)
        for a in adds[1:]:
            d = d + a[at, :].astype(f32)
        d = d * gain_ref[...]
        mean_d = jnp.mean(d, axis=1, keepdims=True)
        mean_du = jnp.mean(d * unit, axis=1, keepdims=True)
        grad = grad_ref[at, :].astype(f32) + inv * (d - mean_d - unit * mean_du)
        outs[0][at, :] = grad
        outs[1][at, :] = grad.astype(bf16)

    by_rows(x_ref.shape[0], 32, body)


def norm_back(x, grad, adds, gain):
    shape = x.shape
    return kernel_call(
        functools.partial(norm_back_kernel, len(adds)),
        [(shape, f32), (shape, bf16)],
        (x, grad, *adds, gain.reshape(1, -1)),
        us=2.0,
    )


def gelu_both(u):
    inner = 0.7978845608028654 * (u + 0.044715 * (u * u * u))
    t = jnp.tanh(inner)
    half = 0.5 * (1.0 + t)
    slope = half + 0.5 * u * (1.0 - t * t) * (0.7978845608028654 * (1.0 + 0.134145 * (u * u)))
    return u * half, slope


def feed_forward_kernel(n, hid, *refs):
    ms, w_ref = refs[:n], refs[n]
    parts, r_ref, slope_ref, up = refs[n + 1 : 2 * n + 1], refs[2 * n + 1], refs[2 * n + 2], refs[2 * n + 3]
    size = ms[0].shape[0]
    for i in range(n):
        up[...] = nn(ms[i][...], w_ref[:, 0:hid])

        def body(at):
            r, slope = gelu_both(up[at, :])
            to = pl.ds(pl.multiple_of(at.start + i * size, 32), 32)
            r_ref[to, :] = r.astype(bf16)
            slope_ref[to, :] = slope.astype(bf16)

        by_rows(size, 32, body)
        parts[i][...] = nt(r_ref[i * size : (i + 1) * size, :], w_ref[:, hid : 2 * hid]).astype(bf16)


def feed_forward(ms, w, hid):
    n, size = len(ms), ms[0].shape[0]
    model = ms[0].shape[1]
    out = kernel_call(
        functools.partial(feed_forward_kernel, n, hid),
        [((size, model), bf16)] * n + [((n * size, hid), bf16)] * 2,
        (*ms, w),
        scratch=[pltpu.VMEM((size, hid), f32)],
        us=5.0,
    )
    return out[:n], out[n], out[n + 1]


def feed_mid_kernel(n, hid, *refs):
    ms, gs, w_ref, gain_ref = refs[:n], refs[n : 2 * n], refs[2 * n], refs[2 * n + 1]
    outs = refs[2 * n + 2 :]
    parts, r_ref, du_ref, gsum_ref, up, dr = outs[:n], outs[n], outs[n + 1], outs[n + 2], outs[n + 3], outs[n + 4]
    size = ms[0].shape[0]
    gsum_ref[...] = jnp.zeros(gsum_ref.shape, f32)
    for i in range(n):
        up[...] = nn(ms[i][...], w_ref[:, 0:hid])
        dr[...] = nn(gs[i][...], w_ref[:, hid : 2 * hid])

        def body(at):
            r, slope = gelu_both(up[at, :])
            to = pl.ds(pl.multiple_of(at.start + i * size, 32), 32)
            r_ref[to, :] = r.astype(bf16)
            du_ref[to, :] = (dr[at, :] * slope).astype(bf16)

        by_rows(size, 32, body)
        part = nt(du_ref[i * size : (i + 1) * size, :], w_ref[:, 0:hid])
        parts[i][...] = part.astype(bf16)
        gsum_ref[...] += jnp.sum(part * ms[i][...].astype(f32), axis=0, keepdims=True)
    gsum_ref[...] = gsum_ref[...] / gain_ref[...]


def feed_mid(ms, gs, w, hid, gain):
    n, size = len(ms), ms[0].shape[0]
    model = ms[0].shape[1]
    out = kernel_call(
        functools.partial(feed_mid_kernel, n, hid),
        [((size, model), bf16)] * n + [((n * size, hid), bf16)] * 2 + [((1, model), f32)],
        (*ms, *gs, w, gain.reshape(1, -1)),
        scratch=[pltpu.VMEM((size, hid), f32)] * 2,
        us=6.0,
    )
    return out[:n], out[n], out[n + 1], out[n + 2]


def feed_back_kernel(n, hid, *refs):
    ms, gs, slope_ref, w_ref, gain_ref = refs[:n], refs[n : 2 * n], refs[2 * n], refs[2 * n + 1], refs[2 * n + 2]
    outs = refs[2 * n + 3 :]
    parts, du_ref, gsum_ref, dr = outs[:n], outs[n], outs[n + 1], outs[n + 2]
    size = ms[0].shape[0]
    gsum_ref[...] = jnp.zeros(gsum_ref.shape, f32)
    for i in range(n):
        dr[...] = nn(gs[i][...], w_ref[:, hid : 2 * hid])

        def body(at):
            to = pl.ds(pl.multiple_of(at.start + i * size, 32), 32)
            du_ref[to, :] = (dr[at, :] * slope_ref[to, :].astype(f32)).astype(bf16)

        by_rows(size, 32, body)
        part = nt(du_ref[i * size : (i + 1) * size, :], w_ref[:, 0:hid])
        parts[i][...] = part.astype(bf16)
        gsum_ref[...] += jnp.sum(part * ms[i][...].astype(f32), axis=0, keepdims=True)
    gsum_ref[...] = gsum_ref[...] / gain_ref[...]


def feed_back(ms, gs, slope, w, hid, gain):
    n, size = len(ms), ms[0].shape[0]
    model = ms[0].shape[1]
    out = kernel_call(
        functools.partial(feed_back_kernel, n, hid),
        [((size, model), bf16)] * n + [((n * size, hid), bf16), ((1, model), f32)],
        (*ms, *gs, slope, w, gain.reshape(1, -1)),
        scratch=[pltpu.VMEM((size, hid), f32)],
        us=4.0,
    )
    return out[:n], out[n], out[n + 1]


def places(core_ref, n, size):
    if n == 1:
        return [pl.ds(0, size)]
    core = core_ref[0]
    return [
        pl.ds(pl.multiple_of(core * size, size), size),
        pl.ds(pl.multiple_of((1 - core) * size, size), size),
    ]


def project_kernel(n, at_lane, channels, core_ref, *refs):
    ns, w_ref, outs = refs[:n], refs[n], refs[n + 1 :]
    size = ns[0].shape[0]
    for i, to in enumerate(places(core_ref, n, size)):
        x = ns[i][...]
        triple = nn(x, w_ref[:, at_lane : at_lane + 3 * channels])
        for j in range(3):
            outs[j][to, :] = triple[:, j * channels : (j + 1) * channels].astype(bf16)
        outs[3][to, :] = x


def project(core, ns, w, at_lane, channels):
    n, size, model = len(ns), ns[0].shape[0], ns[0].shape[1]
    return kernel_call(
        functools.partial(project_kernel, n, at_lane, channels),
        [((n * size, channels), bf16)] * 3 + [((n * size, model), bf16)],
        (*ns, w),
        scalars=(core,),
        us=3.0,
    )


def out_kernel(n, at_lane, core_ref, y_ref, w_ref, *parts):
    channels = y_ref.shape[1]
    size = parts[0].shape[0]
    for i, to in enumerate(places(core_ref, n, size)):
        parts[i][...] = nt(y_ref[to, :].astype(bf16), w_ref[:, at_lane : at_lane + channels]).astype(bf16)


def project_out(core, n, y, w, at_lane):
    size, model = y.shape[0] // n, w.shape[0]
    return kernel_call(
        functools.partial(out_kernel, n, at_lane),
        [((size, model), bf16)] * n,
        (y, w),
        scalars=(core,),
        us=2.0,
    )


def out_back_kernel(n, at_lane, channels, state, core_ref, *refs):
    gs, w_ref = refs[:n], refs[n]
    refs = refs[n + 1 :]
    if state:
        q_ref, rise_ref = refs[:2]
        refs = refs[2:]
    dy_ref, ordered_ref = refs[0], refs[1]
    size = gs[0].shape[0]
    for i, to in enumerate(places(core_ref, n, size)):
        g = gs[i][...]
        dy_ref[to, :] = nn(g, w_ref[:, at_lane : at_lane + channels]).astype(bf16)
        ordered_ref[to, :] = g
    if state:
        qr = (q_ref[...].astype(f32) * scale * rise_ref[...]).astype(bf16)
        refs[2][...] = compact(tn(dy_ref[...], qr))


def out_back(core, gs, w, at_lane, channels, state=()):
    n, size, model = len(gs), gs[0].shape[0], gs[0].shape[1]
    outs = [((n * size, channels), bf16), ((n * size, model), bf16)]
    if state:
        outs.append(((HEAD_DIM, channels), bf16))
    return kernel_call(
        functools.partial(out_back_kernel, n, at_lane, channels, bool(state)),
        outs,
        (*gs, w, *state),
        scalars=(core,),
        us=2.0,
    )


def project_back_kernel(n, at_lane, kind, count, core_ref, dq_ref, *refs):
    others = refs[:count]
    w_ref, n_ref, gain_ref = refs[count : count + 3]
    outs = refs[count + 3 :]
    parts, cat_ref, gsum_ref = outs[:n], outs[n], outs[n + 1]
    rows, channels = dq_ref.shape
    cat_ref[:, 0:channels] = dq_ref[...]
    if kind == "halo":
        dk_ref, dv_ref, extra_ref = others
        cut = rows - extra_ref.shape[0]
        cat_ref[0:cut, channels : 2 * channels] = dk_ref[0:cut, :].astype(bf16)
        cat_ref[cut:rows, channels : 2 * channels] = (
            dk_ref[cut:rows, :] + extra_ref[...].astype(f32)
        ).astype(bf16)
        cat_ref[:, 2 * channels : 3 * channels] = dv_ref[...].astype(bf16)
    else:
        total = others[0][...].astype(f32)
        for other in others[1:]:
            total = total + other[...].astype(f32)
        cat_ref[:, channels : 3 * channels] = total.astype(bf16)
    size = parts[0].shape[0]
    gsum_ref[...] = jnp.zeros(gsum_ref.shape, f32)
    for i, to in enumerate(places(core_ref, n, size)):
        part = nt(cat_ref[to, :], w_ref[:, at_lane : at_lane + 3 * channels])
        parts[i][...] = part.astype(bf16)
        gsum_ref[...] += jnp.sum(part * n_ref[to, :].astype(f32), axis=0, keepdims=True)
    gsum_ref[...] = gsum_ref[...] / gain_ref[...]


def project_back(core, n, kind, dq, others, w, at_lane, normed, gain):
    rows, channels = dq.shape
    size, model = rows // n, normed.shape[1]
    out = kernel_call(
        functools.partial(project_back_kernel, n, at_lane, kind, len(others)),
        [((size, model), bf16)] * n + [((rows, 3 * channels), bf16), ((1, model), f32)],
        (dq, *others, w, normed, gain.reshape(1, -1)),
        scalars=(core,),
        us=3.0,
    )
    return out[:n], out[n], out[n + 1]


def at_rows(value, start, count):
    return lax.dynamic_slice_in_dim(value, start, count, 0)


def tie(*values):
    return lax.optimization_barrier(values)


class Rows:
    halves = 1

    def __init__(self):
        self.blocks = lax.axis_size("ctx")
        self.place = lax.axis_index("ctx")
        self.core = self.place

    def enter(self, rows):
        return rows

    def leave(self, rows):
        return rows

    def leave_grad(self, rows):
        return rows

    def spread(self, rows):
        return [rows]

    def total(self, parts):
        return [lax.psum(parts[0], "tp")]

    def local(self, value):
        return value

    def weights(self, first, lower, upper):
        return [lax.all_gather(w, "fsdp", axis=0, tiled=True) for w in (first, lower, upper)]

    def ids(self, ids, taps_n):
        n = self.blocks
        halo = lax.ppermute(
            ids[ids.shape[0] - taps_n :].astype(bf16), "ctx", [(i, i + 1) for i in range(n - 1)]
        )
        return ids, halo.astype(jnp.int32), None

    def from_previous(self, value):
        n = self.blocks
        return lax.ppermute(value, "ctx", [(i, i + 1) for i in range(n - 1)])

    def to_previous(self, value):
        n = self.blocks
        return lax.ppermute(value, "ctx", [(i + 1, i) for i in range(n - 1)])

    def state_before(self, factor, state):
        factors = lax.all_gather(factor.astype(bf16), "ctx").astype(f32)
        states = lax.all_gather(state, "ctx")

        def one(hop, held):
            return states[hop].astype(f32) + factors[hop] * held

        held = lax.fori_loop(0, self.place, one, jnp.zeros(state.shape, f32))
        return held.astype(bf16)

    def grad_after(self, factor, dstate):
        factors = lax.all_gather(factor.astype(bf16), "ctx").astype(f32)
        states = lax.all_gather(dstate, "ctx")

        def one(hop, held):
            at = self.blocks - 1 - hop
            return states[at].astype(f32) + factors[at] * held

        held = lax.fori_loop(0, self.blocks - 1 - self.place, one, jnp.zeros(dstate.shape, f32))
        return held.astype(bf16)

    def attend(self, q, k, v, ids, prev_ids):
        rows = q.shape[0]
        keys = lax.all_gather(k, "ctx", axis=0, tiled=True)
        values = lax.all_gather(v, "ctx", axis=0, tiled=True)
        key_ids = lax.all_gather(ids.astype(bf16), "ctx", axis=0, tiled=True).astype(jnp.int32)
        low = first_tiles(ids, key_ids)
        high = self.place * (rows // CHUNK) + jnp.arange(rows // CHUNK, dtype=jnp.int32)
        limits = jnp.stack([low, high, high])
        mixed, stats, mixed_bf = attend(
            limits, q, keys, values, ids[:, None], key_ids.reshape(-1, 1, CHUNK)
        )
        return mixed, stats, mixed_bf, (limits, keys, values, key_ids)

    def attend_back(self, kept, q, k, v, grad, mixed, stats, ids, prev_ids):
        limits, keys, values, key_ids = kept
        tiles = ids.reshape(-1, 1, CHUNK)
        dq, dkv = attend_back(
            limits, q, keys, values, grad, mixed, stats, tiles, key_ids[:, None],
            jnp.zeros(q.shape, bf16), bf16, bf16,
        )
        return dq, [lax.psum_scatter(dkv, "ctx", scatter_dimension=0, tiled=True)]

    def reduce(self, value):
        value = lax.psum_scatter(value, "fsdp", scatter_dimension=0, tiled=True)
        return lax.psum(value, "ctx")

    def over_places(self, value):
        return lax.psum(value, "tp")


class Pairs(Rows):
    halves = 2

    def __init__(self):
        self.blocks = 2
        self.core = lax.axis_index("ctx")
        self.chip = lax.axis_index("tp")
        self.place = self.chip // 2
        self.home = self.core == self.place

    def send(self, value, pairs):
        number = [(4 * c + t, 4 * d + u) for (c, t), (d, u) in pairs]
        return lax.ppermute(value, ("ctx", "tp"), number)

    def swap(self, value):
        return lax.ppermute(value, "ctx", [(0, 1), (1, 0)])

    def neighbour(self, value):
        return lax.ppermute(value, "tp", [(0, 1), (1, 0), (2, 3), (3, 2)])

    def across(self, value):
        return lax.ppermute(value, "tp", [(0, 2), (2, 0), (1, 3), (3, 1)])

    def from_home_core(self, value):
        return self.send(value, [((t // 2, t), (1 - t // 2, t)) for t in range(4)])

    def enter(self, rows):
        half = rows.shape[0] // 2
        got = self.from_home_core(at_rows(rows, (1 - self.core) * half, half))
        return jnp.where(self.home, at_rows(rows, self.core * half, half), got)

    def ids(self, ids, taps_n):
        other = self.swap(ids)
        own = jnp.where(self.home, ids, other)
        first = jnp.where(self.core == 0, ids, other)
        before = jnp.where(self.place == 1, first, 0)
        return own, before[ids.shape[0] - taps_n :], before

    def in_order(self, own, other):
        first = self.core == 0
        return jnp.concatenate([jnp.where(first, own, other), jnp.where(first, other, own)])

    def leave(self, rows):
        there = self.across(rows)
        got = self.swap(jnp.where(self.home, there, rows))
        return self.in_order(jnp.where(self.home, rows, there), got)

    def leave_grad(self, rows):
        return self.leave(rows.astype(bf16)).astype(f32)

    def spread(self, rows):
        return [rows, self.swap(rows)]

    def total(self, parts):
        own, other = parts
        both = (own.astype(f32) + self.swap(other).astype(f32)).astype(bf16)
        return [both, self.neighbour(both)]

    def local(self, value):
        got = self.send(
            value, [((c, 2 * c + e), (c, 2 - 2 * c + e)) for c in range(2) for e in range(2)]
        )
        return jnp.where(self.home, value, got)

    def around(self, value):
        return [lax.ppermute(value, "fsdp", [(i, i ^ k) for i in range(4)]) for k in (1, 2, 3)]

    def weights(self, first, lower, upper):
        first = self.local(first)
        first, lower = tie(first, lower)
        lower = self.local(lower)
        lower, upper = tie(lower, upper)
        upper = self.local(upper)
        place, size = lax.axis_index("fsdp"), first.shape[0]
        whole = jnp.zeros((4 * size, first.shape[1]), bf16)
        for k, part in enumerate([first] + self.around(first)):
            whole = lax.dynamic_update_slice_in_dim(whole, part, (place ^ k) * size, 0)
        return [whole] + [lax.all_gather(w, "fsdp", axis=0, tiled=True) for w in (lower, upper)]

    def from_previous(self, value):
        return self.send(value, [((c, t), (c, t + 2)) for c in range(2) for t in range(2)])

    def to_previous(self, value):
        return self.send(value, [((c, t + 2), (c, t)) for c in range(2) for t in range(2)])

    def state_before(self, factor, state):
        return self.from_previous(state)

    def grad_after(self, factor, dstate):
        return self.to_previous(dstate)

    def attend(self, q, k, v, ids, prev_ids):
        before = self.from_previous(jnp.concatenate([k, v], axis=1))
        channels, count = q.shape[1], q.shape[0] // CHUNK
        place = jnp.arange(count, dtype=jnp.int32)
        low = first_tiles(ids, jnp.concatenate([prev_ids, ids]))
        own_limits = jnp.stack([jnp.maximum(low - count, 0), place, place])
        prev_limits = jnp.stack([low, jnp.full_like(low, count - 1), place + count])
        seg_col, tiles, prev_tiles = ids[:, None], ids.reshape(-1, 1, CHUNK), prev_ids.reshape(-1, 1, CHUNK)
        held = attend(own_limits, q, k, v, seg_col, tiles, finish=False)
        keys, values = before[:, :channels], before[:, channels:]
        mixed, stats, mixed_bf = attend(prev_limits, q, keys, values, seg_col, prev_tiles, held)
        return mixed, stats, mixed_bf, (own_limits, prev_limits, keys, values)

    def attend_back(self, kept, q, k, v, grad, mixed, stats, ids, prev_ids):
        own_limits, prev_limits, keys, values = kept
        tiles = ids.reshape(-1, 1, CHUNK)
        dq, dkv_prev = attend_back(
            prev_limits, q, keys, values, grad, mixed, stats, tiles, prev_ids[:, None],
            jnp.zeros(q.shape, bf16), f32, bf16,
        )
        got = self.to_previous(dkv_prev)
        dq, dkv = attend_back(
            own_limits, q, k, v, grad, mixed, stats, tiles, ids[:, None], dq, bf16, f32
        )
        return dq, [dkv, got]

    def reduce(self, value):
        place = lax.axis_index("fsdp")
        size = value.shape[0] // 4
        total = at_rows(value, place * size, size).astype(f32)
        for k in (1, 2, 3):
            part = at_rows(value, (place ^ k) * size, size)
            total = total + lax.ppermute(part, "fsdp", [(i, i ^ k) for i in range(4)]).astype(f32)
        total = total.astype(bf16)
        got = self.send(
            total, [((c, 2 - 2 * c + e), (c, 2 * c + e)) for c in range(2) for e in range(2)]
        )
        total = (total.astype(f32) + got.astype(f32)).astype(bf16)
        return jnp.where(self.home, total, self.from_home_core(total))

    def over_places(self, value):
        value = (value.astype(f32) + self.neighbour(value).astype(f32)).astype(bf16)
        return value.astype(f32) + self.across(value).astype(f32)


def first_tiles(ids, key_ids):
    firsts = ids[::CHUNK]
    return jnp.sum((key_ids[None, :] < firsts[:, None]).astype(jnp.int32), axis=1) // CHUNK


def dot_tn(a, b):
    return jnp.einsum("tf,td->fd", a, b, preferred_element_type=f32).astype(bf16)


def mixer_setup(ids, halo_ids, taps_n, rate_row):
    rows, channels = ids.shape[0], rate_row.shape[1]
    ext = jnp.concatenate([halo_ids, ids])
    at = jnp.arange(rows + taps_n, dtype=jnp.int32)
    same = ext[:, None] == ext[None, :]
    age = jnp.sum((same & (at[None, :] < at[:, None])).astype(jnp.int32), axis=1)[taps_n:]
    rem = jnp.sum((same & (at[None, :] > at[:, None])).astype(jnp.int32), axis=1)
    entry, last = halo_ids[taps_n - 1], ids[rows - 1]
    pos = jnp.arange(rows, dtype=f32)[:, None]
    tail = jnp.exp(-rate_row * (rows - 1.0 - pos)) * (ids == last).astype(f32)[:, None]
    rise = jnp.exp(-rate_row * (pos + 1.0)) * (ids == entry).astype(f32)[:, None]
    factor = jnp.exp(-rate_row * rows) * (entry == last).astype(f32)
    return (
        jnp.broadcast_to(age[:, None], (rows, channels)),
        jnp.broadcast_to(rem[:, None], (rows + taps_n, channels)),
        tail,
        rise,
        factor,
        entry.reshape(1, 1),
    )


def feed_shares(reduced):
    width = reduced.shape[1] // 2
    return reduced[:, :width].astype(f32), reduced[:, width:].T.astype(f32)


def mixer_shares(reduced, channels):
    parts = [reduced[:, j * channels : (j + 1) * channels].astype(f32) for j in range(3)]
    return jnp.stack(parts), reduced[:, 3 * channels : 4 * channels].T.astype(f32)


def run(plan, inputs, cotangent, segments, gains, last_gain, in_weight, h3_out, attn_out, up_weight, down_weight, shift_taps, decay_rate):
    n = plan.halves
    slots = lax.axis_size("fsdp")
    hid = up_weight.shape[2]
    channels = h3_out.shape[0]
    taps_n = shift_taps.shape[0]
    share = h3_out.shape[1]
    core = plan.core.astype(jnp.int32).reshape(1)
    gap = (-3 * channels) % 128
    pad = jnp.zeros((share, gap), bf16)
    in_at, out1_at = 2 * hid, 2 * hid + 3 * channels + gap

    x_in = plan.enter(inputs[0])
    g_in = plan.enter(cotangent[0])
    ids, halo_ids, prev_ids = plan.ids(segments[0] + 1, taps_n)
    rows = ids.shape[0]
    first = jnp.concatenate([in_weight[0, j] for j in range(3)], axis=1)
    lower = jnp.concatenate([up_weight[0], down_weight[0].T, h3_out.T], axis=1)
    upper = jnp.concatenate(
        [up_weight[1], down_weight[1].T] + [in_weight[1, j] for j in range(3)] + [pad, attn_out.T], axis=1
    )
    first, lower, upper = plan.weights(first, lower, upper)
    both = plan.local(jnp.concatenate([shift_taps, decay_rate.reshape(1, -1)]))
    taps, rate_row = both[:taps_n], both[taps_n:]
    age, rem, tail, rise, factor, entry = mixer_setup(ids, halo_ids, taps_n, rate_row)
    seg_col, seg_row = ids[:, None], ids[None, :]

    x0, n0 = norm(x_in, [], gains[0])
    q0, k0, v0, n0 = project(core, plan.spread(n0), first, 0, channels)
    halo = plan.from_previous(k0[rows - taps_n :])
    ks, state_end = shift_forward(k0, halo, taps, age, tail, v0)
    state_in = plan.state_before(factor, state_end)
    y0, saved = h3_forward_call(q0, ks, v0, state_in, rate_row, seg_col, seg_row, entry)
    y0, lower = tie(y0, lower)
    parts = project_out(core, n, y0, lower, 2 * hid)
    x1, m0 = norm(x0, plan.total(parts), gains[1])
    m0s = plan.spread(m0)
    parts, r0, slope0 = feed_forward(m0s, lower, hid)
    x2, n2 = norm(x1, plan.total(parts), gains[2])

    q2, k2, v2, n2 = project(core, plan.spread(n2), upper, in_at, channels)
    mixed, stats, mixed_bf, kept = plan.attend(q2, k2, v2, ids, prev_ids)
    parts = project_out(core, n, mixed_bf, upper, out1_at)
    x3, m1 = norm(x2, plan.total(parts), last_gain)
    m1s = plan.spread(m1)

    g_ins = plan.spread(g_in)
    parts, r1, du1, gain3 = feed_mid(m1s, g_ins, upper, hid, last_gain)
    grad, grad_bf = norm_back(x3, g_in, plan.total(parts), last_gain)
    dmixed, grad_bf1 = out_back(core, plan.spread(grad_bf), upper, out1_at, channels)
    dq, dkv = plan.attend_back(kept, q2, k2, v2, dmixed, mixed, stats, ids, prev_ids)
    parts, cat1, gain2 = project_back(core, n, "sum", dq, dkv, upper, in_at, n2, gains[2])
    grad, grad_bf = norm_back(x2, grad, plan.total(parts), gains[2])

    size = rows // n
    parts = [
        jnp.einsum("tf,df->td", r1[i * size : (i + 1) * size], upper[:, hid : 2 * hid], preferred_element_type=f32).astype(bf16)
        for i in range(n)
    ]
    x4 = x3
    for part in plan.total(parts):
        x4 = x4 + part.astype(f32)
    output = plan.leave(x4.astype(bf16))
    feed1 = plan.reduce(
        jnp.concatenate([dot_tn(jnp.concatenate(m1s), du1), dot_tn(jnp.concatenate(g_ins), r1)], axis=1)
    )
    mix1 = plan.reduce(jnp.concatenate([dot_tn(n2, cat1), dot_tn(grad_bf1, mixed_bf)], axis=1))

    grad_bfs = plan.spread(grad_bf)
    parts, du0, gain1 = feed_back(m0s, grad_bfs, slope0, lower, hid, gains[1])
    feed0 = plan.reduce(
        jnp.concatenate([dot_tn(jnp.concatenate(m0s), du0), dot_tn(jnp.concatenate(grad_bfs), r0)], axis=1)
    )
    grad, grad_bf = norm_back(x1, grad, plan.total(parts), gains[1])
    dy, grad_bf0, dstate = out_back(core, plan.spread(grad_bf), lower, 2 * hid, channels, (q0, rise))
    dstate_end = plan.grad_after(factor, dstate)
    dstate_end, output, feed1 = tie(dstate_end, output, feed1)
    dq, dk, dhalo, dv, dtaps, drate = h3_back_call(
        q0, ks, v0, dy, saved, dstate_end, rate_row, seg_col, seg_row, entry, k0, halo, taps, age, rem
    )
    dq, mix1 = tie(dq, mix1)
    parts, cat0, gain0 = project_back(
        core, n, "halo", dq, (dk, dv, plan.to_previous(dhalo)), first, 0, n0, gains[0]
    )
    grad, _ = norm_back(x0, grad, plan.total(parts), gains[0])
    input_grad = plan.leave_grad(grad)

    mix0 = jnp.concatenate([dot_tn(n0, cat0), dot_tn(grad_bf0, y0)], axis=1)
    mix0 = mix0.reshape(slots, share, 4 * channels)
    taps_each = taps_n // slots
    small = jnp.concatenate(
        [
            dtaps.reshape(slots, taps_each, channels),
            jnp.pad(
                drate.reshape(-1, slots, HEAD_DIM // slots).transpose(1, 0, 2).reshape(slots, 1, -1),
                ((0, 0), (0, 0), (0, channels - channels // slots)),
            ),
            jnp.concatenate([gain0, gain1, gain2, gain3]).reshape(4, slots, share).transpose(1, 0, 2),
        ],
        axis=1,
    ).astype(bf16)
    small = jnp.pad(small, ((0, 0), (0, (-small.shape[1]) % 32), (0, 3 * channels)))
    height = share + small.shape[1]
    mix0 = plan.reduce(jnp.concatenate([mix0, small], axis=1).reshape(slots * height, 4 * channels))
    small = mix0[share:, :channels]
    in0_grad, out0_grad = mixer_shares(mix0[:share], channels)
    dtaps = small[:taps_each].astype(f32)
    drate = small[taps_each, : channels // slots].astype(f32).reshape(-1, HEAD_DIM // slots)
    gain_rows = plan.over_places(small[taps_each + 1 : taps_each + 5]).astype(f32)
    up0_grad, down0_grad = feed_shares(feed0)
    up1_grad, down1_grad = feed_shares(feed1)
    in1_grad, out1_grad = mixer_shares(mix1, channels)
    return (
        output[None].astype(bf16),
        input_grad[None],
        gain_rows[:3],
        gain_rows[3],
        jnp.stack([in0_grad, in1_grad]),
        out0_grad,
        out1_grad,
        jnp.stack([up0_grad, up1_grad]),
        jnp.stack([down0_grad, down1_grad]),
        dtaps,
        drate,
    )


def shards(*arguments):
    paired = lax.axis_size("ctx") == 2 and lax.axis_size("tp") == 4 and lax.axis_size("fsdp") == 4
    return run(Pairs() if paired else Rows(), *arguments)


def solution(mesh):
    placed = (
        P("fsdp", "ctx", None),
        P("fsdp", "ctx", None),
        P("fsdp", "ctx"),
        P(),
        P(),
        P(None, None, "fsdp", "tp"),
        P("tp", "fsdp"),
        P("tp", "fsdp"),
        P(None, "fsdp", "tp"),
        P(None, "tp", "fsdp"),
        P(None, "tp"),
        P("tp", None),
    )
    return jax.shard_map(
        shards,
        mesh=mesh,
        in_specs=placed,
        out_specs=(
            P("fsdp", "ctx", None),
            P("fsdp", "ctx", None),
            P(None, "fsdp"),
            P("fsdp"),
            P(None, None, "fsdp", "tp"),
            P("tp", "fsdp"),
            P("tp", "fsdp"),
            P(None, "fsdp", "tp"),
            P(None, "tp", "fsdp"),
            P("fsdp", "tp"),
            P("tp", "fsdp"),
        ),
        check_vma=False,
    )
```

```python
import functools

import jax
import jax.numpy as jnp
from jax import lax
from jax.experimental import pallas as pl
from jax.experimental.pallas import tpu as pltpu
from jax.sharding import PartitionSpec as P

HEAD_DIM = 64
epsilon = 1e-05
masked_low = -1e30
bf16 = jnp.bfloat16
f32 = jnp.float32
scale = HEAD_DIM ** (-0.5)
CHUNK = 256


def nn(a, b):
    return lax.dot_general(a, b, (((1,), (0,)), ((), ())), preferred_element_type=f32)


def nt(a, b):
    return lax.dot_general(a, b, (((1,), (1,)), ((), ())), preferred_element_type=f32)


def tn(a, b):
    return lax.dot_general(a, b, (((0,), (0,)), ((), ())), preferred_element_type=f32)


def head_masks(rows, channels):
    lane = lax.broadcasted_iota(jnp.int32, (rows, channels), 1)
    return [(lane >= HEAD_DIM * h) & (lane < HEAD_DIM * (h + 1)) for h in range(channels // HEAD_DIM)]


def same_head(channels):
    row = lax.broadcasted_iota(jnp.int32, (channels, channels), 0) // HEAD_DIM
    lane = lax.broadcasted_iota(jnp.int32, (channels, channels), 1) // HEAD_DIM
    return row == lane


def compact(state):
    channels = state.shape[1]
    state = jnp.where(same_head(channels), state, 0.0)
    parts = [state[HEAD_DIM * h : HEAD_DIM * (h + 1), :] for h in range(channels // HEAD_DIM)]
    return sum(parts[1:], parts[0]).astype(bf16)


def expand(small):
    channels = small.shape[1]
    tall = jnp.concatenate([small.astype(f32)] * (channels // HEAD_DIM), axis=0)
    return jnp.where(same_head(channels), tall, 0.0)


def params(mib):
    return pltpu.CompilerParams(vmem_limit_bytes=mib * 1024 * 1024)


def kernel_call(kernel, outs, arrays, scalars=(), scratch=(), mib=12, us=2.0):
    vm = pl.BlockSpec(memory_space=pltpu.VMEM)
    sm = pl.BlockSpec(memory_space=pltpu.SMEM)
    return pl.pallas_call(
        kernel,
        out_shape=[jax.ShapeDtypeStruct(s, d) for s, d in outs],
        in_specs=[sm] * len(scalars) + [vm] * len(arrays),
        out_specs=[vm] * len(outs),
        scratch_shapes=list(scratch),
        compiler_params=params(mib),
        cost_estimate=pl.CostEstimate(flops=int(us * 1e9), bytes_accessed=1000, transcendentals=0),
    )(*scalars, *arrays)


def column_of(row):
    return jnp.broadcast_to(row.astype(f32), (8, row.shape[1])).T[:, 0:1].astype(jnp.int32)


def setup_kernel(taps_n, ids_ref, before_ref, col_ref, before_col_ref, entry_ref, age_ref, rem_ref, own_ref, prev_ref):
    rows = ids_ref.shape[1]
    channels = age_ref.shape[1]
    count = rows // CHUNK
    own, before = ids_ref[...], before_ref[...]
    col_ref[...] = column_of(own)
    before_col_ref[...] = column_of(before)
    entry_ref[...] = before_col_ref[rows - 1 : rows, :]
    lane = lax.broadcasted_iota(jnp.int32, (64, rows), 1)
    row = lax.broadcasted_iota(jnp.int32, (64, rows), 0)
    halo_lane = lane >= rows - taps_n

    def fill(ids, at, start):
        in_own = ids == own
        in_halo = (ids == before) & halo_lane
        both = (in_own & (lane < row + start)).astype(f32) + (in_halo & (lane - rows < row + start)).astype(f32)
        after = (in_own & (lane > row + start)).astype(f32) + (in_halo & (lane - rows > row + start)).astype(f32)
        age = jnp.sum(both, axis=1, keepdims=True).astype(jnp.int32)
        rem = jnp.sum(after, axis=1, keepdims=True).astype(jnp.int32)
        age_ref[at, :] = jnp.broadcast_to(age, (64, channels))
        rem_ref[at, :] = jnp.broadcast_to(rem, (64, channels))

    fill(before_col_ref[rows - 64 : rows, :], pl.ds(0, 64), -64)

    def block(b, carry):
        start = pl.multiple_of(b * 64, 64)
        fill(col_ref[pl.ds(start, 64), :], pl.ds(start + 64, 64), start)
        return carry

    lax.fori_loop(0, rows // 64, block, 0)
    for b in range(count):
        first = own[:, b * CHUNK : b * CHUNK + 1]
        low = jnp.sum((before < first).astype(f32)) + jnp.sum((own < first).astype(f32))
        low = low.astype(jnp.int32) // CHUNK
        own_ref[0, b] = jnp.maximum(low - count, 0)
        own_ref[1, b] = b
        own_ref[2, b] = b
        prev_ref[0, b] = low
        prev_ref[1, b] = count - 1
        prev_ref[2, b] = count + b


def setup_ids(ids, before, taps_n, channels):
    rows = ids.shape[1]
    count = rows // CHUNK
    vm, sm = pl.BlockSpec(memory_space=pltpu.VMEM), pl.BlockSpec(memory_space=pltpu.SMEM)
    shapes = [(rows, 1), (rows, 1), (1, 1), (rows + taps_n, channels), (rows + taps_n, channels), (3, count), (3, count)]
    return pl.pallas_call(
        functools.partial(setup_kernel, taps_n),
        out_shape=[jax.ShapeDtypeStruct(s, jnp.int32) for s in shapes],
        in_specs=[vm] * 2,
        out_specs=[vm] * 5 + [sm] * 2,
        compiler_params=params(8),
        cost_estimate=pl.CostEstimate(flops=int(2e9), bytes_accessed=1000, transcendentals=0),
    )(ids, before)


def tail_and_rise(rate, rows):
    pos = lax.broadcasted_iota(jnp.int32, (rows, rate.shape[1]), 0).astype(f32)
    return jnp.exp(-rate * (rows - 1.0 - pos)), jnp.exp(-rate * (pos + 1.0))


def rising(q_ref, rate_ref, segc_ref, entry_ref):
    rows = q_ref.shape[0]
    rise = tail_and_rise(rate_ref[...], rows)[1]
    rise = rise * ((segc_ref[...] == entry_ref[...]).astype(f32) * scale)
    return (q_ref[...].astype(f32) * rise).astype(bf16)


def rolled_down(ext_ref, age_ref, copies, rows):
    for r in range(8):
        copies[r, 8:rows, :] = jnp.where(age_ref[8:rows, :] >= r, ext_ref[8 - r : rows - r, :], 0.0)


def lane_tiles(channels):
    return [(low, min(low + 128, channels)) for low in range(0, channels, 128)]


def filtered(copies, taps_ref, reach_ref, reach_at, first, step, groups, size, low, high):
    reach = reach_ref[reach_at, low:high]
    base = first if step > 0 else first + step * (groups - 1)
    parts = [None] * groups
    for r in range(8):
        window = copies[r, pl.ds(base, size + 8 * (groups - 1)), low:high]
        for m in range(groups):
            at = 8 * m if step > 0 else 8 * (groups - 1 - m)
            term = window[at : at + size] * taps_ref[8 * m + r : 8 * m + r + 1, low:high]
            parts[m] = term if parts[m] is None else parts[m] + term
    total = parts[0]
    for m in range(1, groups):
        total = total + jnp.where(reach >= 8 * m, parts[m], 0.0)
    return total


def decay_factors(rate_row, rows):
    pos = lax.broadcasted_iota(jnp.int32, (rows, rate_row.shape[1]), 0).astype(f32)
    mid = 0.5 * rows
    q_fac = jnp.exp(-rate_row * (pos - mid))
    k_fac = jnp.exp(rate_row * (pos - mid))
    rise = jnp.exp(-rate_row * (pos + 1.0))
    tail = jnp.exp(-rate_row * (rows - 1.0 - pos))
    whole = jnp.exp(-rate_row * rows)
    return pos, mid, q_fac, k_fac, rise, tail, whole


def h3_kernel(
    taps_n,
    key_ref,
    halo_ref,
    q_ref,
    v_ref,
    taps_ref,
    rate_ref,
    age_ref,
    segc_ref,
    segr_ref,
    ks_ref,
    st_ref,
    y_ref,
    save_ref,
    ext,
    copies,
):
    rows, channels = key_ref.shape
    ext[0:taps_n, :] = halo_ref[...].astype(f32)
    ext[taps_n : taps_n + rows, :] = key_ref[...].astype(f32)
    rolled_down(ext, age_ref, copies, rows + taps_n)

    def block(b, carry):
        start = pl.multiple_of(b * 64, 64)
        for low, high in lane_tiles(channels):
            ks_ref[pl.ds(start, 64), low:high] = filtered(
                copies, taps_ref, age_ref, pl.ds(start + taps_n, 64), start + taps_n, -8, taps_n // 8, 64, low, high
            )
        return carry

    lax.fori_loop(0, rows // 64, block, 0)

    blocks = rows // CHUNK
    _, _, q_fac, k_fac, rise, tail, whole = decay_factors(rate_ref[...], CHUNK)
    heads = head_masks(CHUNK, channels)
    block_diag = same_head(channels)
    causal = lax.broadcasted_iota(jnp.int32, (CHUNK, CHUNK), 0) >= lax.broadcasted_iota(
        jnp.int32, (CHUNK, CHUNK), 1
    )
    state = jnp.zeros((channels, channels), f32)
    for b in range(blocks):
        sl = slice(b * CHUNK, (b + 1) * CHUNK)
        seg_c = segc_ref[sl, :]
        seg_r = segr_ref[:, sl]
        last = segc_ref[(b + 1) * CHUNK - 1 : (b + 1) * CHUNK, :]
        final = (seg_c == last).astype(f32)
        q = q_ref[sl, :].astype(f32) * scale
        k = ks_ref[sl, :]
        v = v_ref[sl, :]
        qf = (q * q_fac).astype(bf16)
        kf = (k * k_fac).astype(bf16)
        kt = (k * (tail * final)).astype(bf16)
        allowed = causal & (seg_c == seg_r)
        save_ref[b, :, :] = state
        y = jnp.zeros((CHUNK, channels), f32)
        if b > 0:
            before = segc_ref[b * CHUNK - 1 : b * CHUNK, :]
            qr = (q * (rise * (seg_c == before).astype(f32))).astype(bf16)
            y = nt(qr, state.astype(bf16))
            state = state * (whole * (last == before).astype(f32))
        for hm in heads:
            scores = nt(jnp.where(hm, qf, jnp.zeros_like(qf)), kf)
            scores = jnp.where(allowed, scores, 0.0).astype(bf16)
            y = y + jnp.where(hm, nn(scores, v), 0.0)
        y_ref[sl, :] = y
        state = state + jnp.where(block_diag, tn(v, kt), 0.0)
    st_ref[...] = compact(state)


def h3_forward(key, halo, q, v, taps, rate_row, age, seg_col, seg_row):
    rows, channels = q.shape
    taps_n = taps.shape[0]
    return kernel_call(
        functools.partial(h3_kernel, taps_n),
        [
            ((rows, channels), f32),
            ((HEAD_DIM, channels), bf16),
            ((rows, channels), f32),
            ((rows // CHUNK, channels, channels), f32),
        ],
        (key, halo, q, v, taps, rate_row, age, seg_col, seg_row),
        scratch=[pltpu.VMEM((rows + taps_n, channels), f32), pltpu.VMEM((8, rows + taps_n, channels), f32)],
        mib=20,
        us=10.0,
    )


def h3_back_kernel(
    taps_n,
    q_ref,
    ks_ref,
    v_ref,
    dy_ref,
    save_ref,
    dst_ref,
    rate_ref,
    segc_ref,
    segr_ref,
    entry_ref,
    key_ref,
    halo_ref,
    taps_ref,
    age_ref,
    rem_ref,
    sin_ref,
    dq_ref,
    dk_ref,
    dhalo_ref,
    dv_ref,
    dtaps_ref,
    drate_ref,
    ext,
    copies,
    dext,
    dcopies,
    tap_acc,
):
    rows, channels = q_ref.shape
    blocks = rows // CHUNK
    pos, mid, q_fac, k_fac, rise, tail, whole = decay_factors(rate_ref[...], CHUNK)
    heads = head_masks(CHUNK, channels)
    block_diag = same_head(channels)
    row = lax.broadcasted_iota(jnp.int32, (CHUNK, CHUNK), 0)
    lane = lax.broadcasted_iota(jnp.int32, (CHUNK, CHUNK), 1)
    dstate = expand(dst_ref[...])
    drate = jnp.zeros((1, channels), f32)
    dext[0:taps_n, :] = jnp.zeros((taps_n, channels), f32)
    dext[rows + taps_n : rows + 2 * taps_n, :] = jnp.zeros((taps_n, channels), f32)
    whole_keeps = []
    for b in range(blocks):
        before = entry_ref[...] if b == 0 else segc_ref[b * CHUNK - 1 : b * CHUNK, :]
        last = segc_ref[(b + 1) * CHUNK - 1 : (b + 1) * CHUNK, :]
        whole_keeps.append(whole * (last == before).astype(f32))
    state_in = expand(sin_ref[...])
    prefix = [jnp.ones_like(whole)]
    for b in range(blocks - 1):
        prefix.append(prefix[-1] * whole_keeps[b])
    for b in reversed(range(blocks)):
        sl = slice(b * CHUNK, (b + 1) * CHUNK)
        seg_c = segc_ref[sl, :]
        seg_r = segr_ref[:, sl]
        before = entry_ref[...] if b == 0 else segc_ref[b * CHUNK - 1 : b * CHUNK, :]
        last = segc_ref[(b + 1) * CHUNK - 1 : (b + 1) * CHUNK, :]
        carried = (seg_c == before).astype(f32)
        final = (seg_c == last).astype(f32)
        q = q_ref[sl, :].astype(f32) * scale
        k = ks_ref[sl, :]
        v = v_ref[sl, :]
        dy = dy_ref[sl, :]
        qf = (q * q_fac).astype(bf16)
        kf = (k * k_fac).astype(bf16)
        rise_c = rise * carried
        tail_c = tail * final
        qr = (q * rise_c).astype(bf16)
        kt = (k * tail_c).astype(bf16)
        same = seg_c == seg_r
        low_mask = (row >= lane) & same
        up_mask = (row <= lane) & same
        state = save_ref[b, :, :] + state_in * prefix[b]
        dstate_b = dstate.astype(bf16)
        dqf = jnp.zeros((CHUNK, channels), f32)
        dkf = jnp.zeros((CHUNK, channels), f32)
        dv = nt(kt, dstate_b)
        zero = jnp.zeros_like(qf)
        for hm in heads:
            kh = jnp.where(hm, kf, zero)
            vh = jnp.where(hm, v, zero)
            scores_t = jnp.where(up_mask, nt(kh, qf), 0.0).astype(bf16)
            dv = dv + jnp.where(hm, nn(scores_t, dy), 0.0)
            dsc = jnp.where(low_mask, nt(dy, vh), 0.0).astype(bf16)
            dsc_t = jnp.where(up_mask, nt(vh, dy), 0.0).astype(bf16)
            dqf = dqf + nn(dsc, kh)
            dkf = dkf + jnp.where(hm, nn(dsc_t, qf), 0.0)
        dqr = nn(dy, state.astype(bf16))
        dkt = nn(v, dstate_b)
        dq_ref[sl, :] = ((dqf * q_fac + dqr * rise_c) * scale).astype(bf16)
        dv_ref[sl, :] = dv.astype(bf16)
        dext[taps_n + b * CHUNK : taps_n + (b + 1) * CHUNK, :] = dkf * k_fac + dkt * tail_c
        part = (pos - mid) * (qf.astype(f32) * dqf - kf.astype(f32) * dkf)
        part = part + (pos + 1.0) * (qr.astype(f32) * dqr)
        part = part + (CHUNK - 1.0 - pos) * (kt.astype(f32) * dkt)
        drate = drate + jnp.sum(part, axis=0, keepdims=True)
        held = dstate * whole_keeps[b]
        drate = drate + CHUNK * jnp.sum(state * held, axis=0, keepdims=True)
        dstate = held + jnp.where(block_diag, tn(dy, qr), 0.0)
    drate_ref[...] = -drate

    total = rows + taps_n
    ext[0:taps_n, :] = halo_ref[...].astype(f32)
    ext[taps_n:total, :] = key_ref[...].astype(f32)
    rolled_down(ext, age_ref, copies, total)
    for r in range(8):
        dcopies[r, 0:total, :] = jnp.where(rem_ref[...] >= r, dext[r : total + r, :], 0.0)
        dcopies[r, total : total + taps_n, :] = jnp.zeros((taps_n, channels), f32)
    tap_acc[...] = jnp.zeros(tap_acc.shape, f32)

    def gathered(start, low, high):
        return filtered(
            dcopies, taps_ref, rem_ref, pl.ds(start, 64), start, 8, taps_n // 8, 64, low, high
        )

    def block(b, carry):
        start = pl.multiple_of(b * 64, 64)
        for low, high in lane_tiles(channels):
            dk_ref[pl.ds(start, 64), low:high] = gathered(start + taps_n, low, high)
        return carry

    lax.fori_loop(0, rows // 64, block, 0)
    for low, high in lane_tiles(channels):
        dhalo_ref[:, low:high] = gathered(0, low, high).astype(bf16)

    def tap_block(b, carry):
        start = pl.multiple_of(b * 64, 64)
        age = age_ref[pl.ds(start + taps_n, 64), :]
        grad = dext[pl.ds(start + taps_n, 64), :]
        for m in range(taps_n // 8):
            held = jnp.where(age >= 8 * m, grad, 0.0)
            for r in range(8):
                term = copies[r, pl.ds(start + taps_n - 8 * m, 64), :] * held
                tap_acc[8 * m + r, :, :] += jnp.sum(term.reshape(8, 8, channels), axis=0)
        return carry

    lax.fori_loop(0, rows // 64, tap_block, 0)
    dtaps_ref[...] = jnp.sum(tap_acc[...], axis=1)


def h3_back_call(q, ks, v, dy, save, dstate, rate_row, seg_col, seg_row, entry, key, halo, taps, age, rem, state_in):
    rows, channels = q.shape
    taps_n = taps.shape[0]
    total = rows + taps_n
    return kernel_call(
        functools.partial(h3_back_kernel, taps_n),
        [
            ((rows, channels), bf16),
            ((rows, channels), f32),
            ((taps_n, channels), bf16),
            ((rows, channels), bf16),
            ((taps_n, channels), f32),
            ((1, channels), f32),
        ],
        (q, ks, v, dy, save, dstate, rate_row, seg_col, seg_row, entry, key, halo, taps, age, rem, state_in),
        scratch=[
            pltpu.VMEM((total, channels), f32),
            pltpu.VMEM((8, total, channels), f32),
            pltpu.VMEM((total + taps_n, channels), f32),
            pltpu.VMEM((8, total + taps_n, channels), f32),
            pltpu.VMEM((taps_n, 8, channels), f32),
        ],
        mib=26,
        us=18.0,
    )


def attend_kernel(resume, finish, lim_ref, q_ref, kv_ref, segc_ref, segr_ref, *refs):
    if resume:
        acc_in, col_in = refs[:2]
        refs = refs[2:]
    rows, channels = q_ref.shape
    n_heads = channels // HEAD_DIM
    heads = head_masks(CHUNK, channels)
    row = lax.broadcasted_iota(jnp.int32, (CHUNK, CHUNK), 0)
    lane = lax.broadcasted_iota(jnp.int32, (CHUNK, CHUNK), 1)
    stat_lane = lax.broadcasted_iota(jnp.int32, (CHUNK, 128), 1)
    for b in range(rows // CHUNK):
        sl = slice(b * CHUNK, (b + 1) * CHUNK)
        low, high, diagonal = lim_ref[0, b], lim_ref[1, b], lim_ref[2, b]
        q = q_ref[sl, :]
        seg_c = segc_ref[sl, :]
        qh = [jnp.where(hm, q, jnp.zeros_like(q)) for hm in heads]

        def step(t, carry):
            at = pl.multiple_of(t * CHUNK, CHUNK)
            keys = kv_ref[pl.ds(at, CHUNK), 0:channels]
            values = kv_ref[pl.ds(at, CHUNK), channels : 2 * channels]
            seg_r = segr_ref[:, pl.ds(at, CHUNK)]
            allowed = (row >= lane + (t - diagonal) * CHUNK) & (seg_c == seg_r)
            new = []
            for h in range(n_heads):
                top, total, acc = carry[h]
                z = jnp.where(allowed, nt(qh[h], keys) * scale, masked_low)
                new_top = jnp.maximum(top, jnp.max(z, axis=1, keepdims=True))
                shrink = jnp.exp(top - new_top)
                e = jnp.where(allowed, jnp.exp(z - new_top), 0.0)
                total = total * shrink + jnp.sum(e, axis=1, keepdims=True)
                acc = acc * shrink + nn(e.astype(bf16), values)
                new.append((new_top, total, acc))
            return tuple(new)

        if resume:
            col = col_in[sl, :]
            held = acc_in[sl, :]
            start = tuple((col[:, h : h + 1], col[:, 8 + h : 9 + h], held) for h in range(n_heads))
        else:
            start = tuple(
                (
                    jnp.full((CHUNK, 1), masked_low, f32),
                    jnp.zeros((CHUNK, 1), f32),
                    jnp.zeros((CHUNK, channels), f32),
                )
                for _ in range(n_heads)
            )
        state = lax.fori_loop(low, high + 1, step, start)
        out = jnp.zeros((CHUNK, channels), f32)
        stats = jnp.zeros((CHUNK, 128), f32)
        for h in range(n_heads):
            top, total, acc = state[h]
            out = jnp.where(heads[h], acc / total if finish else acc, out)
            stats = jnp.where(stat_lane == h, top, stats)
            stats = jnp.where(stat_lane == 8 + h, total, stats)
        refs[0][sl, :] = out
        if finish:
            refs[1][b, :, :] = stats.T[0:16, :]
            refs[2][sl, :] = out.astype(bf16)
        else:
            refs[1][sl, :] = stats


def attend(lim, q, kv, seg_col, seg_tiles, held=(), finish=True):
    rows, channels = q.shape
    if finish:
        outs = [((rows, channels), f32), ((rows // CHUNK, 16, CHUNK), f32), ((rows, channels), bf16)]
    else:
        outs = [((rows, channels), f32), ((rows, 128), f32)]
    return kernel_call(
        functools.partial(attend_kernel, bool(held), finish),
        outs,
        (q, kv, seg_col, seg_tiles, *held),
        scalars=(lim,),
        mib=16 + kv.shape[0] // 512,
        us=5.0,
    )


def attend_back_kernel(
    resume, lim_ref, q_ref, kv_ref, do_ref, o_ref, stat_ref, qseg_ref, kseg_ref, *refs
):
    dq_ref, dkv_ref, acc = refs[-3:]
    rows, channels = q_ref.shape
    n_heads = channels // HEAD_DIM
    heads = head_masks(CHUNK, channels)
    row = lax.broadcasted_iota(jnp.int32, (CHUNK, CHUNK), 0)
    lane = lax.broadcasted_iota(jnp.int32, (CHUNK, CHUNK), 1)
    stat_lane = lax.broadcasted_iota(jnp.int32, (CHUNK, 128), 1)
    acc[...] = jnp.zeros(acc.shape, f32)
    for b in range(rows // CHUNK):
        sl = slice(b * CHUNK, (b + 1) * CHUNK)
        low, high, diagonal = lim_ref[0, b], lim_ref[1, b], lim_ref[2, b]
        q = q_ref[sl, :]
        do = do_ref[sl, :].astype(f32)
        o = o_ref[sl, :]
        seg_q = qseg_ref[:, sl]
        zero = jnp.zeros_like(q)
        qh = [jnp.where(hm, q, zero) for hm in heads]
        cols = jnp.zeros((CHUNK, 128), f32)
        for h in range(n_heads):
            inner = jnp.sum(jnp.where(heads[h], do * o, 0.0), axis=1, keepdims=True)
            cols = jnp.where(stat_lane == h, inner, cols)
        inner_rows = cols.T
        totals = stat_ref[b, 8:16, :]
        inv_cols = jnp.concatenate([1.0 / jnp.maximum(totals, 1e-30), jnp.zeros((120, CHUNK), f32)]).T
        wh = []
        for h in range(n_heads):
            inv = inv_cols[:, h : h + 1]
            wh.append(jnp.where(heads[h], do * inv, 0.0).astype(bf16))

        def step(t, dq):
            at = pl.multiple_of(t * CHUNK, CHUNK)
            keys = kv_ref[pl.ds(at, CHUNK), 0:channels]
            values = kv_ref[pl.ds(at, CHUNK), channels : 2 * channels]
            seg_k = kseg_ref[pl.ds(at, CHUNK), :]
            allowed = (lane >= row + (t - diagonal) * CHUNK) & (seg_k == seg_q)
            dk = jnp.zeros((CHUNK, channels), f32)
            dv = jnp.zeros((CHUNK, channels), f32)
            for h in range(n_heads):
                top = stat_ref[b, h : h + 1, :]
                total = stat_ref[b, 8 + h : 9 + h, :]
                z = jnp.where(allowed, nt(keys, qh[h]) * scale, masked_low)
                e = jnp.where(allowed, jnp.exp(z - top), 0.0)
                dp = nt(values, wh[h])
                dz = (e * (dp - inner_rows[h : h + 1, :] / total)).astype(bf16)
                dk = dk + nn(dz, qh[h])
                dv = dv + nn(e.astype(bf16), wh[h])
                dq = dq + jnp.where(heads[h], tn(dz, keys), 0.0)
            acc[0, pl.ds(at, CHUNK), :] += dk
            acc[1, pl.ds(at, CHUNK), :] += dv
            return dq

        dq = lax.fori_loop(low, high + 1, step, jnp.zeros((CHUNK, channels), f32))
        dq = dq * scale
        if resume:
            dq = dq + refs[0][sl, :]
        dq_ref[sl, :] = dq.astype(dq_ref.dtype)
    dkv_ref[:, 0:channels] = (acc[0] * scale).astype(dkv_ref.dtype)
    dkv_ref[:, channels : 2 * channels] = acc[1].astype(dkv_ref.dtype)


def attend_back(lim, q, kv, do, o, stats, q_tiles, key_col, dq_type, dkv_type, held=()):
    rows, channels = q.shape
    return kernel_call(
        functools.partial(attend_back_kernel, bool(held)),
        [((rows, channels), dq_type), ((kv.shape[0], 2 * channels), dkv_type)],
        (q, kv, do, o, stats, q_tiles, key_col, *held),
        scalars=(lim,),
        scratch=[pltpu.VMEM((2, kv.shape[0], channels), f32)],
        mib=18 + kv.shape[0] // 256,
        us=7.0,
    )


def by_rows(rows, step, body):
    def one(i, carry):
        body(pl.ds(pl.multiple_of(i * step, step), step))
        return carry

    lax.fori_loop(0, rows // step, one, 0)


def norm_kernel(n_add, x_ref, *refs):
    adds, gain_ref, outs = refs[:n_add], refs[n_add], refs[n_add + 1 :]

    def body(at):
        x = x_ref[at, :].astype(f32)
        for a in adds:
            x = x + a[at, :].astype(f32)
        center = jnp.mean(x, axis=1, keepdims=True)
        moved = x - center
        inv = lax.rsqrt(jnp.mean(moved * moved, axis=1, keepdims=True) + epsilon)
        outs[0][at, :] = x
        outs[1][at, :] = (moved * inv * gain_ref[...]).astype(bf16)

    by_rows(x_ref.shape[0], 32, body)


def norm(x, adds, gain):
    shape = x.shape
    return kernel_call(
        functools.partial(norm_kernel, len(adds)),
        [(shape, f32), (shape, bf16)],
        (x, *adds, gain.reshape(1, -1)),
        us=2.0,
    )


def norm_back_kernel(n_add, x_ref, grad_ref, *refs):
    adds, gain_ref, outs = refs[:n_add], refs[n_add], refs[n_add + 1 :]

    def body(at):
        x = x_ref[at, :]
        center = jnp.mean(x, axis=1, keepdims=True)
        moved = x - center
        inv = lax.rsqrt(jnp.mean(moved * moved, axis=1, keepdims=True) + epsilon)
        unit = moved * inv
        d = adds[0][at, :].astype(f32)
        for a in adds[1:]:
            d = d + a[at, :].astype(f32)
        d = d * gain_ref[...]
        mean_d = jnp.mean(d, axis=1, keepdims=True)
        mean_du = jnp.mean(d * unit, axis=1, keepdims=True)
        grad = grad_ref[at, :].astype(f32) + inv * (d - mean_d - unit * mean_du)
        outs[0][at, :] = grad
        outs[1][at, :] = grad.astype(bf16)

    by_rows(x_ref.shape[0], 32, body)


def norm_back(x, grad, adds, gain):
    shape = x.shape
    return kernel_call(
        functools.partial(norm_back_kernel, len(adds)),
        [(shape, f32), (shape, bf16)],
        (x, grad, *adds, gain.reshape(1, -1)),
        us=2.0,
    )


def gelu_both(u):
    inner = 0.7978845608028654 * (u + 0.044715 * (u * u * u))
    t = jnp.tanh(inner)
    half = 0.5 * (1.0 + t)
    slope = half + 0.5 * u * (1.0 - t * t) * (0.7978845608028654 * (1.0 + 0.134145 * (u * u)))
    return u * half, slope


def gather_rows(refs, to):
    size = refs[0].shape[0]
    for i, ref in enumerate(refs):
        to[i * size : (i + 1) * size, :] = ref[...]


def feed_forward_kernel(n, hid, *refs):
    ms, w_ref = refs[:n], refs[n]
    parts, r_ref, slope_ref, rows, up = refs[n + 1 : 2 * n + 1], *refs[2 * n + 1 :]
    size = ms[0].shape[0]
    gather_rows(ms, rows)
    up[...] = nn(rows[...], w_ref[:, 0:hid])

    def body(at):
        r, slope = gelu_both(up[at, :])
        r_ref[at, :] = r.astype(bf16)
        slope_ref[at, :] = slope.astype(bf16)

    by_rows(n * size, 32, body)
    up[...] = nt(r_ref[...], w_ref[:, hid : 2 * hid])
    for i in range(n):
        parts[i][...] = up[i * size : (i + 1) * size, :].astype(bf16)


def feed_forward(ms, w, hid):
    n, size, model = len(ms), ms[0].shape[0], ms[0].shape[1]
    out = kernel_call(
        functools.partial(feed_forward_kernel, n, hid),
        [((size, model), bf16)] * n + [((n * size, hid), bf16)] * 2,
        (*ms, w),
        scratch=[pltpu.VMEM((n * size, model), bf16), pltpu.VMEM((n * size, hid), f32)],
        us=5.0,
    )
    return out[:n], out[n], out[n + 1]


def feed_mid_kernel(n, hid, *refs):
    ms, gs, w_ref, gain_ref = refs[:n], refs[n : 2 * n], refs[2 * n], refs[2 * n + 1]
    outs = refs[2 * n + 2 :]
    parts, r_ref, du_ref, gsum_ref, rows, up, dr = outs[:n], *outs[n:]
    size = ms[0].shape[0]
    gather_rows(ms, rows)
    up[...] = nn(rows[...], w_ref[:, 0:hid])
    gather_rows(gs, rows)
    dr[...] = nn(rows[...], w_ref[:, hid : 2 * hid])

    def body(at):
        r, slope = gelu_both(up[at, :])
        r_ref[at, :] = r.astype(bf16)
        du_ref[at, :] = (dr[at, :] * slope).astype(bf16)

    by_rows(n * size, 32, body)
    finish_back(ms, du_ref, w_ref, gain_ref, parts, gsum_ref, up, hid)


def finish_back(ms, du_ref, w_ref, gain_ref, parts, gsum_ref, part, hid):
    size = ms[0].shape[0]
    part[...] = nt(du_ref[...], w_ref[:, 0:hid])
    gsum = jnp.zeros(gsum_ref.shape, f32)
    for i, m in enumerate(ms):
        own = part[i * size : (i + 1) * size, :]
        parts[i][...] = own.astype(bf16)
        gsum = gsum + jnp.sum(own * m[...].astype(f32), axis=0, keepdims=True)
    gsum_ref[...] = gsum / gain_ref[...]


def feed_mid(ms, gs, w, hid, gain):
    n, size, model = len(ms), ms[0].shape[0], ms[0].shape[1]
    out = kernel_call(
        functools.partial(feed_mid_kernel, n, hid),
        [((size, model), bf16)] * n + [((n * size, hid), bf16)] * 2 + [((1, model), f32)],
        (*ms, *gs, w, gain.reshape(1, -1)),
        scratch=[pltpu.VMEM((n * size, model), bf16)] + [pltpu.VMEM((n * size, hid), f32)] * 2,
        mib=16,
        us=6.0,
    )
    return out[:n], out[n], out[n + 1], out[n + 2]


def feed_back_kernel(n, hid, *refs):
    ms, gs, slope_ref, w_ref, gain_ref = refs[:n], refs[n : 2 * n], refs[2 * n], refs[2 * n + 1], refs[2 * n + 2]
    outs = refs[2 * n + 3 :]
    parts, du_ref, gsum_ref, rows, dr = outs[:n], *outs[n:]
    gather_rows(gs, rows)
    dr[...] = nn(rows[...], w_ref[:, hid : 2 * hid])

    def body(at):
        du_ref[at, :] = (dr[at, :] * slope_ref[at, :].astype(f32)).astype(bf16)

    by_rows(dr.shape[0], 32, body)
    finish_back(ms, du_ref, w_ref, gain_ref, parts, gsum_ref, dr, hid)


def feed_back(ms, gs, slope, w, hid, gain):
    n, size, model = len(ms), ms[0].shape[0], ms[0].shape[1]
    out = kernel_call(
        functools.partial(feed_back_kernel, n, hid),
        [((size, model), bf16)] * n + [((n * size, hid), bf16), ((1, model), f32)],
        (*ms, *gs, slope, w, gain.reshape(1, -1)),
        scratch=[pltpu.VMEM((n * size, model), bf16), pltpu.VMEM((n * size, hid), f32)],
        us=4.0,
    )
    return out[:n], out[n], out[n + 1]


def add_kernel(a_ref, b_ref, out_ref):
    def body(at):
        out_ref[at, :] = (a_ref[at, :].astype(f32) + b_ref[at, :].astype(f32)).astype(bf16)

    by_rows(a_ref.shape[0], 96, body)


def add(a, b):
    return kernel_call(add_kernel, [(a.shape, bf16)], (a, b), mib=4, us=1.0)[0]


def places(core_ref, halves, n, size):
    if halves == 1:
        return [pl.ds(i * size, size) for i in range(n)]
    core, half = core_ref[0], n // 2 * size
    own = [pl.ds(pl.multiple_of(core * half + i * size, size), size) for i in range(n // 2)]
    return own + [pl.ds(pl.multiple_of((1 - core) * half + i * size, size), size) for i in range(n // 2)]


def project_kernel(halves, n, core_ref, *refs):
    ns, w_ref, outs = refs[:n], refs[n], refs[n + 1 :]
    size = ns[0].shape[0]
    for i, to in enumerate(places(core_ref, halves, n, size)):
        x = ns[i][...]
        for j in range(3):
            outs[j][to, :] = nn(x, w_ref[j]).astype(bf16)
        outs[3][to, :] = x
    if len(outs) > 4:
        channels = outs[0].shape[1]
        outs[4][:, 0:channels] = outs[1][...]
        outs[4][:, channels : 2 * channels] = outs[2][...]


def project(core, halves, ns, w, pair=False):
    n, size, model, channels = len(ns), ns[0].shape[0], ns[0].shape[1], w.shape[2]
    return kernel_call(
        functools.partial(project_kernel, halves, n),
        [((n * size, channels), bf16)] * 3
        + [((n * size, model), bf16)]
        + [((n * size, 2 * channels), bf16)] * pair,
        (*ns, w),
        scalars=(core,),
        us=3.0,
    )


def out_kernel(halves, n, index, state, core_ref, y_ref, w_ref, *refs):
    if state:
        sin_ref = refs[4]
        parts, yb_ref = refs[5 : 5 + n], refs[5 + n]
        qr = rising(*refs[:4])
        yb_ref[...] = (y_ref[...] + nt(qr, expand(sin_ref[...]).astype(bf16))).astype(bf16)
    else:
        parts, yb_ref = refs[:n], y_ref
    size = parts[0].shape[0]
    for i, to in enumerate(places(core_ref, halves, n, size)):
        parts[i][...] = nt(yb_ref[to, :], w_ref[index]).astype(bf16)


def project_out(core, halves, n, y, w, index, state=()):
    size, model = y.shape[0] // n, w.shape[1]
    outs = [((size, model), bf16)] * n
    if state:
        outs.append((y.shape, bf16))
    return kernel_call(
        functools.partial(out_kernel, halves, n, index, bool(state)),
        outs,
        (y, w, *state),
        scalars=(core,),
        us=2.0,
    )


def out_back_kernel(halves, n, index, state, core_ref, *refs):
    gs, w_ref = refs[:n], refs[n]
    refs = refs[n + 1 :]
    if state:
        rising_refs = refs[:4]
        refs = refs[4:]
    dy_ref, ordered_ref = refs[0], refs[1]
    size = gs[0].shape[0]
    for i, to in enumerate(places(core_ref, halves, n, size)):
        g = gs[i][...]
        dy_ref[to, :] = nn(g, w_ref[index]).astype(bf16)
        ordered_ref[to, :] = g
    if state:
        refs[2][...] = compact(tn(dy_ref[...], rising(*rising_refs)))


def out_back(core, halves, gs, w, index, state=()):
    n, size, model, channels = len(gs), gs[0].shape[0], gs[0].shape[1], w.shape[2]
    outs = [((n * size, channels), bf16), ((n * size, model), bf16)]
    if state:
        outs.append(((HEAD_DIM, channels), bf16))
    return kernel_call(
        functools.partial(out_back_kernel, halves, n, index, bool(state)),
        outs,
        (*gs, w, *state),
        scalars=(core,),
        us=2.0,
    )


def project_back_kernel(halves, n, kind, count, core_ref, dq_ref, *refs):
    others = refs[:count]
    w_ref, n_ref, gain_ref = refs[count : count + 3]
    outs = refs[count + 3 :]
    parts, cat_ref, gsum_ref = outs[:n], outs[n], outs[n + 1]
    rows, channels = dq_ref.shape
    cat_ref[:, 0:channels] = dq_ref[...]
    if kind == "halo":
        dk_ref, dv_ref, extra_ref = others
        cut = rows - extra_ref.shape[0]
        cat_ref[0:cut, channels : 2 * channels] = dk_ref[0:cut, :].astype(bf16)
        cat_ref[cut:rows, channels : 2 * channels] = (
            dk_ref[cut:rows, :] + extra_ref[...].astype(f32)
        ).astype(bf16)
        cat_ref[:, 2 * channels : 3 * channels] = dv_ref[...].astype(bf16)
    else:
        total = others[0][...].astype(f32)
        for other in others[1:]:
            total = total + other[...].astype(f32)
        cat_ref[:, channels : 3 * channels] = total.astype(bf16)
    size = parts[0].shape[0]
    gsum_ref[...] = jnp.zeros(gsum_ref.shape, f32)
    for i, to in enumerate(places(core_ref, halves, n, size)):
        part = sum(nt(cat_ref[to, j * channels : (j + 1) * channels], w_ref[j]) for j in range(3))
        parts[i][...] = part.astype(bf16)
        gsum_ref[...] += jnp.sum(part * n_ref[to, :].astype(f32), axis=0, keepdims=True)
    gsum_ref[...] = gsum_ref[...] / gain_ref[...]


def project_back(core, halves, n, kind, dq, others, w, normed, gain):
    rows, channels = dq.shape
    size, model = rows // n, normed.shape[1]
    out = kernel_call(
        functools.partial(project_back_kernel, halves, n, kind, len(others)),
        [((size, model), bf16)] * n + [((rows, 3 * channels), bf16), ((1, model), f32)],
        (dq, *others, w, normed, gain.reshape(1, -1)),
        scalars=(core,),
        us=3.0,
    )
    return out[:n], out[n], out[n + 1]


def at_rows(value, start, count):
    return lax.dynamic_slice_in_dim(value, start, count, 0)


def tie(*values):
    return lax.optimization_barrier(values)


class Rows:
    halves = 1
    chunks = 1
    grad_type = f32

    def __init__(self):
        self.blocks = lax.axis_size("ctx")
        self.place = lax.axis_index("ctx")
        self.core = self.place

    def enter(self, rows):
        return rows

    def leave_start(self, rows):
        return rows

    def leave_end(self, rows, there):
        return rows

    def spread(self, rows):
        return [rows]

    def half_sum(self, parts):
        return parts[0]

    def total(self, value):
        return [lax.psum(value, "tp")]

    def local(self, value):
        return value

    def assemble(self, share):
        return lax.all_gather(share, "fsdp", axis=1, tiled=True)

    def setup(self, ids, taps_n, channels):
        row = ids
        ids = ids[0]
        n, rows = self.blocks, ids.shape[0]
        halo = lax.ppermute(ids[rows - taps_n :].astype(bf16), "ctx", [(i, i + 1) for i in range(n - 1)])
        ext = jnp.concatenate([halo.astype(jnp.int32), ids])
        at = jnp.arange(ext.shape[0], dtype=jnp.int32)
        same = ext[:, None] == ext[None, :]
        age = jnp.sum((same & (at[None, :] < at[:, None])).astype(jnp.int32), axis=1)
        rem = jnp.sum((same & (at[None, :] > at[:, None])).astype(jnp.int32), axis=1)
        age, rem = [jnp.broadcast_to(v[:, None], (ext.shape[0], channels)) for v in (age, rem)]
        key_ids = lax.all_gather(ids.astype(bf16), "ctx", axis=0, tiled=True).astype(jnp.int32)
        count = rows // CHUNK
        high = self.place * count + jnp.arange(count, dtype=jnp.int32)
        firsts = ids[::CHUNK]
        low = jnp.sum((key_ids[None, :] < firsts[:, None]).astype(jnp.int32), axis=1) // CHUNK
        limits = jnp.stack([low, high, high])
        entry = ext[taps_n - 1].reshape(1, 1)
        return row, ids[:, None], entry, age, rem, (limits, ids[:, None], row, key_ids[:, None], key_ids[None])

    def from_previous(self, value):
        n = self.blocks
        return lax.ppermute(value, "ctx", [(i, i + 1) for i in range(n - 1)])

    def to_previous(self, value):
        n = self.blocks
        return lax.ppermute(value, "ctx", [(i + 1, i) for i in range(n - 1)])

    def state_before(self, factor, state):
        factors = lax.all_gather(factor.astype(bf16), "ctx").astype(f32)
        states = lax.all_gather(state, "ctx")

        def one(hop, held):
            return states[hop].astype(f32) + factors[hop] * held

        held = lax.fori_loop(0, self.place, one, jnp.zeros(state.shape, f32))
        return held.astype(bf16)

    def grad_after(self, factor, dstate):
        factors = lax.all_gather(factor.astype(bf16), "ctx").astype(f32)
        states = lax.all_gather(dstate, "ctx")

        def one(hop, held):
            at = self.blocks - 1 - hop
            return states[at].astype(f32) + factors[at] * held

        held = lax.fori_loop(0, self.blocks - 1 - self.place, one, jnp.zeros(dstate.shape, f32))
        return held.astype(bf16)

    def attend(self, setup, q, kv):
        limits, col, _, _, key_tiles = setup
        kv = lax.all_gather(kv, "ctx", axis=0, tiled=True)
        return attend(limits, q, kv, col, key_tiles), kv

    def attend_back(self, setup, kept, q, kv, grad, mixed, stats, wait):
        limits, _, tiles, key_col, _ = setup
        dq, dkv = attend_back(limits, q, kept, grad, mixed, stats, tiles, key_col, bf16, bf16)
        return dq, [lax.psum_scatter(dkv, "ctx", scatter_dimension=0, tiled=True)], wait

    def scatter(self, value):
        return [lax.psum_scatter(value, "fsdp", scatter_dimension=0, tiled=True)]

    def scattered(self, parts):
        return parts[0]

    def to_owner(self, value):
        return lax.psum(value, "ctx")

    def owned(self, value, got):
        return got

    def over_places(self, value):
        return lax.psum(value, ("ctx", "tp"))


class Pairs(Rows):
    halves = 2
    chunks = 1
    grad_type = bf16

    def __init__(self):
        self.blocks = 2
        self.core = lax.axis_index("ctx")
        self.chip = lax.axis_index("tp")
        self.place = self.chip // 2
        self.home = self.core == self.place

    def send(self, value, pairs):
        number = [(4 * c + t, 4 * d + u) for (c, t), (d, u) in pairs]
        return lax.ppermute(value, ("ctx", "tp"), number)

    def swap(self, value):
        return lax.ppermute(value, "ctx", [(0, 1), (1, 0)])

    def neighbour(self, value):
        return lax.ppermute(value, "tp", [(0, 1), (1, 0), (2, 3), (3, 2)])

    def across(self, value):
        return lax.ppermute(value, "tp", [(0, 2), (2, 0), (1, 3), (3, 1)])

    def from_home_core(self, value):
        return self.send(value, [((t // 2, t), (1 - t // 2, t)) for t in range(4)])

    def enter(self, rows):
        half = rows.shape[0] // 2
        got = self.from_home_core(at_rows(rows, (1 - self.core) * half, half))
        return jnp.where(self.home, at_rows(rows, self.core * half, half), got)

    def setup(self, ids, taps_n, channels):
        other = self.swap(ids)
        own = jnp.where(self.home, ids, other)
        first = jnp.where(self.core == 0, ids, other)
        before = jnp.where(self.place == 1, first, 0)
        col, before_col, entry, age, rem, own_limits, prev_limits = setup_ids(own, before, taps_n, channels)
        return own, col, entry, age, rem, (own_limits, prev_limits, col, before_col, own, before)

    def in_order(self, own, other):
        first = self.core == 0
        return jnp.concatenate([jnp.where(first, own, other), jnp.where(first, other, own)])

    def leave_start(self, rows):
        return self.across(rows)

    def leave_end(self, rows, there):
        got = self.swap(jnp.where(self.home, there, rows))
        return self.in_order(jnp.where(self.home, rows, there), got)

    def spread(self, rows):
        return [rows, self.swap(rows)]

    def half_sum(self, parts):
        return add(parts[0], self.swap(parts[1]))

    def total(self, value):
        return [value, self.neighbour(value)]

    def local(self, value):
        got = self.send(
            value, [((c, 2 * c + e), (c, 2 - 2 * c + e)) for c in range(2) for e in range(2)]
        )
        return jnp.where(self.home, value, got)

    def around(self, value):
        return [lax.ppermute(value, "fsdp", [(i, i ^ k) for i in range(4)]) for k in (1, 2, 3)]

    def assemble(self, share):
        place, size = lax.axis_index("fsdp"), share.shape[1]
        whole = jnp.zeros((share.shape[0], 4 * size, share.shape[2]), share.dtype)
        for k, part in enumerate([share] + self.around(share)):
            whole = lax.dynamic_update_slice_in_dim(whole, part, (place ^ k) * size, 1)
        return whole

    def from_previous(self, value):
        return self.send(value, [((c, t), (c, t + 2)) for c in range(2) for t in range(2)])

    def to_previous(self, value):
        return self.send(value, [((c, t + 2), (c, t)) for c in range(2) for t in range(2)])

    def state_before(self, factor, state):
        return self.from_previous(state)

    def grad_after(self, factor, dstate):
        return self.to_previous(dstate)

    def attend(self, setup, q, kv):
        own_limits, prev_limits, col, _, tiles, prev_tiles = setup
        before = self.from_previous(kv)
        held = attend(own_limits, q, kv, col, tiles, finish=False)
        return attend(prev_limits, q, before, col, prev_tiles, held), before

    def attend_back(self, setup, before, q, kv, grad, mixed, stats, wait):
        own_limits, prev_limits, col, prev_col, tiles, _ = setup
        dq, dkv_prev = attend_back(prev_limits, q, before, grad, mixed, stats, tiles, prev_col, f32, bf16)
        got = self.to_previous(dkv_prev)
        dq, *wait = tie(dq, *wait)
        dq, dkv = attend_back(own_limits, q, kv, grad, mixed, stats, tiles, col, bf16, f32, (dq,))
        return dq, [dkv, got], wait

    def scatter(self, value):
        place = lax.axis_index("fsdp")
        size = value.shape[0] // 4
        parts = [at_rows(value, place * size, size)]
        for k in (1, 2, 3):
            part = at_rows(value, (place ^ k) * size, size)
            parts.append(lax.ppermute(part, "fsdp", [(i, i ^ k) for i in range(4)]))
        return parts

    def scattered(self, parts):
        return sum(part.astype(f32) for part in parts).astype(bf16)

    def to_owner(self, value):
        return self.send(
            value, [((c, 2 - 2 * c + e), (c, 2 * c + e)) for c in range(2) for e in range(2)]
        )

    def owned(self, value, got):
        value = (value.astype(f32) + got.astype(f32)).astype(bf16)
        return jnp.where(self.home, value, self.from_home_core(value))

    def over_places(self, value):
        for step in (self.swap, self.neighbour, self.across):
            value = (value.astype(f32) + step(value).astype(f32)).astype(bf16)
        return value


def dot_tn(a, b):
    return jnp.einsum("tf,td->fd", a, b, preferred_element_type=f32).astype(bf16)


def feed_shares(reduced):
    width = reduced.shape[1] // 2
    return reduced[:, :width].astype(f32), reduced[:, width:].T.astype(f32)


def mixer_shares(reduced, channels):
    parts = [reduced[:, j * channels : (j + 1) * channels].astype(f32) for j in range(3)]
    return jnp.stack(parts), reduced[:, 3 * channels : 4 * channels].T.astype(f32)


def run(plan, inputs, cotangent, segments, gains, last_gain, in_weight, h3_out, attn_out, up_weight, down_weight, shift_taps, decay_rate):
    halves, chunks = plan.halves, plan.chunks
    pieces = halves * chunks
    slots = lax.axis_size("fsdp")
    hid = up_weight.shape[2]
    channels = h3_out.shape[0]
    taps_n = shift_taps.shape[0]
    share = h3_out.shape[1]
    core = plan.core.astype(jnp.int32).reshape(1)

    def split(value):
        size = value.shape[0] // chunks
        return [value[i * size : (i + 1) * size] for i in range(chunks)]

    def by_piece(spreads):
        return [s[i] for i in range(halves) for s in spreads]

    def by_chunk(parts):
        return [[parts[i * chunks + j] for i in range(halves)] for j in range(chunks)]

    def joined(spreads):
        return jnp.concatenate([piece for s in spreads for piece in s])

    def norms(xs, adds, gain):
        out = [norm(x, a, gain) for x, a in zip(xs, adds)]
        return [o[0] for o in out], [plan.spread(o[1]) for o in out]

    def norm_backs(xs, grads, adds, gain):
        out = [norm_back(x, g, a, gain) for x, g, a in zip(xs, grads, adds)]
        return [o[0] for o in out], [plan.spread(o[1]) for o in out]

    def totals(parts, *others):
        sums = [plan.half_sum(p) for p in parts]
        sums[-1], *others = tie(sums[-1], *others)
        adds = [plan.total(v) for v in sums]
        return (adds, *others) if others else adds

    def with_sums(adds, *others):
        adds[-1][-1], *others = tie(adds[-1][-1], *others)
        return others

    weights0 = plan.local(jnp.concatenate([in_weight[0], h3_out.T[None]]))
    xs = split(plan.enter(inputs[0]))
    seg_row, seg_col, entry, age, rem, setup = plan.setup(segments + 1, taps_n, channels)
    rows = seg_row.shape[1]
    small = jnp.concatenate([shift_taps, decay_rate.reshape(1, -1)])
    feed = [jnp.concatenate([up_weight[i], down_weight[i].T], axis=1) for i in range(2)]
    mix = jnp.concatenate([in_weight[1], attn_out.T[None]])
    x0, n0s = norms(xs, [[]] * chunks, gains[0])
    weights0, small, feed[0], *flat = tie(weights0, small, feed[0], *[p for s in n0s for p in s])
    n0s = [flat[halves * i : halves * (i + 1)] for i in range(chunks)]
    weights0 = plan.assemble(weights0)
    feed[0], mix = tie(plan.local(feed[0]), mix)
    small, mix = plan.local(small), plan.local(mix)
    weights0, age, rem = tie(weights0, age, rem)

    q0, k0, v0, n0 = project(core, halves, by_piece(n0s), weights0)
    k0, small = tie(k0, small)
    halo = plan.from_previous(k0[rows - taps_n :])
    halo, feed[0], feed[1] = tie(halo, feed[0], feed[1])
    feed0 = lax.all_gather(feed[0], "fsdp", axis=0, tiled=True)
    feed[1] = plan.local(feed[1])
    taps, rate_row = small[:taps_n], small[taps_n:]
    factor = jnp.exp(-rate_row * rows) * (entry == seg_row[:, rows - 1 :]).astype(f32)
    ks, state_end, y0, saved = h3_forward(k0, halo, q0, v0, taps, rate_row, age, seg_col, seg_row)
    state_in = plan.state_before(factor, state_end)
    *parts, y0 = project_out(core, halves, pieces, y0, weights0, 3, (q0, rate_row, seg_col, entry, state_in))
    adds, g_in = totals(by_chunk(parts), cotangent[0])
    gs = split(plan.enter(g_in))
    flat = [p for g in gs for p in plan.spread(g)]
    feed0, feed[1], mix, *flat = with_sums(adds, feed0, feed[1], mix, *flat)
    g_ins = [flat[halves * i : halves * (i + 1)] for i in range(chunks)]
    mix1 = lax.all_gather(mix, "fsdp", axis=1, tiled=True)
    feed1 = lax.all_gather(feed[1], "fsdp", axis=0, tiled=True)
    x1, m0s = norms(x0, adds, gains[1])
    out = [feed_forward(m, feed0, hid) for m in m0s]
    parts, r0, slope0 = [[o[i] for o in out] for i in range(3)]
    x2, n2s = norms(x1, totals(parts), gains[2])

    q2, _, _, n2, kv2 = project(core, halves, by_piece(n2s), mix1, True)
    (mixed, stats, mixed_bf), kept = plan.attend(setup, q2, kv2)
    parts = project_out(core, halves, pieces, mixed_bf, mix1, 3)
    x3, m1s = norms(x2, totals(by_chunk(parts)), last_gain)

    out = [feed_mid(m, g, feed1, hid, last_gain) for m, g in zip(m1s, g_ins)]
    parts, r1, du1, gain3 = [[o[i] for o in out] for i in range(4)]
    adds, r1, du1, m1s, g_ins = totals(parts, r1, du1, m1s, g_ins)
    size = r1[0].shape[0] // halves
    last = [
        [
            jnp.einsum(
                "tf,df->td", r[i * size : (i + 1) * size], feed1[:, hid:], preferred_element_type=f32
            ).astype(bf16)
            for i in range(halves)
        ]
        for r in r1
    ]
    feed1_grad = jnp.concatenate(
        [
            dot_tn(joined(m1s), jnp.concatenate(du1)),
            dot_tn(joined(g_ins), jnp.concatenate(r1)),
        ],
        axis=1,
    )
    feed1_grad, *flat = with_sums(adds, feed1_grad, *[p for s in last for p in s])
    feed1_parts = plan.scatter(feed1_grad)
    last = totals([flat[halves * i : halves * (i + 1)] for i in range(chunks)])
    grads, gbs = norm_backs(x3, gs, adds, last_gain)
    dmixed, grad_bf1 = out_back(core, halves, by_piece(gbs), mix1, 3)
    flat = [a for adds in last for a in adds]
    dq, dkv, flat = plan.attend_back(setup, kept, q2, kv2, dmixed, mixed, stats, flat)
    dkv[0], *feed1_parts = tie(dkv[0], *feed1_parts)
    feed1_grad = plan.scattered(feed1_parts)
    count = len(flat) // chunks
    x4 = []
    for i in range(chunks):
        x4.append(x3[i] + sum(a.astype(f32) for a in flat[count * i : count * (i + 1)]))
    x4 = jnp.concatenate(x4).astype(bf16)
    dkv[-1], feed1_grad, x4 = tie(dkv[-1], feed1_grad, x4)
    parts, cat1, gain2 = project_back(core, halves, pieces, "sum", dq, dkv, mix1, n2, gains[2])
    adds, cat1, n2 = totals(by_chunk(parts), cat1, n2)
    mix1_grad = jnp.concatenate([dot_tn(n2, cat1), dot_tn(grad_bf1, mixed_bf)], axis=1)
    mix1_grad, feed1_grad, x4 = with_sums(adds, mix1_grad, feed1_grad, x4)
    x4_there = plan.leave_start(x4)
    mix1_parts = plan.scatter(mix1_grad)
    grads, gbs = norm_backs(x2, grads, adds, gains[2])

    out = [feed_back(m, g, s, feed0, hid, gains[1]) for m, g, s in zip(m0s, gbs, slope0)]
    parts, du0, gain1 = [[o[i] for o in out] for i in range(3)]
    adds, m0s, du0, gbs, r0 = totals(parts, m0s, du0, gbs, r0)
    feed0_grad = jnp.concatenate(
        [
            dot_tn(joined(m0s), jnp.concatenate(du0)),
            dot_tn(joined(gbs), jnp.concatenate(r0)),
        ],
        axis=1,
    )
    feed0_grad, x4_there, *mix1_parts = with_sums(adds, feed0_grad, x4_there, *mix1_parts)
    feed0_parts = plan.scatter(feed0_grad)
    grads, gbs = norm_backs(x1, grads, adds, gains[1])
    mix1_grad = plan.scattered(mix1_parts)
    dy, grad_bf0, dstate = out_back(
        core, halves, by_piece(gbs), weights0, 3, (q0, rate_row, seg_col, entry)
    )
    dstate_end = plan.grad_after(factor, dstate)
    dstate_end, feed1_grad, mix1_grad = tie(dstate_end, feed1_grad, mix1_grad)
    feed1_got, mix1_got = plan.to_owner(feed1_grad), plan.to_owner(mix1_grad)
    dq, dk, dhalo, dv, dtaps, drate = h3_back_call(
        q0, ks, v0, dy, saved, dstate_end, rate_row, seg_col, seg_row, entry, k0, halo, taps, age, rem, state_in
    )
    halo_grad = plan.to_previous(dhalo)
    dq, feed1_got, mix1_got, *feed0_parts = tie(dq, feed1_got, mix1_got, *feed0_parts)
    feed0_grad = plan.scattered(feed0_parts)
    halo_grad, feed0_grad = tie(halo_grad, feed0_grad)
    feed0_got = plan.to_owner(feed0_grad)
    parts, cat0, gain0 = project_back(
        core, halves, pieces, "halo", dq, (dk, dv, halo_grad), weights0, n0, gains[0]
    )
    adds, cat0, n0, dtaps = totals(by_chunk(parts), cat0, n0, dtaps)

    mix0 = jnp.concatenate([dot_tn(n0, cat0), dot_tn(grad_bf0, y0)], axis=1)
    mix0 = mix0.reshape(slots, share, 4 * channels)
    taps_each = taps_n // slots
    small = jnp.concatenate(
        [
            dtaps.reshape(slots, taps_each, channels),
            jnp.pad(
                drate.reshape(-1, slots, HEAD_DIM // slots).transpose(1, 0, 2).reshape(slots, 1, -1),
                ((0, 0), (0, 0), (0, channels - channels // slots)),
            ),
            jnp.concatenate([gain0, sum(gain1), gain2, sum(gain3)]).reshape(4, slots, share).transpose(1, 0, 2),
        ],
        axis=1,
    ).astype(bf16)
    small = jnp.pad(small, ((0, 0), (0, (-small.shape[1]) % 32), (0, 3 * channels)))
    height = share + small.shape[1]
    mix0_parts = plan.scatter(jnp.concatenate([mix0, small], axis=1).reshape(slots * height, 4 * channels))
    grads = [
        norm_back(x, g, a, gains[0])[0].astype(plan.grad_type) for x, g, a in zip(x0, grads, adds)
    ]
    mix0 = plan.scattered(mix0_parts)
    mix0_got = plan.to_owner(mix0)
    grads[-1], feed1_got, mix1_got, x4_there, feed0_got, gain_rows = tie(
        grads[-1], feed1_got, mix1_got, x4_there, feed0_got, mix0[share + taps_each + 1 : share + taps_each + 5, :channels]
    )
    there = [plan.leave_start(g) for g in grads]
    gain_rows = plan.over_places(gain_rows).astype(f32)
    output = plan.leave_end(x4, x4_there)
    feed1 = plan.owned(feed1_grad, feed1_got)
    mix1 = plan.owned(mix1_grad, mix1_got)
    feed0 = plan.owned(feed0_grad, feed0_got)
    mix0 = plan.owned(mix0, mix0_got)
    input_grad = plan.leave_end(jnp.concatenate(grads), jnp.concatenate(there)).astype(f32)
    small = mix0[share:, :channels]
    in0_grad, out0_grad = mixer_shares(mix0[:share], channels)
    dtaps = small[:taps_each].astype(f32)
    drate = small[taps_each, : channels // slots].astype(f32).reshape(-1, HEAD_DIM // slots)
    up0_grad, down0_grad = feed_shares(feed0)
    up1_grad, down1_grad = feed_shares(feed1)
    in1_grad, out1_grad = mixer_shares(mix1, channels)
    return (
        output[None],
        input_grad[None],
        gain_rows[:3],
        gain_rows[3],
        jnp.stack([in0_grad, in1_grad]),
        out0_grad,
        out1_grad,
        jnp.stack([up0_grad, up1_grad]),
        jnp.stack([down0_grad, down1_grad]),
        dtaps,
        drate,
    )


def shards(*arguments):
    paired = lax.axis_size("ctx") == 2 and lax.axis_size("tp") == 4 and lax.axis_size("fsdp") == 4
    return run(Pairs() if paired else Rows(), *arguments)


def solution(mesh):
    placed = (
        P("fsdp", "ctx", None),
        P("fsdp", "ctx", None),
        P("fsdp", "ctx"),
        P(),
        P(),
        P(None, None, "fsdp", "tp"),
        P("tp", "fsdp"),
        P("tp", "fsdp"),
        P(None, "fsdp", "tp"),
        P(None, "tp", "fsdp"),
        P(None, "tp"),
        P("tp", None),
    )
    return jax.shard_map(
        shards,
        mesh=mesh,
        in_specs=placed,
        out_specs=(
            P("fsdp", "ctx", None),
            P("fsdp", "ctx", None),
            P(None, "fsdp"),
            P("fsdp"),
            P(None, None, "fsdp", "tp"),
            P("tp", "fsdp"),
            P("tp", "fsdp"),
            P(None, "fsdp", "tp"),
            P(None, "tp", "fsdp"),
            P("fsdp", "tp"),
            P("tp", "fsdp"),
        ),
        check_vma=False,
    )
```

```python
import functools

import jax
import jax.numpy as jnp
from jax import lax
from jax.experimental import pallas as pl
from jax.experimental.pallas import tpu as pltpu
from jax.sharding import PartitionSpec as P

HEAD_DIM = 64
epsilon = 1e-05
masked_low = -1e30
bf16 = jnp.bfloat16
f32 = jnp.float32
scale = HEAD_DIM ** (-0.5)
CHUNK = 256


def nn(a, b):
    return lax.dot_general(a, b, (((1,), (0,)), ((), ())), preferred_element_type=f32)


def nt(a, b):
    return lax.dot_general(a, b, (((1,), (1,)), ((), ())), preferred_element_type=f32)


def tn(a, b):
    return lax.dot_general(a, b, (((0,), (0,)), ((), ())), preferred_element_type=f32)


def head_masks(rows, channels):
    lane = lax.broadcasted_iota(jnp.int32, (rows, channels), 1)
    return [(lane >= HEAD_DIM * h) & (lane < HEAD_DIM * (h + 1)) for h in range(channels // HEAD_DIM)]


def same_head(channels):
    row = lax.broadcasted_iota(jnp.int32, (channels, channels), 0) // HEAD_DIM
    lane = lax.broadcasted_iota(jnp.int32, (channels, channels), 1) // HEAD_DIM
    return row == lane


def compact(state):
    channels = state.shape[1]
    state = jnp.where(same_head(channels), state, 0.0)
    parts = [state[HEAD_DIM * h : HEAD_DIM * (h + 1), :] for h in range(channels // HEAD_DIM)]
    return sum(parts[1:], parts[0]).astype(bf16)


def expand(small):
    channels = small.shape[1]
    tall = jnp.concatenate([small.astype(f32)] * (channels // HEAD_DIM), axis=0)
    return jnp.where(same_head(channels), tall, 0.0)


def params(mib):
    return pltpu.CompilerParams(vmem_limit_bytes=mib * 1024 * 1024)


def kernel_call(kernel, outs, arrays, scalars=(), scratch=(), mib=12, us=2.0):
    vm = pl.BlockSpec(memory_space=pltpu.VMEM)
    sm = pl.BlockSpec(memory_space=pltpu.SMEM)
    return pl.pallas_call(
        kernel,
        out_shape=[jax.ShapeDtypeStruct(s, d) for s, d in outs],
        in_specs=[sm] * len(scalars) + [vm] * len(arrays),
        out_specs=[vm] * len(outs),
        scratch_shapes=list(scratch),
        compiler_params=params(mib),
        cost_estimate=pl.CostEstimate(flops=int(us * 1e9), bytes_accessed=1000, transcendentals=0),
    )(*scalars, *arrays)


def column_of(row):
    return jnp.broadcast_to(row.astype(f32), (8, row.shape[1])).T[:, 0:1].astype(jnp.int32)


def setup_kernel(taps_n, ids_ref, before_ref, col_ref, before_col_ref, entry_ref, age_ref, rem_ref, own_ref, prev_ref):
    rows = ids_ref.shape[1]
    channels = age_ref.shape[1]
    count = rows // CHUNK
    own, before = ids_ref[...], before_ref[...]
    col_ref[...] = column_of(own)
    before_col_ref[...] = column_of(before)
    entry_ref[...] = before_col_ref[rows - 1 : rows, :]
    lane = lax.broadcasted_iota(jnp.int32, (64, rows), 1)
    row = lax.broadcasted_iota(jnp.int32, (64, rows), 0)
    halo_lane = lane >= rows - taps_n

    def fill(ids, at, start):
        in_own = ids == own
        in_halo = (ids == before) & halo_lane
        both = (in_own & (lane < row + start)).astype(f32) + (in_halo & (lane - rows < row + start)).astype(f32)
        after = (in_own & (lane > row + start)).astype(f32) + (in_halo & (lane - rows > row + start)).astype(f32)
        age = jnp.sum(both, axis=1, keepdims=True).astype(jnp.int32)
        rem = jnp.sum(after, axis=1, keepdims=True).astype(jnp.int32)
        age_ref[at, :] = jnp.broadcast_to(age, (64, channels))
        rem_ref[at, :] = jnp.broadcast_to(rem, (64, channels))

    fill(before_col_ref[rows - 64 : rows, :], pl.ds(0, 64), -64)

    def block(b, carry):
        start = pl.multiple_of(b * 64, 64)
        fill(col_ref[pl.ds(start, 64), :], pl.ds(start + 64, 64), start)
        return carry

    lax.fori_loop(0, rows // 64, block, 0)
    for b in range(count):
        first = own[:, b * CHUNK : b * CHUNK + 1]
        low = jnp.sum((before < first).astype(f32)) + jnp.sum((own < first).astype(f32))
        low = low.astype(jnp.int32) // CHUNK
        own_ref[0, b] = jnp.maximum(low - count, 0)
        own_ref[1, b] = b
        own_ref[2, b] = b
        prev_ref[0, b] = low
        prev_ref[1, b] = count - 1
        prev_ref[2, b] = count + b


def setup_ids(ids, before, taps_n, channels):
    rows = ids.shape[1]
    count = rows // CHUNK
    vm, sm = pl.BlockSpec(memory_space=pltpu.VMEM), pl.BlockSpec(memory_space=pltpu.SMEM)
    shapes = [(rows, 1), (rows, 1), (1, 1), (rows + taps_n, channels), (rows + taps_n, channels), (3, count), (3, count)]
    return pl.pallas_call(
        functools.partial(setup_kernel, taps_n),
        out_shape=[jax.ShapeDtypeStruct(s, jnp.int32) for s in shapes],
        in_specs=[vm] * 2,
        out_specs=[vm] * 5 + [sm] * 2,
        compiler_params=params(8),
        cost_estimate=pl.CostEstimate(flops=int(2e9), bytes_accessed=1000, transcendentals=0),
    )(ids, before)


def tail_and_rise(rate, rows):
    pos = lax.broadcasted_iota(jnp.int32, (rows, rate.shape[1]), 0).astype(f32)
    return jnp.exp(-rate * (rows - 1.0 - pos)), jnp.exp(-rate * (pos + 1.0))


def rising(q_ref, rate_ref, segc_ref, entry_ref):
    rows = q_ref.shape[0]
    rise = tail_and_rise(rate_ref[...], rows)[1]
    rise = rise * ((segc_ref[...] == entry_ref[...]).astype(f32) * scale)
    return (q_ref[...].astype(f32) * rise).astype(bf16)


def rolled_down(ext_ref, age_ref, copies, rows):
    for r in range(8):
        copies[r, 8:rows, :] = jnp.where(age_ref[8:rows, :] >= r, ext_ref[8 - r : rows - r, :], 0.0)


def lane_tiles(channels):
    return [(low, min(low + 128, channels)) for low in range(0, channels, 128)]


def filtered(copies, taps_ref, reach_ref, reach_at, first, step, groups, size, low, high):
    reach = reach_ref[reach_at, low:high]
    base = first if step > 0 else first + step * (groups - 1)
    parts = [None] * groups
    for r in range(8):
        window = copies[r, pl.ds(base, size + 8 * (groups - 1)), low:high]
        for m in range(groups):
            at = 8 * m if step > 0 else 8 * (groups - 1 - m)
            term = window[at : at + size] * taps_ref[8 * m + r : 8 * m + r + 1, low:high]
            parts[m] = term if parts[m] is None else parts[m] + term
    total = parts[0]
    for m in range(1, groups):
        total = total + jnp.where(reach >= 8 * m, parts[m], 0.0)
    return total


def decay_factors(rate_row, rows):
    pos = lax.broadcasted_iota(jnp.int32, (rows, rate_row.shape[1]), 0).astype(f32)
    mid = 0.5 * rows
    q_fac = jnp.exp(-rate_row * (pos - mid))
    k_fac = jnp.exp(rate_row * (pos - mid))
    rise = jnp.exp(-rate_row * (pos + 1.0))
    tail = jnp.exp(-rate_row * (rows - 1.0 - pos))
    whole = jnp.exp(-rate_row * rows)
    return pos, mid, q_fac, k_fac, rise, tail, whole


def h3_kernel(
    taps_n,
    key_ref,
    halo_ref,
    q_ref,
    v_ref,
    taps_ref,
    rate_ref,
    age_ref,
    segc_ref,
    segr_ref,
    ks_ref,
    st_ref,
    y_ref,
    save_ref,
    ext,
    copies,
):
    rows, channels = key_ref.shape
    ext[0:taps_n, :] = halo_ref[...].astype(f32)
    ext[taps_n : taps_n + rows, :] = key_ref[...].astype(f32)
    rolled_down(ext, age_ref, copies, rows + taps_n)

    def block(b, carry):
        start = pl.multiple_of(b * 64, 64)
        for low, high in lane_tiles(channels):
            ks_ref[pl.ds(start, 64), low:high] = filtered(
                copies, taps_ref, age_ref, pl.ds(start + taps_n, 64), start + taps_n, -8, taps_n // 8, 64, low, high
            )
        return carry

    lax.fori_loop(0, rows // 64, block, 0)

    blocks = rows // CHUNK
    _, _, q_fac, k_fac, rise, tail, whole = decay_factors(rate_ref[...], CHUNK)
    heads = head_masks(CHUNK, channels)
    block_diag = same_head(channels)
    causal = lax.broadcasted_iota(jnp.int32, (CHUNK, CHUNK), 0) >= lax.broadcasted_iota(
        jnp.int32, (CHUNK, CHUNK), 1
    )
    state = jnp.zeros((channels, channels), f32)
    for b in range(blocks):
        sl = slice(b * CHUNK, (b + 1) * CHUNK)
        seg_c = segc_ref[sl, :]
        seg_r = segr_ref[:, sl]
        last = segc_ref[(b + 1) * CHUNK - 1 : (b + 1) * CHUNK, :]
        final = (seg_c == last).astype(f32)
        q = q_ref[sl, :].astype(f32) * scale
        k = ks_ref[sl, :]
        v = v_ref[sl, :]
        qf = (q * q_fac).astype(bf16)
        kf = (k * k_fac).astype(bf16)
        kt = (k * (tail * final)).astype(bf16)
        allowed = causal & (seg_c == seg_r)
        save_ref[b, :, :] = state
        y = jnp.zeros((CHUNK, channels), f32)
        if b > 0:
            before = segc_ref[b * CHUNK - 1 : b * CHUNK, :]
            qr = (q * (rise * (seg_c == before).astype(f32))).astype(bf16)
            y = nt(qr, state.astype(bf16))
            state = state * (whole * (last == before).astype(f32))
        for hm in heads:
            scores = nt(jnp.where(hm, qf, jnp.zeros_like(qf)), kf)
            scores = jnp.where(allowed, scores, 0.0).astype(bf16)
            y = y + jnp.where(hm, nn(scores, v), 0.0)
        y_ref[sl, :] = y
        state = state + jnp.where(block_diag, tn(v, kt), 0.0)
    st_ref[...] = compact(state)


def h3_forward(key, halo, q, v, taps, rate_row, age, seg_col, seg_row):
    rows, channels = q.shape
    taps_n = taps.shape[0]
    return kernel_call(
        functools.partial(h3_kernel, taps_n),
        [
            ((rows, channels), f32),
            ((HEAD_DIM, channels), bf16),
            ((rows, channels), f32),
            ((rows // CHUNK, channels, channels), f32),
        ],
        (key, halo, q, v, taps, rate_row, age, seg_col, seg_row),
        scratch=[pltpu.VMEM((rows + taps_n, channels), f32), pltpu.VMEM((8, rows + taps_n, channels), f32)],
        mib=20,
        us=10.0,
    )


def h3_back_kernel(
    taps_n,
    q_ref,
    ks_ref,
    v_ref,
    dy_ref,
    save_ref,
    dst_ref,
    rate_ref,
    segc_ref,
    segr_ref,
    entry_ref,
    key_ref,
    halo_ref,
    taps_ref,
    age_ref,
    rem_ref,
    sin_ref,
    dq_ref,
    dk_ref,
    dhalo_ref,
    dv_ref,
    dtaps_ref,
    drate_ref,
    ext,
    copies,
    dext,
    dcopies,
    tap_acc,
):
    rows, channels = q_ref.shape
    blocks = rows // CHUNK
    pos, mid, q_fac, k_fac, rise, tail, whole = decay_factors(rate_ref[...], CHUNK)
    heads = head_masks(CHUNK, channels)
    block_diag = same_head(channels)
    row = lax.broadcasted_iota(jnp.int32, (CHUNK, CHUNK), 0)
    lane = lax.broadcasted_iota(jnp.int32, (CHUNK, CHUNK), 1)
    dstate = expand(dst_ref[...])
    drate = jnp.zeros((1, channels), f32)
    dext[0:taps_n, :] = jnp.zeros((taps_n, channels), f32)
    dext[rows + taps_n : rows + 2 * taps_n, :] = jnp.zeros((taps_n, channels), f32)
    whole_keeps = []
    for b in range(blocks):
        before = entry_ref[...] if b == 0 else segc_ref[b * CHUNK - 1 : b * CHUNK, :]
        last = segc_ref[(b + 1) * CHUNK - 1 : (b + 1) * CHUNK, :]
        whole_keeps.append(whole * (last == before).astype(f32))
    state_in = expand(sin_ref[...])
    prefix = [jnp.ones_like(whole)]
    for b in range(blocks - 1):
        prefix.append(prefix[-1] * whole_keeps[b])
    for b in reversed(range(blocks)):
        sl = slice(b * CHUNK, (b + 1) * CHUNK)
        seg_c = segc_ref[sl, :]
        seg_r = segr_ref[:, sl]
        before = entry_ref[...] if b == 0 else segc_ref[b * CHUNK - 1 : b * CHUNK, :]
        last = segc_ref[(b + 1) * CHUNK - 1 : (b + 1) * CHUNK, :]
        carried = (seg_c == before).astype(f32)
        final = (seg_c == last).astype(f32)
        q = q_ref[sl, :].astype(f32) * scale
        k = ks_ref[sl, :]
        v = v_ref[sl, :]
        dy = dy_ref[sl, :]
        qf = (q * q_fac).astype(bf16)
        kf = (k * k_fac).astype(bf16)
        rise_c = rise * carried
        tail_c = tail * final
        qr = (q * rise_c).astype(bf16)
        kt = (k * tail_c).astype(bf16)
        same = seg_c == seg_r
        low_mask = (row >= lane) & same
        up_mask = (row <= lane) & same
        state = save_ref[b, :, :] + state_in * prefix[b]
        dstate_b = dstate.astype(bf16)
        dqf = jnp.zeros((CHUNK, channels), f32)
        dkf = jnp.zeros((CHUNK, channels), f32)
        dv = nt(kt, dstate_b)
        zero = jnp.zeros_like(qf)
        for hm in heads:
            kh = jnp.where(hm, kf, zero)
            vh = jnp.where(hm, v, zero)
            scores_t = jnp.where(up_mask, nt(kh, qf), 0.0).astype(bf16)
            dv = dv + jnp.where(hm, nn(scores_t, dy), 0.0)
            dsc = jnp.where(low_mask, nt(dy, vh), 0.0).astype(bf16)
            dsc_t = jnp.where(up_mask, nt(vh, dy), 0.0).astype(bf16)
            dqf = dqf + nn(dsc, kh)
            dkf = dkf + jnp.where(hm, nn(dsc_t, qf), 0.0)
        dqr = nn(dy, state.astype(bf16))
        dkt = nn(v, dstate_b)
        dq_ref[sl, :] = ((dqf * q_fac + dqr * rise_c) * scale).astype(bf16)
        dv_ref[sl, :] = dv.astype(bf16)
        dext[taps_n + b * CHUNK : taps_n + (b + 1) * CHUNK, :] = dkf * k_fac + dkt * tail_c
        part = (pos - mid) * (qf.astype(f32) * dqf - kf.astype(f32) * dkf)
        part = part + (pos + 1.0) * (qr.astype(f32) * dqr)
        part = part + (CHUNK - 1.0 - pos) * (kt.astype(f32) * dkt)
        drate = drate + jnp.sum(part, axis=0, keepdims=True)
        held = dstate * whole_keeps[b]
        drate = drate + CHUNK * jnp.sum(state * held, axis=0, keepdims=True)
        dstate = held + jnp.where(block_diag, tn(dy, qr), 0.0)
    drate_ref[...] = -drate

    total = rows + taps_n
    ext[0:taps_n, :] = halo_ref[...].astype(f32)
    ext[taps_n:total, :] = key_ref[...].astype(f32)
    rolled_down(ext, age_ref, copies, total)
    for r in range(8):
        dcopies[r, 0:total, :] = jnp.where(rem_ref[...] >= r, dext[r : total + r, :], 0.0)
        dcopies[r, total : total + taps_n, :] = jnp.zeros((taps_n, channels), f32)
    tap_acc[...] = jnp.zeros(tap_acc.shape, f32)

    def gathered(start, low, high):
        return filtered(
            dcopies, taps_ref, rem_ref, pl.ds(start, 64), start, 8, taps_n // 8, 64, low, high
        )

    def block(b, carry):
        start = pl.multiple_of(b * 64, 64)
        for low, high in lane_tiles(channels):
            dk_ref[pl.ds(start, 64), low:high] = gathered(start + taps_n, low, high)
        return carry

    lax.fori_loop(0, rows // 64, block, 0)
    for low, high in lane_tiles(channels):
        dhalo_ref[:, low:high] = gathered(0, low, high).astype(bf16)

    def tap_block(b, carry):
        start = pl.multiple_of(b * 64, 64)
        age = age_ref[pl.ds(start + taps_n, 64), :]
        grad = dext[pl.ds(start + taps_n, 64), :]
        for m in range(taps_n // 8):
            held = jnp.where(age >= 8 * m, grad, 0.0)
            for r in range(8):
                term = copies[r, pl.ds(start + taps_n - 8 * m, 64), :] * held
                tap_acc[8 * m + r, :, :] += jnp.sum(term.reshape(8, 8, channels), axis=0)
        return carry

    lax.fori_loop(0, rows // 64, tap_block, 0)
    dtaps_ref[...] = jnp.sum(tap_acc[...], axis=1)


def h3_back_call(q, ks, v, dy, save, dstate, rate_row, seg_col, seg_row, entry, key, halo, taps, age, rem, state_in):
    rows, channels = q.shape
    taps_n = taps.shape[0]
    total = rows + taps_n
    return kernel_call(
        functools.partial(h3_back_kernel, taps_n),
        [
            ((rows, channels), bf16),
            ((rows, channels), f32),
            ((taps_n, channels), bf16),
            ((rows, channels), bf16),
            ((taps_n, channels), f32),
            ((1, channels), f32),
        ],
        (q, ks, v, dy, save, dstate, rate_row, seg_col, seg_row, entry, key, halo, taps, age, rem, state_in),
        scratch=[
            pltpu.VMEM((total, channels), f32),
            pltpu.VMEM((8, total, channels), f32),
            pltpu.VMEM((total + taps_n, channels), f32),
            pltpu.VMEM((8, total + taps_n, channels), f32),
            pltpu.VMEM((taps_n, 8, channels), f32),
        ],
        mib=26,
        us=18.0,
    )


def attend_kernel(resume, finish, lim_ref, q_ref, kv_ref, segc_ref, segr_ref, *refs):
    if resume:
        acc_in, col_in = refs[:2]
        refs = refs[2:]
    rows, channels = q_ref.shape
    n_heads = channels // HEAD_DIM
    heads = head_masks(CHUNK, channels)
    row = lax.broadcasted_iota(jnp.int32, (CHUNK, CHUNK), 0)
    lane = lax.broadcasted_iota(jnp.int32, (CHUNK, CHUNK), 1)
    stat_lane = lax.broadcasted_iota(jnp.int32, (CHUNK, 128), 1)
    for b in range(rows // CHUNK):
        sl = slice(b * CHUNK, (b + 1) * CHUNK)
        low, high, diagonal = lim_ref[0, b], lim_ref[1, b], lim_ref[2, b]
        q = q_ref[sl, :]
        seg_c = segc_ref[sl, :]
        qh = [jnp.where(hm, q, jnp.zeros_like(q)) for hm in heads]

        def step(t, carry):
            at = pl.multiple_of(t * CHUNK, CHUNK)
            keys = kv_ref[pl.ds(at, CHUNK), 0:channels]
            values = kv_ref[pl.ds(at, CHUNK), channels : 2 * channels]
            seg_r = segr_ref[:, pl.ds(at, CHUNK)]
            allowed = (row >= lane + (t - diagonal) * CHUNK) & (seg_c == seg_r)
            new = []
            for h in range(n_heads):
                top, total, acc = carry[h]
                z = jnp.where(allowed, nt(qh[h], keys) * scale, masked_low)
                new_top = jnp.maximum(top, jnp.max(z, axis=1, keepdims=True))
                shrink = jnp.exp(top - new_top)
                e = jnp.where(allowed, jnp.exp(z - new_top), 0.0)
                total = total * shrink + jnp.sum(e, axis=1, keepdims=True)
                acc = acc * shrink + nn(e.astype(bf16), values)
                new.append((new_top, total, acc))
            return tuple(new)

        if resume:
            col = col_in[sl, :]
            held = acc_in[sl, :]
            start = tuple((col[:, h : h + 1], col[:, 8 + h : 9 + h], held) for h in range(n_heads))
        else:
            start = tuple(
                (
                    jnp.full((CHUNK, 1), masked_low, f32),
                    jnp.zeros((CHUNK, 1), f32),
                    jnp.zeros((CHUNK, channels), f32),
                )
                for _ in range(n_heads)
            )
        state = lax.fori_loop(low, high + 1, step, start)
        out = jnp.zeros((CHUNK, channels), f32)
        stats = jnp.zeros((CHUNK, 128), f32)
        for h in range(n_heads):
            top, total, acc = state[h]
            out = jnp.where(heads[h], acc / total if finish else acc, out)
            stats = jnp.where(stat_lane == h, top, stats)
            stats = jnp.where(stat_lane == 8 + h, total, stats)
        refs[0][sl, :] = out
        if finish:
            refs[1][b, :, :] = stats.T[0:16, :]
            refs[2][sl, :] = out.astype(bf16)
        else:
            refs[1][sl, :] = stats


def attend(lim, q, kv, seg_col, seg_tiles, held=(), finish=True):
    rows, channels = q.shape
    if finish:
        outs = [((rows, channels), f32), ((rows // CHUNK, 16, CHUNK), f32), ((rows, channels), bf16)]
    else:
        outs = [((rows, channels), f32), ((rows, 128), f32)]
    return kernel_call(
        functools.partial(attend_kernel, bool(held), finish),
        outs,
        (q, kv, seg_col, seg_tiles, *held),
        scalars=(lim,),
        mib=16 + kv.shape[0] // 512,
        us=5.0,
    )


def attend_back_kernel(
    resume, lim_ref, q_ref, kv_ref, do_ref, o_ref, stat_ref, qseg_ref, kseg_ref, *refs
):
    dq_ref, dkv_ref, acc = refs[-3:]
    rows, channels = q_ref.shape
    n_heads = channels // HEAD_DIM
    heads = head_masks(CHUNK, channels)
    row = lax.broadcasted_iota(jnp.int32, (CHUNK, CHUNK), 0)
    lane = lax.broadcasted_iota(jnp.int32, (CHUNK, CHUNK), 1)
    stat_lane = lax.broadcasted_iota(jnp.int32, (CHUNK, 128), 1)
    acc[...] = jnp.zeros(acc.shape, f32)
    for b in range(rows // CHUNK):
        sl = slice(b * CHUNK, (b + 1) * CHUNK)
        low, high, diagonal = lim_ref[0, b], lim_ref[1, b], lim_ref[2, b]
        q = q_ref[sl, :]
        do = do_ref[sl, :].astype(f32)
        o = o_ref[sl, :]
        seg_q = qseg_ref[:, sl]
        zero = jnp.zeros_like(q)
        qh = [jnp.where(hm, q, zero) for hm in heads]
        cols = jnp.zeros((CHUNK, 128), f32)
        for h in range(n_heads):
            inner = jnp.sum(jnp.where(heads[h], do * o, 0.0), axis=1, keepdims=True)
            cols = jnp.where(stat_lane == h, inner, cols)
        inner_rows = cols.T
        totals = stat_ref[b, 8:16, :]
        inv_cols = jnp.concatenate([1.0 / jnp.maximum(totals, 1e-30), jnp.zeros((120, CHUNK), f32)]).T
        wh = []
        for h in range(n_heads):
            inv = inv_cols[:, h : h + 1]
            wh.append(jnp.where(heads[h], do * inv, 0.0).astype(bf16))

        def step(t, dq):
            at = pl.multiple_of(t * CHUNK, CHUNK)
            keys = kv_ref[pl.ds(at, CHUNK), 0:channels]
            values = kv_ref[pl.ds(at, CHUNK), channels : 2 * channels]
            seg_k = kseg_ref[pl.ds(at, CHUNK), :]
            allowed = (lane >= row + (t - diagonal) * CHUNK) & (seg_k == seg_q)
            dk = jnp.zeros((CHUNK, channels), f32)
            dv = jnp.zeros((CHUNK, channels), f32)
            for h in range(n_heads):
                top = stat_ref[b, h : h + 1, :]
                total = stat_ref[b, 8 + h : 9 + h, :]
                z = jnp.where(allowed, nt(keys, qh[h]) * scale, masked_low)
                e = jnp.where(allowed, jnp.exp(z - top), 0.0)
                dp = nt(values, wh[h])
                dz = (e * (dp - inner_rows[h : h + 1, :] / total)).astype(bf16)
                dk = dk + nn(dz, qh[h])
                dv = dv + nn(e.astype(bf16), wh[h])
                dq = dq + jnp.where(heads[h], tn(dz, keys), 0.0)
            acc[0, pl.ds(at, CHUNK), :] += dk
            acc[1, pl.ds(at, CHUNK), :] += dv
            return dq

        dq = lax.fori_loop(low, high + 1, step, jnp.zeros((CHUNK, channels), f32))
        dq = dq * scale
        if resume:
            dq = dq + refs[0][sl, :]
        dq_ref[sl, :] = dq.astype(dq_ref.dtype)
    dkv_ref[:, 0:channels] = (acc[0] * scale).astype(dkv_ref.dtype)
    dkv_ref[:, channels : 2 * channels] = acc[1].astype(dkv_ref.dtype)


def attend_back(lim, q, kv, do, o, stats, q_tiles, key_col, dq_type, dkv_type, held=()):
    rows, channels = q.shape
    return kernel_call(
        functools.partial(attend_back_kernel, bool(held)),
        [((rows, channels), dq_type), ((kv.shape[0], 2 * channels), dkv_type)],
        (q, kv, do, o, stats, q_tiles, key_col, *held),
        scalars=(lim,),
        scratch=[pltpu.VMEM((2, kv.shape[0], channels), f32)],
        mib=18 + kv.shape[0] // 256,
        us=7.0,
    )


def by_rows(rows, step, body):
    def one(i, carry):
        body(pl.ds(pl.multiple_of(i * step, step), step))
        return carry

    lax.fori_loop(0, rows // step, one, 0)


def norm_kernel(n_add, x_ref, *refs):
    adds, gain_ref, outs = refs[:n_add], refs[n_add], refs[n_add + 1 :]

    def body(at):
        x = x_ref[at, :].astype(f32)
        for a in adds:
            x = x + a[at, :].astype(f32)
        center = jnp.mean(x, axis=1, keepdims=True)
        moved = x - center
        inv = lax.rsqrt(jnp.mean(moved * moved, axis=1, keepdims=True) + epsilon)
        outs[0][at, :] = x
        outs[1][at, :] = (moved * inv * gain_ref[...]).astype(bf16)

    by_rows(x_ref.shape[0], 128, body)


def norm(x, adds, gain):
    shape = x.shape
    return kernel_call(
        functools.partial(norm_kernel, len(adds)),
        [(shape, f32), (shape, bf16)],
        (x, *adds, gain.reshape(1, -1)),
        us=2.0,
    )


def norm_back_kernel(n_add, x_ref, grad_ref, *refs):
    adds, gain_ref, outs = refs[:n_add], refs[n_add], refs[n_add + 1 :]

    def body(at):
        x = x_ref[at, :]
        center = jnp.mean(x, axis=1, keepdims=True)
        moved = x - center
        inv = lax.rsqrt(jnp.mean(moved * moved, axis=1, keepdims=True) + epsilon)
        unit = moved * inv
        d = adds[0][at, :].astype(f32)
        for a in adds[1:]:
            d = d + a[at, :].astype(f32)
        d = d * gain_ref[...]
        mean_d = jnp.mean(d, axis=1, keepdims=True)
        mean_du = jnp.mean(d * unit, axis=1, keepdims=True)
        grad = grad_ref[at, :].astype(f32) + inv * (d - mean_d - unit * mean_du)
        outs[0][at, :] = grad
        outs[1][at, :] = grad.astype(bf16)

    by_rows(x_ref.shape[0], 128, body)


def norm_back(x, grad, adds, gain):
    shape = x.shape
    return kernel_call(
        functools.partial(norm_back_kernel, len(adds)),
        [(shape, f32), (shape, bf16)],
        (x, grad, *adds, gain.reshape(1, -1)),
        us=2.0,
    )


def gelu_both(u):
    inner = 0.7978845608028654 * (u + 0.044715 * (u * u * u))
    t = jnp.tanh(inner)
    half = 0.5 * (1.0 + t)
    slope = half + 0.5 * u * (1.0 - t * t) * (0.7978845608028654 * (1.0 + 0.134145 * (u * u)))
    return u * half, slope


def gather_rows(refs, to):
    size = refs[0].shape[0]
    for i, ref in enumerate(refs):
        to[i * size : (i + 1) * size, :] = ref[...]


def feed_forward_kernel(n, hid, *refs):
    ms, w_ref = refs[:n], refs[n]
    parts, r_ref, slope_ref, rows, up = refs[n + 1 : 2 * n + 1], *refs[2 * n + 1 :]
    size = ms[0].shape[0]
    gather_rows(ms, rows)
    up[...] = nn(rows[...], w_ref[:, 0:hid])

    def body(at):
        r, slope = gelu_both(up[at, :])
        r_ref[at, :] = r.astype(bf16)
        slope_ref[at, :] = slope.astype(bf16)

    by_rows(n * size, 32, body)
    up[...] = nt(r_ref[...], w_ref[:, hid : 2 * hid])
    for i in range(n):
        parts[i][...] = up[i * size : (i + 1) * size, :].astype(bf16)


def feed_forward(ms, w, hid):
    n, size, model = len(ms), ms[0].shape[0], ms[0].shape[1]
    out = kernel_call(
        functools.partial(feed_forward_kernel, n, hid),
        [((size, model), bf16)] * n + [((n * size, hid), bf16)] * 2,
        (*ms, w),
        scratch=[pltpu.VMEM((n * size, model), bf16), pltpu.VMEM((n * size, hid), f32)],
        us=5.0,
    )
    return out[:n], out[n], out[n + 1]


def feed_mid_kernel(n, hid, *refs):
    ms, gs, w_ref, gain_ref = refs[:n], refs[n : 2 * n], refs[2 * n], refs[2 * n + 1]
    outs = refs[2 * n + 2 :]
    parts, r_ref, du_ref, gsum_ref, rows, up, dr = outs[:n], *outs[n:]
    size = ms[0].shape[0]
    gather_rows(ms, rows)
    up[...] = nn(rows[...], w_ref[:, 0:hid])
    gather_rows(gs, rows)
    dr[...] = nn(rows[...], w_ref[:, hid : 2 * hid])

    def body(at):
        r, slope = gelu_both(up[at, :])
        r_ref[at, :] = r.astype(bf16)
        du_ref[at, :] = (dr[at, :] * slope).astype(bf16)

    by_rows(n * size, 32, body)
    finish_back(ms, du_ref, w_ref, gain_ref, parts, gsum_ref, up, hid)


def finish_back(ms, du_ref, w_ref, gain_ref, parts, gsum_ref, part, hid):
    size = ms[0].shape[0]
    part[...] = nt(du_ref[...], w_ref[:, 0:hid])
    gsum = jnp.zeros(gsum_ref.shape, f32)
    for i, m in enumerate(ms):
        own = part[i * size : (i + 1) * size, :]
        parts[i][...] = own.astype(bf16)
        gsum = gsum + jnp.sum(own * m[...].astype(f32), axis=0, keepdims=True)
    gsum_ref[...] = gsum / gain_ref[...]


def feed_mid(ms, gs, w, hid, gain):
    n, size, model = len(ms), ms[0].shape[0], ms[0].shape[1]
    out = kernel_call(
        functools.partial(feed_mid_kernel, n, hid),
        [((size, model), bf16)] * n + [((n * size, hid), bf16)] * 2 + [((1, model), f32)],
        (*ms, *gs, w, gain.reshape(1, -1)),
        scratch=[pltpu.VMEM((n * size, model), bf16)] + [pltpu.VMEM((n * size, hid), f32)] * 2,
        mib=16,
        us=6.0,
    )
    return out[:n], out[n], out[n + 1], out[n + 2]


def feed_back_kernel(n, hid, *refs):
    ms, gs, slope_ref, w_ref, gain_ref = refs[:n], refs[n : 2 * n], refs[2 * n], refs[2 * n + 1], refs[2 * n + 2]
    outs = refs[2 * n + 3 :]
    parts, du_ref, gsum_ref, rows, dr = outs[:n], *outs[n:]
    gather_rows(gs, rows)
    dr[...] = nn(rows[...], w_ref[:, hid : 2 * hid])

    def body(at):
        du_ref[at, :] = (dr[at, :] * slope_ref[at, :].astype(f32)).astype(bf16)

    by_rows(dr.shape[0], 32, body)
    finish_back(ms, du_ref, w_ref, gain_ref, parts, gsum_ref, dr, hid)


def feed_back(ms, gs, slope, w, hid, gain):
    n, size, model = len(ms), ms[0].shape[0], ms[0].shape[1]
    out = kernel_call(
        functools.partial(feed_back_kernel, n, hid),
        [((size, model), bf16)] * n + [((n * size, hid), bf16), ((1, model), f32)],
        (*ms, *gs, slope, w, gain.reshape(1, -1)),
        scratch=[pltpu.VMEM((n * size, model), bf16), pltpu.VMEM((n * size, hid), f32)],
        us=4.0,
    )
    return out[:n], out[n], out[n + 1]


def add_kernel(a_ref, b_ref, out_ref):
    def body(at):
        out_ref[at, :] = (a_ref[at, :].astype(f32) + b_ref[at, :].astype(f32)).astype(bf16)

    by_rows(a_ref.shape[0], 96, body)


def add(a, b):
    return kernel_call(add_kernel, [(a.shape, bf16)], (a, b), mib=4, us=1.0)[0]


def places(core_ref, halves, n, size):
    if halves == 1:
        return [pl.ds(i * size, size) for i in range(n)]
    core, half = core_ref[0], n // 2 * size
    own = [pl.ds(pl.multiple_of(core * half + i * size, size), size) for i in range(n // 2)]
    return own + [pl.ds(pl.multiple_of((1 - core) * half + i * size, size), size) for i in range(n // 2)]


def project_kernel(halves, n, core_ref, *refs):
    ns, w_ref, outs = refs[:n], refs[n], refs[n + 1 :]
    size = ns[0].shape[0]
    for i, to in enumerate(places(core_ref, halves, n, size)):
        x = ns[i][...]
        for j in range(3):
            outs[j][to, :] = nn(x, w_ref[j]).astype(bf16)
        outs[3][to, :] = x
    if len(outs) > 4:
        channels = outs[0].shape[1]
        outs[4][:, 0:channels] = outs[1][...]
        outs[4][:, channels : 2 * channels] = outs[2][...]


def project(core, halves, ns, w, pair=False):
    n, size, model, channels = len(ns), ns[0].shape[0], ns[0].shape[1], w.shape[2]
    return kernel_call(
        functools.partial(project_kernel, halves, n),
        [((n * size, channels), bf16)] * 3
        + [((n * size, model), bf16)]
        + [((n * size, 2 * channels), bf16)] * pair,
        (*ns, w),
        scalars=(core,),
        us=3.0,
    )


def out_kernel(halves, n, index, state, core_ref, y_ref, w_ref, *refs):
    if state:
        sin_ref = refs[4]
        parts, yb_ref = refs[5 : 5 + n], refs[5 + n]
        qr = rising(*refs[:4])
        yb_ref[...] = (y_ref[...] + nt(qr, expand(sin_ref[...]).astype(bf16))).astype(bf16)
    else:
        parts, yb_ref = refs[:n], y_ref
    size = parts[0].shape[0]
    for i, to in enumerate(places(core_ref, halves, n, size)):
        parts[i][...] = nt(yb_ref[to, :], w_ref[index]).astype(bf16)


def project_out(core, halves, n, y, w, index, state=()):
    size, model = y.shape[0] // n, w.shape[1]
    outs = [((size, model), bf16)] * n
    if state:
        outs.append((y.shape, bf16))
    return kernel_call(
        functools.partial(out_kernel, halves, n, index, bool(state)),
        outs,
        (y, w, *state),
        scalars=(core,),
        us=2.0,
    )


def out_back_kernel(halves, n, index, state, core_ref, *refs):
    gs, w_ref = refs[:n], refs[n]
    refs = refs[n + 1 :]
    if state:
        rising_refs = refs[:4]
        refs = refs[4:]
    dy_ref, ordered_ref = refs[0], refs[1]
    size = gs[0].shape[0]
    for i, to in enumerate(places(core_ref, halves, n, size)):
        g = gs[i][...]
        dy_ref[to, :] = nn(g, w_ref[index]).astype(bf16)
        ordered_ref[to, :] = g
    if state:
        refs[2][...] = compact(tn(dy_ref[...], rising(*rising_refs)))


def out_back(core, halves, gs, w, index, state=()):
    n, size, model, channels = len(gs), gs[0].shape[0], gs[0].shape[1], w.shape[2]
    outs = [((n * size, channels), bf16), ((n * size, model), bf16)]
    if state:
        outs.append(((HEAD_DIM, channels), bf16))
    return kernel_call(
        functools.partial(out_back_kernel, halves, n, index, bool(state)),
        outs,
        (*gs, w, *state),
        scalars=(core,),
        us=2.0,
    )


def project_back_kernel(halves, n, kind, count, core_ref, dq_ref, *refs):
    others = refs[:count]
    w_ref, n_ref, gain_ref = refs[count : count + 3]
    outs = refs[count + 3 :]
    parts, cat_ref, gsum_ref = outs[:n], outs[n], outs[n + 1]
    rows, channels = dq_ref.shape
    cat_ref[:, 0:channels] = dq_ref[...]
    if kind == "halo":
        dk_ref, dv_ref, extra_ref = others
        cut = rows - extra_ref.shape[0]
        cat_ref[0:cut, channels : 2 * channels] = dk_ref[0:cut, :].astype(bf16)
        cat_ref[cut:rows, channels : 2 * channels] = (
            dk_ref[cut:rows, :] + extra_ref[...].astype(f32)
        ).astype(bf16)
        cat_ref[:, 2 * channels : 3 * channels] = dv_ref[...].astype(bf16)
    else:
        total = others[0][...].astype(f32)
        for other in others[1:]:
            total = total + other[...].astype(f32)
        cat_ref[:, channels : 3 * channels] = total.astype(bf16)
    size = parts[0].shape[0]
    gsum_ref[...] = jnp.zeros(gsum_ref.shape, f32)
    for i, to in enumerate(places(core_ref, halves, n, size)):
        part = sum(nt(cat_ref[to, j * channels : (j + 1) * channels], w_ref[j]) for j in range(3))
        parts[i][...] = part.astype(bf16)
        gsum_ref[...] += jnp.sum(part * n_ref[to, :].astype(f32), axis=0, keepdims=True)
    gsum_ref[...] = gsum_ref[...] / gain_ref[...]


def project_back(core, halves, n, kind, dq, others, w, normed, gain):
    rows, channels = dq.shape
    size, model = rows // n, normed.shape[1]
    out = kernel_call(
        functools.partial(project_back_kernel, halves, n, kind, len(others)),
        [((size, model), bf16)] * n + [((rows, 3 * channels), bf16), ((1, model), f32)],
        (dq, *others, w, normed, gain.reshape(1, -1)),
        scalars=(core,),
        us=3.0,
    )
    return out[:n], out[n], out[n + 1]


def at_rows(value, start, count):
    return lax.dynamic_slice_in_dim(value, start, count, 0)


def tie(*values):
    return lax.optimization_barrier(values)


class Rows:
    halves = 1
    chunks = 1
    grad_type = f32

    def __init__(self):
        self.blocks = lax.axis_size("ctx")
        self.place = lax.axis_index("ctx")
        self.core = self.place

    def enter(self, rows):
        return rows

    def leave_start(self, rows):
        return rows

    def leave_end(self, rows, there):
        return rows

    def spread(self, rows):
        return [rows]

    def half_sum(self, parts):
        return parts[0]

    def total(self, value):
        return [lax.psum(value, "tp")]

    def local(self, value):
        return value

    def assemble(self, share):
        return lax.all_gather(share, "fsdp", axis=1, tiled=True)

    def setup(self, ids, taps_n, channels):
        row = ids
        ids = ids[0]
        n, rows = self.blocks, ids.shape[0]
        halo = lax.ppermute(ids[rows - taps_n :].astype(bf16), "ctx", [(i, i + 1) for i in range(n - 1)])
        ext = jnp.concatenate([halo.astype(jnp.int32), ids])
        at = jnp.arange(ext.shape[0], dtype=jnp.int32)
        same = ext[:, None] == ext[None, :]
        age = jnp.sum((same & (at[None, :] < at[:, None])).astype(jnp.int32), axis=1)
        rem = jnp.sum((same & (at[None, :] > at[:, None])).astype(jnp.int32), axis=1)
        age, rem = [jnp.broadcast_to(v[:, None], (ext.shape[0], channels)) for v in (age, rem)]
        key_ids = lax.all_gather(ids.astype(bf16), "ctx", axis=0, tiled=True).astype(jnp.int32)
        count = rows // CHUNK
        high = self.place * count + jnp.arange(count, dtype=jnp.int32)
        firsts = ids[::CHUNK]
        low = jnp.sum((key_ids[None, :] < firsts[:, None]).astype(jnp.int32), axis=1) // CHUNK
        limits = jnp.stack([low, high, high])
        entry = ext[taps_n - 1].reshape(1, 1)
        return row, ids[:, None], entry, age, rem, (limits, ids[:, None], row, key_ids[:, None], key_ids[None])

    def from_previous(self, value):
        n = self.blocks
        return lax.ppermute(value, "ctx", [(i, i + 1) for i in range(n - 1)])

    def to_previous(self, value):
        n = self.blocks
        return lax.ppermute(value, "ctx", [(i + 1, i) for i in range(n - 1)])

    def state_before(self, factor, state):
        factors = lax.all_gather(factor.astype(bf16), "ctx").astype(f32)
        states = lax.all_gather(state, "ctx")

        def one(hop, held):
            return states[hop].astype(f32) + factors[hop] * held

        held = lax.fori_loop(0, self.place, one, jnp.zeros(state.shape, f32))
        return held.astype(bf16)

    def grad_after(self, factor, dstate):
        factors = lax.all_gather(factor.astype(bf16), "ctx").astype(f32)
        states = lax.all_gather(dstate, "ctx")

        def one(hop, held):
            at = self.blocks - 1 - hop
            return states[at].astype(f32) + factors[at] * held

        held = lax.fori_loop(0, self.blocks - 1 - self.place, one, jnp.zeros(dstate.shape, f32))
        return held.astype(bf16)

    def attend(self, setup, q, kv):
        limits, col, _, _, key_tiles = setup
        kv = lax.all_gather(kv, "ctx", axis=0, tiled=True)
        return attend(limits, q, kv, col, key_tiles), kv

    def attend_back(self, setup, kept, q, kv, grad, mixed, stats, wait):
        limits, _, tiles, key_col, _ = setup
        dq, dkv = attend_back(limits, q, kept, grad, mixed, stats, tiles, key_col, bf16, bf16)
        return dq, [lax.psum_scatter(dkv, "ctx", scatter_dimension=0, tiled=True)], wait

    def scatter(self, value):
        return [lax.psum_scatter(value, "fsdp", scatter_dimension=0, tiled=True)]

    def scattered(self, parts):
        return parts[0]

    def to_owner(self, value):
        return lax.psum(value, "ctx")

    def owned(self, value, got):
        return got

    def over_places(self, value):
        return lax.psum(value, ("ctx", "tp"))


class Pairs(Rows):
    halves = 2
    chunks = 1
    grad_type = bf16

    def __init__(self):
        self.blocks = 2
        self.core = lax.axis_index("ctx")
        self.chip = lax.axis_index("tp")
        self.place = self.chip // 2
        self.home = self.core == self.place

    def send(self, value, pairs):
        number = [(4 * c + t, 4 * d + u) for (c, t), (d, u) in pairs]
        return lax.ppermute(value, ("ctx", "tp"), number)

    def swap(self, value):
        return lax.ppermute(value, "ctx", [(0, 1), (1, 0)])

    def neighbour(self, value):
        return lax.ppermute(value, "tp", [(0, 1), (1, 0), (2, 3), (3, 2)])

    def across(self, value):
        return lax.ppermute(value, "tp", [(0, 2), (2, 0), (1, 3), (3, 1)])

    def from_home_core(self, value):
        return self.send(value, [((t // 2, t), (1 - t // 2, t)) for t in range(4)])

    def enter(self, rows):
        half = rows.shape[0] // 2
        got = self.from_home_core(at_rows(rows, (1 - self.core) * half, half))
        return jnp.where(self.home, at_rows(rows, self.core * half, half), got)

    def setup(self, ids, taps_n, channels):
        other = self.swap(ids)
        own = jnp.where(self.home, ids, other)
        first = jnp.where(self.core == 0, ids, other)
        before = jnp.where(self.place == 1, first, 0)
        col, before_col, entry, age, rem, own_limits, prev_limits = setup_ids(own, before, taps_n, channels)
        return own, col, entry, age, rem, (own_limits, prev_limits, col, before_col, own, before)

    def in_order(self, own, other):
        first = self.core == 0
        return jnp.concatenate([jnp.where(first, own, other), jnp.where(first, other, own)])

    def leave_start(self, rows):
        return self.across(rows)

    def leave_end(self, rows, there):
        got = self.swap(jnp.where(self.home, there, rows))
        return self.in_order(jnp.where(self.home, rows, there), got)

    def spread(self, rows):
        return [rows, self.swap(rows)]

    def half_sum(self, parts):
        return add(parts[0], self.swap(parts[1]))

    def total(self, value):
        return [value, self.neighbour(value)]

    def local(self, value):
        got = self.send(
            value, [((c, 2 * c + e), (c, 2 - 2 * c + e)) for c in range(2) for e in range(2)]
        )
        return jnp.where(self.home, value, got)

    def around(self, value):
        return [lax.ppermute(value, "fsdp", [(i, i ^ k) for i in range(4)]) for k in (1, 2, 3)]

    def assemble(self, share):
        place, size = lax.axis_index("fsdp"), share.shape[1]
        whole = jnp.zeros((share.shape[0], 4 * size, share.shape[2]), share.dtype)
        for k, part in enumerate([share] + self.around(share)):
            whole = lax.dynamic_update_slice_in_dim(whole, part, (place ^ k) * size, 1)
        return whole

    def from_previous(self, value):
        return self.send(value, [((c, t), (c, t + 2)) for c in range(2) for t in range(2)])

    def to_previous(self, value):
        return self.send(value, [((c, t + 2), (c, t)) for c in range(2) for t in range(2)])

    def state_before(self, factor, state):
        return self.from_previous(state)

    def grad_after(self, factor, dstate):
        return self.to_previous(dstate)

    def attend(self, setup, q, kv):
        own_limits, prev_limits, col, _, tiles, prev_tiles = setup
        before = self.from_previous(kv)
        held = attend(own_limits, q, kv, col, tiles, finish=False)
        return attend(prev_limits, q, before, col, prev_tiles, held), before

    def attend_back(self, setup, before, q, kv, grad, mixed, stats, wait):
        own_limits, prev_limits, col, prev_col, tiles, _ = setup
        dq, dkv_prev = attend_back(prev_limits, q, before, grad, mixed, stats, tiles, prev_col, f32, bf16)
        got = self.to_previous(dkv_prev)
        dq, *wait = tie(dq, *wait)
        dq, dkv = attend_back(own_limits, q, kv, grad, mixed, stats, tiles, col, bf16, f32, (dq,))
        return dq, [dkv, got], wait

    def scatter(self, value):
        place = lax.axis_index("fsdp")
        size = value.shape[0] // 4
        parts = [at_rows(value, place * size, size)]
        for k in (1, 2, 3):
            part = at_rows(value, (place ^ k) * size, size)
            parts.append(lax.ppermute(part, "fsdp", [(i, i ^ k) for i in range(4)]))
        return parts

    def scattered(self, parts):
        return sum(part.astype(f32) for part in parts).astype(bf16)

    def to_owner(self, value):
        return self.send(
            value, [((c, 2 - 2 * c + e), (c, 2 * c + e)) for c in range(2) for e in range(2)]
        )

    def owned(self, value, got):
        value = (value.astype(f32) + got.astype(f32)).astype(bf16)
        return jnp.where(self.home, value, self.from_home_core(value))

    def over_places(self, value):
        for step in (self.swap, self.neighbour, self.across):
            value = (value.astype(f32) + step(value).astype(f32)).astype(bf16)
        return value


def dot_tn(a, b):
    return jnp.einsum("tf,td->fd", a, b, preferred_element_type=f32).astype(bf16)


def feed_shares(reduced):
    width = reduced.shape[1] // 2
    return reduced[:, :width].astype(f32), reduced[:, width:].T.astype(f32)


def mixer_shares(reduced, channels):
    parts = [reduced[:, j * channels : (j + 1) * channels].astype(f32) for j in range(3)]
    return jnp.stack(parts), reduced[:, 3 * channels : 4 * channels].T.astype(f32)


def run(plan, inputs, cotangent, segments, gains, last_gain, in_weight, h3_out, attn_out, up_weight, down_weight, shift_taps, decay_rate):
    halves, chunks = plan.halves, plan.chunks
    pieces = halves * chunks
    slots = lax.axis_size("fsdp")
    hid = up_weight.shape[2]
    channels = h3_out.shape[0]
    taps_n = shift_taps.shape[0]
    share = h3_out.shape[1]
    core = plan.core.astype(jnp.int32).reshape(1)

    def split(value):
        size = value.shape[0] // chunks
        return [value[i * size : (i + 1) * size] for i in range(chunks)]

    def by_piece(spreads):
        return [s[i] for i in range(halves) for s in spreads]

    def by_chunk(parts):
        return [[parts[i * chunks + j] for i in range(halves)] for j in range(chunks)]

    def joined(spreads):
        return jnp.concatenate([piece for s in spreads for piece in s])

    def norms(xs, adds, gain):
        out = [norm(x, a, gain) for x, a in zip(xs, adds)]
        return [o[0] for o in out], [plan.spread(o[1]) for o in out]

    def norm_backs(xs, grads, adds, gain):
        out = [norm_back(x, g, a, gain) for x, g, a in zip(xs, grads, adds)]
        return [o[0] for o in out], [plan.spread(o[1]) for o in out]

    def totals(parts, *others):
        sums = [plan.half_sum(p) for p in parts]
        sums[-1], *others = tie(sums[-1], *others)
        adds = [plan.total(v) for v in sums]
        return (adds, *others) if others else adds

    def with_sums(adds, *others):
        adds[-1][-1], *others = tie(adds[-1][-1], *others)
        return others

    weights0 = plan.local(jnp.concatenate([in_weight[0], h3_out.T[None]]))
    xs = split(plan.enter(inputs[0]))
    seg_row, seg_col, entry, age, rem, setup = plan.setup(segments + 1, taps_n, channels)
    rows = seg_row.shape[1]
    small = jnp.concatenate([shift_taps, decay_rate.reshape(1, -1)])
    feed = [jnp.concatenate([up_weight[i], down_weight[i].T], axis=1) for i in range(2)]
    mix = jnp.concatenate([in_weight[1], attn_out.T[None]])
    x0, n0s = norms(xs, [[]] * chunks, gains[0])
    weights0, small, feed[0] = tie(weights0, small, feed[0])
    weights0 = plan.assemble(weights0)
    feed[0], mix = tie(plan.local(feed[0]), mix)
    small, mix = plan.local(small), plan.local(mix)
    weights0, age, rem = tie(weights0, age, rem)

    q0, k0, v0, n0 = project(core, halves, by_piece(n0s), weights0)
    k0, small = tie(k0, small)
    halo = plan.from_previous(k0[rows - taps_n :])
    halo, feed[0], feed[1] = tie(halo, feed[0], feed[1])
    feed0 = lax.all_gather(feed[0], "fsdp", axis=0, tiled=True)
    feed[1] = plan.local(feed[1])
    taps, rate_row = small[:taps_n], small[taps_n:]
    factor = jnp.exp(-rate_row * rows) * (entry == seg_row[:, rows - 1 :]).astype(f32)
    ks, state_end, y0, saved = h3_forward(k0, halo, q0, v0, taps, rate_row, age, seg_col, seg_row)
    state_in = plan.state_before(factor, state_end)
    state_in, mix = tie(state_in, mix)
    mix1 = lax.all_gather(mix, "fsdp", axis=1, tiled=True)
    *parts, y0 = project_out(core, halves, pieces, y0, weights0, 3, (q0, rate_row, seg_col, entry, state_in))
    adds = totals(by_chunk(parts))
    feed0, feed[1] = with_sums(adds, feed0, feed[1])
    feed1 = lax.all_gather(feed[1], "fsdp", axis=0, tiled=True)
    x1, m0s = norms(x0, adds, gains[1])
    out = [feed_forward(m, feed0, hid) for m in m0s]
    parts, r0, slope0 = [[o[i] for o in out] for i in range(3)]
    x2, n2s = norms(x1, totals(parts), gains[2])

    n2s[0][0], g_in = tie(n2s[0][0], cotangent[0])
    gs = split(plan.enter(g_in))
    flat = [p for g in gs for p in plan.spread(g)]
    mix1, *flat = tie(mix1, *flat)
    g_ins = [flat[halves * i : halves * (i + 1)] for i in range(chunks)]

    q2, _, _, n2, kv2 = project(core, halves, by_piece(n2s), mix1, True)
    (mixed, stats, mixed_bf), kept = plan.attend(setup, q2, kv2)
    parts = project_out(core, halves, pieces, mixed_bf, mix1, 3)
    x3, m1s = norms(x2, totals(by_chunk(parts)), last_gain)

    out = [feed_mid(m, g, feed1, hid, last_gain) for m, g in zip(m1s, g_ins)]
    parts, r1, du1, gain3 = [[o[i] for o in out] for i in range(4)]
    adds, r1, du1, m1s, g_ins = totals(parts, r1, du1, m1s, g_ins)
    size = r1[0].shape[0] // halves
    last = [
        [
            jnp.einsum(
                "tf,df->td", r[i * size : (i + 1) * size], feed1[:, hid:], preferred_element_type=f32
            ).astype(bf16)
            for i in range(halves)
        ]
        for r in r1
    ]
    feed1_grad = jnp.concatenate(
        [
            dot_tn(joined(m1s), jnp.concatenate(du1)),
            dot_tn(joined(g_ins), jnp.concatenate(r1)),
        ],
        axis=1,
    )
    feed1_grad, *flat = with_sums(adds, feed1_grad, *[p for s in last for p in s])
    feed1_parts = plan.scatter(feed1_grad)
    last = totals([flat[halves * i : halves * (i + 1)] for i in range(chunks)])
    grads, gbs = norm_backs(x3, gs, adds, last_gain)
    dmixed, grad_bf1 = out_back(core, halves, by_piece(gbs), mix1, 3)
    flat = [a for adds in last for a in adds]
    dq, dkv, flat = plan.attend_back(setup, kept, q2, kv2, dmixed, mixed, stats, flat)
    dkv[0], *feed1_parts = tie(dkv[0], *feed1_parts)
    feed1_grad = plan.scattered(feed1_parts)
    count = len(flat) // chunks
    x4 = []
    for i in range(chunks):
        x4.append(x3[i] + sum(a.astype(f32) for a in flat[count * i : count * (i + 1)]))
    x4 = jnp.concatenate(x4).astype(bf16)
    dkv[-1], feed1_grad, x4 = tie(dkv[-1], feed1_grad, x4)
    parts, cat1, gain2 = project_back(core, halves, pieces, "sum", dq, dkv, mix1, n2, gains[2])
    adds, cat1, n2 = totals(by_chunk(parts), cat1, n2)
    mix1_grad = jnp.concatenate([dot_tn(n2, cat1), dot_tn(grad_bf1, mixed_bf)], axis=1)
    mix1_grad, feed1_grad, x4 = with_sums(adds, mix1_grad, feed1_grad, x4)
    x4_there = plan.leave_start(x4)
    mix1_parts = plan.scatter(mix1_grad)
    grads, gbs = norm_backs(x2, grads, adds, gains[2])

    out = [feed_back(m, g, s, feed0, hid, gains[1]) for m, g, s in zip(m0s, gbs, slope0)]
    parts, du0, gain1 = [[o[i] for o in out] for i in range(3)]
    adds, m0s, du0, gbs, r0 = totals(parts, m0s, du0, gbs, r0)
    feed0_grad = jnp.concatenate(
        [
            dot_tn(joined(m0s), jnp.concatenate(du0)),
            dot_tn(joined(gbs), jnp.concatenate(r0)),
        ],
        axis=1,
    )
    feed0_grad, x4_there, *mix1_parts = with_sums(adds, feed0_grad, x4_there, *mix1_parts)
    feed0_parts = plan.scatter(feed0_grad)
    grads, gbs = norm_backs(x1, grads, adds, gains[1])
    mix1_grad = plan.scattered(mix1_parts)
    dy, grad_bf0, dstate = out_back(
        core, halves, by_piece(gbs), weights0, 3, (q0, rate_row, seg_col, entry)
    )
    dstate_end = plan.grad_after(factor, dstate)
    dstate_end, feed1_grad, mix1_grad = tie(dstate_end, feed1_grad, mix1_grad)
    feed1_got, mix1_got = plan.to_owner(feed1_grad), plan.to_owner(mix1_grad)
    output = plan.leave_end(x4, x4_there)
    dq, dk, dhalo, dv, dtaps, drate = h3_back_call(
        q0, ks, v0, dy, saved, dstate_end, rate_row, seg_col, seg_row, entry, k0, halo, taps, age, rem, state_in
    )
    halo_grad = plan.to_previous(dhalo)
    dq, feed1_got, mix1_got, output, *feed0_parts = tie(dq, feed1_got, mix1_got, output, *feed0_parts)
    feed0_grad = plan.scattered(feed0_parts)
    halo_grad, feed0_grad = tie(halo_grad, feed0_grad)
    feed0_got = plan.to_owner(feed0_grad)
    parts, cat0, gain0 = project_back(
        core, halves, pieces, "halo", dq, (dk, dv, halo_grad), weights0, n0, gains[0]
    )
    adds, cat0, n0, dtaps = totals(by_chunk(parts), cat0, n0, dtaps)

    mix0 = jnp.concatenate([dot_tn(n0, cat0), dot_tn(grad_bf0, y0)], axis=1)
    mix0 = mix0.reshape(slots, share, 4 * channels)
    taps_each = taps_n // slots
    small = jnp.concatenate(
        [
            dtaps.reshape(slots, taps_each, channels),
            jnp.pad(
                drate.reshape(-1, slots, HEAD_DIM // slots).transpose(1, 0, 2).reshape(slots, 1, -1),
                ((0, 0), (0, 0), (0, channels - channels // slots)),
            ),
            jnp.concatenate([gain0, sum(gain1), gain2, sum(gain3)]).reshape(4, slots, share).transpose(1, 0, 2),
        ],
        axis=1,
    ).astype(bf16)
    small = jnp.pad(small, ((0, 0), (0, (-small.shape[1]) % 32), (0, 3 * channels)))
    height = share + small.shape[1]
    mix0_parts = plan.scatter(jnp.concatenate([mix0, small], axis=1).reshape(slots * height, 4 * channels))
    grads = [
        norm_back(x, g, a, gains[0])[0].astype(plan.grad_type) for x, g, a in zip(x0, grads, adds)
    ]
    mix0 = plan.scattered(mix0_parts)
    mix0_got = plan.to_owner(mix0)
    grads[-1], feed1_got, mix1_got, feed0_got, gain_rows = tie(
        grads[-1], feed1_got, mix1_got, feed0_got, mix0[share + taps_each + 1 : share + taps_each + 5, :channels]
    )
    there = [plan.leave_start(g) for g in grads]
    gain_rows = plan.over_places(gain_rows).astype(f32)
    feed1 = plan.owned(feed1_grad, feed1_got)
    mix1 = plan.owned(mix1_grad, mix1_got)
    feed0 = plan.owned(feed0_grad, feed0_got)
    mix0 = plan.owned(mix0, mix0_got)
    input_grad = plan.leave_end(jnp.concatenate(grads), jnp.concatenate(there)).astype(f32)
    small = mix0[share:, :channels]
    in0_grad, out0_grad = mixer_shares(mix0[:share], channels)
    dtaps = small[:taps_each].astype(f32)
    drate = small[taps_each, : channels // slots].astype(f32).reshape(-1, HEAD_DIM // slots)
    up0_grad, down0_grad = feed_shares(feed0)
    up1_grad, down1_grad = feed_shares(feed1)
    in1_grad, out1_grad = mixer_shares(mix1, channels)
    return (
        output[None],
        input_grad[None],
        gain_rows[:3],
        gain_rows[3],
        jnp.stack([in0_grad, in1_grad]),
        out0_grad,
        out1_grad,
        jnp.stack([up0_grad, up1_grad]),
        jnp.stack([down0_grad, down1_grad]),
        dtaps,
        drate,
    )


def shards(*arguments):
    paired = lax.axis_size("ctx") == 2 and lax.axis_size("tp") == 4 and lax.axis_size("fsdp") == 4
    return run(Pairs() if paired else Rows(), *arguments)


def solution(mesh):
    placed = (
        P("fsdp", "ctx", None),
        P("fsdp", "ctx", None),
        P("fsdp", "ctx"),
        P(),
        P(),
        P(None, None, "fsdp", "tp"),
        P("tp", "fsdp"),
        P("tp", "fsdp"),
        P(None, "fsdp", "tp"),
        P(None, "tp", "fsdp"),
        P(None, "tp"),
        P("tp", None),
    )
    return jax.shard_map(
        shards,
        mesh=mesh,
        in_specs=placed,
        out_specs=(
            P("fsdp", "ctx", None),
            P("fsdp", "ctx", None),
            P(None, "fsdp"),
            P("fsdp"),
            P(None, None, "fsdp", "tp"),
            P("tp", "fsdp"),
            P("tp", "fsdp"),
            P(None, "fsdp", "tp"),
            P(None, "tp", "fsdp"),
            P("fsdp", "tp"),
            P("tp", "fsdp"),
        ),
        check_vma=False,
    )
```

```python
import functools

import jax
import jax.numpy as jnp
from jax import lax
from jax.experimental import pallas as pl
from jax.experimental.pallas import tpu as pltpu
from jax.sharding import PartitionSpec as P

HEAD_DIM = 64
epsilon = 1e-05
masked_low = -1e30
bf16 = jnp.bfloat16
f32 = jnp.float32
scale = HEAD_DIM ** (-0.5)
CHUNK = 256


def nn(a, b):
    return lax.dot_general(a, b, (((1,), (0,)), ((), ())), preferred_element_type=f32)


def nt(a, b):
    return lax.dot_general(a, b, (((1,), (1,)), ((), ())), preferred_element_type=f32)


def tn(a, b):
    return lax.dot_general(a, b, (((0,), (0,)), ((), ())), preferred_element_type=f32)


def head_masks(rows, channels):
    lane = lax.broadcasted_iota(jnp.int32, (rows, channels), 1)
    return [(lane >= HEAD_DIM * h) & (lane < HEAD_DIM * (h + 1)) for h in range(channels // HEAD_DIM)]


def same_head(channels):
    row = lax.broadcasted_iota(jnp.int32, (channels, channels), 0) // HEAD_DIM
    lane = lax.broadcasted_iota(jnp.int32, (channels, channels), 1) // HEAD_DIM
    return row == lane


def compact(state):
    channels = state.shape[1]
    state = jnp.where(same_head(channels), state, 0.0)
    parts = [state[HEAD_DIM * h : HEAD_DIM * (h + 1), :] for h in range(channels // HEAD_DIM)]
    return sum(parts[1:], parts[0]).astype(bf16)


def expand(small):
    channels = small.shape[1]
    tall = jnp.concatenate([small.astype(f32)] * (channels // HEAD_DIM), axis=0)
    return jnp.where(same_head(channels), tall, 0.0)


def params(mib):
    return pltpu.CompilerParams(vmem_limit_bytes=mib * 1024 * 1024)


def kernel_call(kernel, outs, arrays, scalars=(), scratch=(), mib=12, us=2.0):
    vm = pl.BlockSpec(memory_space=pltpu.VMEM)
    sm = pl.BlockSpec(memory_space=pltpu.SMEM)
    return pl.pallas_call(
        kernel,
        out_shape=[jax.ShapeDtypeStruct(s, d) for s, d in outs],
        in_specs=[sm] * len(scalars) + [vm] * len(arrays),
        out_specs=[vm] * len(outs),
        scratch_shapes=list(scratch),
        compiler_params=params(mib),
        cost_estimate=pl.CostEstimate(flops=int(us * 1e9), bytes_accessed=1000, transcendentals=0),
    )(*scalars, *arrays)


def column_of(row):
    return jnp.broadcast_to(row.astype(f32), (8, row.shape[1])).T[:, 0:1].astype(jnp.int32)


def setup_kernel(taps_n, ids_ref, before_ref, col_ref, before_col_ref, entry_ref, age_ref, rem_ref, own_ref, prev_ref):
    rows = ids_ref.shape[1]
    channels = age_ref.shape[1]
    count = rows // CHUNK
    own, before = ids_ref[...], before_ref[...]
    col_ref[...] = column_of(own)
    before_col_ref[...] = column_of(before)
    entry_ref[...] = before_col_ref[rows - 1 : rows, :]
    lane = lax.broadcasted_iota(jnp.int32, (64, rows), 1)
    row = lax.broadcasted_iota(jnp.int32, (64, rows), 0)
    halo_lane = lane >= rows - taps_n

    def fill(ids, at, start):
        in_own = ids == own
        in_halo = (ids == before) & halo_lane
        both = (in_own & (lane < row + start)).astype(f32) + (in_halo & (lane - rows < row + start)).astype(f32)
        after = (in_own & (lane > row + start)).astype(f32) + (in_halo & (lane - rows > row + start)).astype(f32)
        age = jnp.sum(both, axis=1, keepdims=True).astype(jnp.int32)
        rem = jnp.sum(after, axis=1, keepdims=True).astype(jnp.int32)
        age_ref[at, :] = jnp.broadcast_to(age, (64, channels))
        rem_ref[at, :] = jnp.broadcast_to(rem, (64, channels))

    fill(before_col_ref[rows - 64 : rows, :], pl.ds(0, 64), -64)

    def block(b, carry):
        start = pl.multiple_of(b * 64, 64)
        fill(col_ref[pl.ds(start, 64), :], pl.ds(start + 64, 64), start)
        return carry

    lax.fori_loop(0, rows // 64, block, 0)
    for b in range(count):
        first = own[:, b * CHUNK : b * CHUNK + 1]
        low = jnp.sum((before < first).astype(f32)) + jnp.sum((own < first).astype(f32))
        low = low.astype(jnp.int32) // CHUNK
        own_ref[0, b] = jnp.maximum(low - count, 0)
        own_ref[1, b] = b
        own_ref[2, b] = b
        prev_ref[0, b] = low
        prev_ref[1, b] = count - 1
        prev_ref[2, b] = count + b


def setup_ids(ids, before, taps_n, channels):
    rows = ids.shape[1]
    count = rows // CHUNK
    vm, sm = pl.BlockSpec(memory_space=pltpu.VMEM), pl.BlockSpec(memory_space=pltpu.SMEM)
    shapes = [(rows, 1), (rows, 1), (1, 1), (rows + taps_n, channels), (rows + taps_n, channels), (3, count), (3, count)]
    return pl.pallas_call(
        functools.partial(setup_kernel, taps_n),
        out_shape=[jax.ShapeDtypeStruct(s, jnp.int32) for s in shapes],
        in_specs=[vm] * 2,
        out_specs=[vm] * 5 + [sm] * 2,
        compiler_params=params(8),
        cost_estimate=pl.CostEstimate(flops=int(2e9), bytes_accessed=1000, transcendentals=0),
    )(ids, before)


def tail_and_rise(rate, rows):
    pos = lax.broadcasted_iota(jnp.int32, (rows, rate.shape[1]), 0).astype(f32)
    return jnp.exp(-rate * (rows - 1.0 - pos)), jnp.exp(-rate * (pos + 1.0))


def rising(q_ref, rate_ref, segc_ref, entry_ref):
    rows = q_ref.shape[0]
    rise = tail_and_rise(rate_ref[...], rows)[1]
    rise = rise * ((segc_ref[...] == entry_ref[...]).astype(f32) * scale)
    return (q_ref[...].astype(f32) * rise).astype(bf16)


def rolled_down(ext_ref, age_ref, copies, rows):
    for r in range(8):
        copies[r, 8:rows, :] = jnp.where(age_ref[8:rows, :] >= r, ext_ref[8 - r : rows - r, :], 0.0)


def lane_tiles(channels):
    return [(low, min(low + 128, channels)) for low in range(0, channels, 128)]


def filtered(copies, taps_ref, reach_ref, reach_at, first, step, groups, size, low, high):
    reach = reach_ref[reach_at, low:high]
    base = first if step > 0 else first + step * (groups - 1)
    parts = [None] * groups
    for r in range(8):
        window = copies[r, pl.ds(base, size + 8 * (groups - 1)), low:high]
        for m in range(groups):
            at = 8 * m if step > 0 else 8 * (groups - 1 - m)
            term = window[at : at + size] * taps_ref[8 * m + r : 8 * m + r + 1, low:high]
            parts[m] = term if parts[m] is None else parts[m] + term
    total = parts[0]
    for m in range(1, groups):
        total = total + jnp.where(reach >= 8 * m, parts[m], 0.0)
    return total


def decay_factors(rate_row, rows):
    pos = lax.broadcasted_iota(jnp.int32, (rows, rate_row.shape[1]), 0).astype(f32)
    mid = 0.5 * rows
    q_fac = jnp.exp(-rate_row * (pos - mid))
    k_fac = jnp.exp(rate_row * (pos - mid))
    rise = jnp.exp(-rate_row * (pos + 1.0))
    tail = jnp.exp(-rate_row * (rows - 1.0 - pos))
    whole = jnp.exp(-rate_row * rows)
    return pos, mid, q_fac, k_fac, rise, tail, whole


def h3_kernel(
    taps_n,
    key_ref,
    halo_ref,
    q_ref,
    v_ref,
    taps_ref,
    rate_ref,
    age_ref,
    segc_ref,
    segr_ref,
    ks_ref,
    st_ref,
    y_ref,
    save_ref,
    ext,
    copies,
):
    rows, channels = key_ref.shape
    ext[0:taps_n, :] = halo_ref[...].astype(f32)
    ext[taps_n : taps_n + rows, :] = key_ref[...].astype(f32)
    rolled_down(ext, age_ref, copies, rows + taps_n)

    def block(b, carry):
        start = pl.multiple_of(b * 64, 64)
        for low, high in lane_tiles(channels):
            ks_ref[pl.ds(start, 64), low:high] = filtered(
                copies, taps_ref, age_ref, pl.ds(start + taps_n, 64), start + taps_n, -8, taps_n // 8, 64, low, high
            )
        return carry

    lax.fori_loop(0, rows // 64, block, 0)

    blocks = rows // CHUNK
    _, _, q_fac, k_fac, rise, tail, whole = decay_factors(rate_ref[...], CHUNK)
    heads = head_masks(CHUNK, channels)
    block_diag = same_head(channels)
    causal = lax.broadcasted_iota(jnp.int32, (CHUNK, CHUNK), 0) >= lax.broadcasted_iota(
        jnp.int32, (CHUNK, CHUNK), 1
    )
    state = jnp.zeros((channels, channels), f32)
    for b in range(blocks):
        sl = slice(b * CHUNK, (b + 1) * CHUNK)
        seg_c = segc_ref[sl, :]
        seg_r = segr_ref[:, sl]
        last = segc_ref[(b + 1) * CHUNK - 1 : (b + 1) * CHUNK, :]
        final = (seg_c == last).astype(f32)
        q = q_ref[sl, :].astype(f32) * scale
        k = ks_ref[sl, :]
        v = v_ref[sl, :]
        qf = (q * q_fac).astype(bf16)
        kf = (k * k_fac).astype(bf16)
        kt = (k * (tail * final)).astype(bf16)
        allowed = causal & (seg_c == seg_r)
        save_ref[b, :, :] = state
        y = jnp.zeros((CHUNK, channels), f32)
        if b > 0:
            before = segc_ref[b * CHUNK - 1 : b * CHUNK, :]
            qr = (q * (rise * (seg_c == before).astype(f32))).astype(bf16)
            y = nt(qr, state.astype(bf16))
            state = state * (whole * (last == before).astype(f32))
        for hm in heads:
            scores = nt(jnp.where(hm, qf, jnp.zeros_like(qf)), kf)
            scores = jnp.where(allowed, scores, 0.0).astype(bf16)
            y = y + jnp.where(hm, nn(scores, v), 0.0)
        y_ref[sl, :] = y
        state = state + jnp.where(block_diag, tn(v, kt), 0.0)
    st_ref[...] = compact(state)


def h3_forward(key, halo, q, v, taps, rate_row, age, seg_col, seg_row):
    rows, channels = q.shape
    taps_n = taps.shape[0]
    return kernel_call(
        functools.partial(h3_kernel, taps_n),
        [
            ((rows, channels), f32),
            ((HEAD_DIM, channels), bf16),
            ((rows, channels), f32),
            ((rows // CHUNK, channels, channels), f32),
        ],
        (key, halo, q, v, taps, rate_row, age, seg_col, seg_row),
        scratch=[pltpu.VMEM((rows + taps_n, channels), f32), pltpu.VMEM((8, rows + taps_n, channels), f32)],
        mib=20,
        us=10.0,
    )


def h3_back_kernel(
    taps_n,
    q_ref,
    ks_ref,
    v_ref,
    dy_ref,
    save_ref,
    dst_ref,
    rate_ref,
    segc_ref,
    segr_ref,
    entry_ref,
    key_ref,
    halo_ref,
    taps_ref,
    age_ref,
    rem_ref,
    sin_ref,
    dq_ref,
    dk_ref,
    dhalo_ref,
    dv_ref,
    dtaps_ref,
    drate_ref,
    ext,
    copies,
    dext,
    dcopies,
    tap_acc,
):
    rows, channels = q_ref.shape
    blocks = rows // CHUNK
    pos, mid, q_fac, k_fac, rise, tail, whole = decay_factors(rate_ref[...], CHUNK)
    heads = head_masks(CHUNK, channels)
    block_diag = same_head(channels)
    row = lax.broadcasted_iota(jnp.int32, (CHUNK, CHUNK), 0)
    lane = lax.broadcasted_iota(jnp.int32, (CHUNK, CHUNK), 1)
    dstate = expand(dst_ref[...])
    drate = jnp.zeros((1, channels), f32)
    dext[0:taps_n, :] = jnp.zeros((taps_n, channels), f32)
    dext[rows + taps_n : rows + 2 * taps_n, :] = jnp.zeros((taps_n, channels), f32)
    whole_keeps = []
    for b in range(blocks):
        before = entry_ref[...] if b == 0 else segc_ref[b * CHUNK - 1 : b * CHUNK, :]
        last = segc_ref[(b + 1) * CHUNK - 1 : (b + 1) * CHUNK, :]
        whole_keeps.append(whole * (last == before).astype(f32))
    state_in = expand(sin_ref[...])
    prefix = [jnp.ones_like(whole)]
    for b in range(blocks - 1):
        prefix.append(prefix[-1] * whole_keeps[b])
    for b in reversed(range(blocks)):
        sl = slice(b * CHUNK, (b + 1) * CHUNK)
        seg_c = segc_ref[sl, :]
        seg_r = segr_ref[:, sl]
        before = entry_ref[...] if b == 0 else segc_ref[b * CHUNK - 1 : b * CHUNK, :]
        last = segc_ref[(b + 1) * CHUNK - 1 : (b + 1) * CHUNK, :]
        carried = (seg_c == before).astype(f32)
        final = (seg_c == last).astype(f32)
        q = q_ref[sl, :].astype(f32) * scale
        k = ks_ref[sl, :]
        v = v_ref[sl, :]
        dy = dy_ref[sl, :]
        qf = (q * q_fac).astype(bf16)
        kf = (k * k_fac).astype(bf16)
        rise_c = rise * carried
        tail_c = tail * final
        qr = (q * rise_c).astype(bf16)
        kt = (k * tail_c).astype(bf16)
        same = seg_c == seg_r
        low_mask = (row >= lane) & same
        up_mask = (row <= lane) & same
        state = save_ref[b, :, :] + state_in * prefix[b]
        dstate_b = dstate.astype(bf16)
        dqf = jnp.zeros((CHUNK, channels), f32)
        dkf = jnp.zeros((CHUNK, channels), f32)
        dv = nt(kt, dstate_b)
        zero = jnp.zeros_like(qf)
        for hm in heads:
            kh = jnp.where(hm, kf, zero)
            vh = jnp.where(hm, v, zero)
            scores_t = jnp.where(up_mask, nt(kh, qf), 0.0).astype(bf16)
            dv = dv + jnp.where(hm, nn(scores_t, dy), 0.0)
            dsc = jnp.where(low_mask, nt(dy, vh), 0.0).astype(bf16)
            dsc_t = jnp.where(up_mask, nt(vh, dy), 0.0).astype(bf16)
            dqf = dqf + nn(dsc, kh)
            dkf = dkf + jnp.where(hm, nn(dsc_t, qf), 0.0)
        dqr = nn(dy, state.astype(bf16))
        dkt = nn(v, dstate_b)
        dq_ref[sl, :] = ((dqf * q_fac + dqr * rise_c) * scale).astype(bf16)
        dv_ref[sl, :] = dv.astype(bf16)
        dext[taps_n + b * CHUNK : taps_n + (b + 1) * CHUNK, :] = dkf * k_fac + dkt * tail_c
        part = (pos - mid) * (qf.astype(f32) * dqf - kf.astype(f32) * dkf)
        part = part + (pos + 1.0) * (qr.astype(f32) * dqr)
        part = part + (CHUNK - 1.0 - pos) * (kt.astype(f32) * dkt)
        drate = drate + jnp.sum(part, axis=0, keepdims=True)
        held = dstate * whole_keeps[b]
        drate = drate + CHUNK * jnp.sum(state * held, axis=0, keepdims=True)
        dstate = held + jnp.where(block_diag, tn(dy, qr), 0.0)
    drate_ref[...] = -drate

    total = rows + taps_n
    ext[0:taps_n, :] = halo_ref[...].astype(f32)
    ext[taps_n:total, :] = key_ref[...].astype(f32)
    rolled_down(ext, age_ref, copies, total)
    for r in range(8):
        dcopies[r, 0:total, :] = jnp.where(rem_ref[...] >= r, dext[r : total + r, :], 0.0)
        dcopies[r, total : total + taps_n, :] = jnp.zeros((taps_n, channels), f32)
    tap_acc[...] = jnp.zeros(tap_acc.shape, f32)

    def gathered(start, low, high):
        return filtered(
            dcopies, taps_ref, rem_ref, pl.ds(start, 64), start, 8, taps_n // 8, 64, low, high
        )

    def block(b, carry):
        start = pl.multiple_of(b * 64, 64)
        for low, high in lane_tiles(channels):
            dk_ref[pl.ds(start, 64), low:high] = gathered(start + taps_n, low, high)
        return carry

    lax.fori_loop(0, rows // 64, block, 0)
    for low, high in lane_tiles(channels):
        dhalo_ref[:, low:high] = gathered(0, low, high).astype(bf16)

    def tap_block(b, carry):
        start = pl.multiple_of(b * 64, 64)
        age = age_ref[pl.ds(start + taps_n, 64), :]
        grad = dext[pl.ds(start + taps_n, 64), :]
        for m in range(taps_n // 8):
            held = jnp.where(age >= 8 * m, grad, 0.0)
            for r in range(8):
                term = copies[r, pl.ds(start + taps_n - 8 * m, 64), :] * held
                tap_acc[8 * m + r, :, :] += jnp.sum(term.reshape(8, 8, channels), axis=0)
        return carry

    lax.fori_loop(0, rows // 64, tap_block, 0)
    dtaps_ref[...] = jnp.sum(tap_acc[...], axis=1)


def h3_back_call(q, ks, v, dy, save, dstate, rate_row, seg_col, seg_row, entry, key, halo, taps, age, rem, state_in):
    rows, channels = q.shape
    taps_n = taps.shape[0]
    total = rows + taps_n
    return kernel_call(
        functools.partial(h3_back_kernel, taps_n),
        [
            ((rows, channels), bf16),
            ((rows, channels), f32),
            ((taps_n, channels), bf16),
            ((rows, channels), bf16),
            ((taps_n, channels), f32),
            ((1, channels), f32),
        ],
        (q, ks, v, dy, save, dstate, rate_row, seg_col, seg_row, entry, key, halo, taps, age, rem, state_in),
        scratch=[
            pltpu.VMEM((total, channels), f32),
            pltpu.VMEM((8, total, channels), f32),
            pltpu.VMEM((total + taps_n, channels), f32),
            pltpu.VMEM((8, total + taps_n, channels), f32),
            pltpu.VMEM((taps_n, 8, channels), f32),
        ],
        mib=26,
        us=18.0,
    )


def attend_kernel(resume, finish, lim_ref, q_ref, kv_ref, segc_ref, segr_ref, *refs):
    if resume:
        acc_in, col_in = refs[:2]
        refs = refs[2:]
    rows, channels = q_ref.shape
    n_heads = channels // HEAD_DIM
    heads = head_masks(CHUNK, channels)
    row = lax.broadcasted_iota(jnp.int32, (CHUNK, CHUNK), 0)
    lane = lax.broadcasted_iota(jnp.int32, (CHUNK, CHUNK), 1)
    stat_lane = lax.broadcasted_iota(jnp.int32, (CHUNK, 128), 1)
    for b in range(rows // CHUNK):
        sl = slice(b * CHUNK, (b + 1) * CHUNK)
        low, high, diagonal = lim_ref[0, b], lim_ref[1, b], lim_ref[2, b]
        q = q_ref[sl, :]
        seg_c = segc_ref[sl, :]
        qh = [jnp.where(hm, q, jnp.zeros_like(q)) for hm in heads]

        def step(t, carry):
            at = pl.multiple_of(t * CHUNK, CHUNK)
            keys = kv_ref[pl.ds(at, CHUNK), 0:channels]
            values = kv_ref[pl.ds(at, CHUNK), channels : 2 * channels]
            seg_r = segr_ref[:, pl.ds(at, CHUNK)]
            allowed = (row >= lane + (t - diagonal) * CHUNK) & (seg_c == seg_r)
            new = []
            for h in range(n_heads):
                top, total, acc = carry[h]
                z = jnp.where(allowed, nt(qh[h], keys) * scale, masked_low)
                new_top = jnp.maximum(top, jnp.max(z, axis=1, keepdims=True))
                shrink = jnp.exp(top - new_top)
                e = jnp.where(allowed, jnp.exp(z - new_top), 0.0)
                total = total * shrink + jnp.sum(e, axis=1, keepdims=True)
                acc = acc * shrink + nn(e.astype(bf16), values)
                new.append((new_top, total, acc))
            return tuple(new)

        if resume:
            col = col_in[sl, :]
            held = acc_in[sl, :]
            start = tuple((col[:, h : h + 1], col[:, 8 + h : 9 + h], held) for h in range(n_heads))
        else:
            start = tuple(
                (
                    jnp.full((CHUNK, 1), masked_low, f32),
                    jnp.zeros((CHUNK, 1), f32),
                    jnp.zeros((CHUNK, channels), f32),
                )
                for _ in range(n_heads)
            )
        state = lax.fori_loop(low, high + 1, step, start)
        out = jnp.zeros((CHUNK, channels), f32)
        stats = jnp.zeros((CHUNK, 128), f32)
        for h in range(n_heads):
            top, total, acc = state[h]
            out = jnp.where(heads[h], acc / total if finish else acc, out)
            stats = jnp.where(stat_lane == h, top, stats)
            stats = jnp.where(stat_lane == 8 + h, total, stats)
        refs[0][sl, :] = out
        if finish:
            refs[1][b, :, :] = stats.T[0:16, :]
            refs[2][sl, :] = out.astype(bf16)
        else:
            refs[1][sl, :] = stats


def attend(lim, q, kv, seg_col, seg_tiles, held=(), finish=True):
    rows, channels = q.shape
    if finish:
        outs = [((rows, channels), f32), ((rows // CHUNK, 16, CHUNK), f32), ((rows, channels), bf16)]
    else:
        outs = [((rows, channels), f32), ((rows, 128), f32)]
    return kernel_call(
        functools.partial(attend_kernel, bool(held), finish),
        outs,
        (q, kv, seg_col, seg_tiles, *held),
        scalars=(lim,),
        mib=16 + kv.shape[0] // 512,
        us=5.0,
    )


def attend_back_kernel(
    resume, lim_ref, q_ref, kv_ref, do_ref, o_ref, stat_ref, qseg_ref, kseg_ref, *refs
):
    dq_ref, dkv_ref, acc = refs[-3:]
    rows, channels = q_ref.shape
    n_heads = channels // HEAD_DIM
    heads = head_masks(CHUNK, channels)
    row = lax.broadcasted_iota(jnp.int32, (CHUNK, CHUNK), 0)
    lane = lax.broadcasted_iota(jnp.int32, (CHUNK, CHUNK), 1)
    stat_lane = lax.broadcasted_iota(jnp.int32, (CHUNK, 128), 1)
    acc[...] = jnp.zeros(acc.shape, f32)
    for b in range(rows // CHUNK):
        sl = slice(b * CHUNK, (b + 1) * CHUNK)
        low, high, diagonal = lim_ref[0, b], lim_ref[1, b], lim_ref[2, b]
        q = q_ref[sl, :]
        do = do_ref[sl, :].astype(f32)
        o = o_ref[sl, :]
        seg_q = qseg_ref[:, sl]
        zero = jnp.zeros_like(q)
        qh = [jnp.where(hm, q, zero) for hm in heads]
        cols = jnp.zeros((CHUNK, 128), f32)
        for h in range(n_heads):
            inner = jnp.sum(jnp.where(heads[h], do * o, 0.0), axis=1, keepdims=True)
            cols = jnp.where(stat_lane == h, inner, cols)
        inner_rows = cols.T
        totals = stat_ref[b, 8:16, :]
        inv_cols = jnp.concatenate([1.0 / jnp.maximum(totals, 1e-30), jnp.zeros((120, CHUNK), f32)]).T
        wh = []
        for h in range(n_heads):
            inv = inv_cols[:, h : h + 1]
            wh.append(jnp.where(heads[h], do * inv, 0.0).astype(bf16))

        def step(t, dq):
            at = pl.multiple_of(t * CHUNK, CHUNK)
            keys = kv_ref[pl.ds(at, CHUNK), 0:channels]
            values = kv_ref[pl.ds(at, CHUNK), channels : 2 * channels]
            seg_k = kseg_ref[pl.ds(at, CHUNK), :]
            allowed = (lane >= row + (t - diagonal) * CHUNK) & (seg_k == seg_q)
            dk = jnp.zeros((CHUNK, channels), f32)
            dv = jnp.zeros((CHUNK, channels), f32)
            for h in range(n_heads):
                top = stat_ref[b, h : h + 1, :]
                total = stat_ref[b, 8 + h : 9 + h, :]
                z = jnp.where(allowed, nt(keys, qh[h]) * scale, masked_low)
                e = jnp.where(allowed, jnp.exp(z - top), 0.0)
                dp = nt(values, wh[h])
                dz = (e * (dp - inner_rows[h : h + 1, :] / total)).astype(bf16)
                dk = dk + nn(dz, qh[h])
                dv = dv + nn(e.astype(bf16), wh[h])
                dq = dq + jnp.where(heads[h], tn(dz, keys), 0.0)
            acc[0, pl.ds(at, CHUNK), :] += dk
            acc[1, pl.ds(at, CHUNK), :] += dv
            return dq

        dq = lax.fori_loop(low, high + 1, step, jnp.zeros((CHUNK, channels), f32))
        dq = dq * scale
        if resume:
            dq = dq + refs[0][sl, :]
        dq_ref[sl, :] = dq.astype(dq_ref.dtype)
    dkv_ref[:, 0:channels] = (acc[0] * scale).astype(dkv_ref.dtype)
    dkv_ref[:, channels : 2 * channels] = acc[1].astype(dkv_ref.dtype)


def attend_back(lim, q, kv, do, o, stats, q_tiles, key_col, dq_type, dkv_type, held=()):
    rows, channels = q.shape
    return kernel_call(
        functools.partial(attend_back_kernel, bool(held)),
        [((rows, channels), dq_type), ((kv.shape[0], 2 * channels), dkv_type)],
        (q, kv, do, o, stats, q_tiles, key_col, *held),
        scalars=(lim,),
        scratch=[pltpu.VMEM((2, kv.shape[0], channels), f32)],
        mib=18 + kv.shape[0] // 256,
        us=7.0,
    )


def by_rows(rows, step, body):
    def one(i, carry):
        body(pl.ds(pl.multiple_of(i * step, step), step))
        return carry

    lax.fori_loop(0, rows // step, one, 0)


def norm_kernel(n_add, x_ref, *refs):
    adds, gain_ref, outs = refs[:n_add], refs[n_add], refs[n_add + 1 :]

    def body(at):
        x = x_ref[at, :].astype(f32)
        for a in adds:
            x = x + a[at, :].astype(f32)
        center = jnp.mean(x, axis=1, keepdims=True)
        moved = x - center
        inv = lax.rsqrt(jnp.mean(moved * moved, axis=1, keepdims=True) + epsilon)
        outs[0][at, :] = x
        outs[1][at, :] = (moved * inv * gain_ref[...]).astype(bf16)

    by_rows(x_ref.shape[0], 128, body)


def norm(x, adds, gain):
    shape = x.shape
    return kernel_call(
        functools.partial(norm_kernel, len(adds)),
        [(shape, f32), (shape, bf16)],
        (x, *adds, gain.reshape(1, -1)),
        us=2.0,
    )


def norm_back_kernel(n_add, x_ref, grad_ref, *refs):
    adds, gain_ref, outs = refs[:n_add], refs[n_add], refs[n_add + 1 :]

    def body(at):
        x = x_ref[at, :]
        center = jnp.mean(x, axis=1, keepdims=True)
        moved = x - center
        inv = lax.rsqrt(jnp.mean(moved * moved, axis=1, keepdims=True) + epsilon)
        unit = moved * inv
        d = adds[0][at, :].astype(f32)
        for a in adds[1:]:
            d = d + a[at, :].astype(f32)
        d = d * gain_ref[...]
        mean_d = jnp.mean(d, axis=1, keepdims=True)
        mean_du = jnp.mean(d * unit, axis=1, keepdims=True)
        grad = grad_ref[at, :].astype(f32) + inv * (d - mean_d - unit * mean_du)
        outs[0][at, :] = grad
        outs[1][at, :] = grad.astype(bf16)

    by_rows(x_ref.shape[0], 128, body)


def norm_back(x, grad, adds, gain):
    shape = x.shape
    return kernel_call(
        functools.partial(norm_back_kernel, len(adds)),
        [(shape, f32), (shape, bf16)],
        (x, grad, *adds, gain.reshape(1, -1)),
        us=2.0,
    )


def gelu_both(u):
    inner = 0.7978845608028654 * (u + 0.044715 * (u * u * u))
    t = jnp.tanh(inner)
    half = 0.5 * (1.0 + t)
    slope = half + 0.5 * u * (1.0 - t * t) * (0.7978845608028654 * (1.0 + 0.134145 * (u * u)))
    return u * half, slope


def gather_rows(refs, to):
    size = refs[0].shape[0]
    for i, ref in enumerate(refs):
        to[i * size : (i + 1) * size, :] = ref[...]


def feed_forward_kernel(n, hid, *refs):
    ms, w_ref = refs[:n], refs[n]
    parts, r_ref, slope_ref, rows, up = refs[n + 1 : 2 * n + 1], *refs[2 * n + 1 :]
    size = ms[0].shape[0]
    gather_rows(ms, rows)
    up[...] = nn(rows[...], w_ref[:, 0:hid])

    def body(at):
        r, slope = gelu_both(up[at, :])
        r_ref[at, :] = r.astype(bf16)
        slope_ref[at, :] = slope.astype(bf16)

    by_rows(n * size, 32, body)
    up[...] = nt(r_ref[...], w_ref[:, hid : 2 * hid])
    for i in range(n):
        parts[i][...] = up[i * size : (i + 1) * size, :].astype(bf16)


def feed_forward(ms, w, hid):
    n, size, model = len(ms), ms[0].shape[0], ms[0].shape[1]
    out = kernel_call(
        functools.partial(feed_forward_kernel, n, hid),
        [((size, model), bf16)] * n + [((n * size, hid), bf16)] * 2,
        (*ms, w),
        scratch=[pltpu.VMEM((n * size, model), bf16), pltpu.VMEM((n * size, hid), f32)],
        us=5.0,
    )
    return out[:n], out[n], out[n + 1]


def feed_mid_kernel(n, hid, *refs):
    ms, gs, w_ref, gain_ref = refs[:n], refs[n : 2 * n], refs[2 * n], refs[2 * n + 1]
    outs = refs[2 * n + 2 :]
    parts, r_ref, du_ref, gsum_ref, rows, up, dr = outs[:n], *outs[n:]
    size = ms[0].shape[0]
    gather_rows(ms, rows)
    up[...] = nn(rows[...], w_ref[:, 0:hid])
    gather_rows(gs, rows)
    dr[...] = nn(rows[...], w_ref[:, hid : 2 * hid])

    def body(at):
        r, slope = gelu_both(up[at, :])
        r_ref[at, :] = r.astype(bf16)
        du_ref[at, :] = (dr[at, :] * slope).astype(bf16)

    by_rows(n * size, 32, body)
    finish_back(ms, du_ref, w_ref, gain_ref, parts, gsum_ref, up, hid)


def finish_back(ms, du_ref, w_ref, gain_ref, parts, gsum_ref, part, hid):
    size = ms[0].shape[0]
    part[...] = nt(du_ref[...], w_ref[:, 0:hid])
    gsum = jnp.zeros(gsum_ref.shape, f32)
    for i, m in enumerate(ms):
        own = part[i * size : (i + 1) * size, :]
        parts[i][...] = own.astype(bf16)
        gsum = gsum + jnp.sum(own * m[...].astype(f32), axis=0, keepdims=True)
    gsum_ref[...] = gsum / gain_ref[...]


def feed_mid(ms, gs, w, hid, gain):
    n, size, model = len(ms), ms[0].shape[0], ms[0].shape[1]
    out = kernel_call(
        functools.partial(feed_mid_kernel, n, hid),
        [((size, model), bf16)] * n + [((n * size, hid), bf16)] * 2 + [((1, model), f32)],
        (*ms, *gs, w, gain.reshape(1, -1)),
        scratch=[pltpu.VMEM((n * size, model), bf16)] + [pltpu.VMEM((n * size, hid), f32)] * 2,
        mib=16,
        us=6.0,
    )
    return out[:n], out[n], out[n + 1], out[n + 2]


def feed_back_kernel(n, hid, *refs):
    ms, gs, slope_ref, w_ref, gain_ref = refs[:n], refs[n : 2 * n], refs[2 * n], refs[2 * n + 1], refs[2 * n + 2]
    outs = refs[2 * n + 3 :]
    parts, du_ref, gsum_ref, rows, dr = outs[:n], *outs[n:]
    gather_rows(gs, rows)
    dr[...] = nn(rows[...], w_ref[:, hid : 2 * hid])

    def body(at):
        du_ref[at, :] = (dr[at, :] * slope_ref[at, :].astype(f32)).astype(bf16)

    by_rows(dr.shape[0], 32, body)
    finish_back(ms, du_ref, w_ref, gain_ref, parts, gsum_ref, dr, hid)


def feed_back(ms, gs, slope, w, hid, gain):
    n, size, model = len(ms), ms[0].shape[0], ms[0].shape[1]
    out = kernel_call(
        functools.partial(feed_back_kernel, n, hid),
        [((size, model), bf16)] * n + [((n * size, hid), bf16), ((1, model), f32)],
        (*ms, *gs, slope, w, gain.reshape(1, -1)),
        scratch=[pltpu.VMEM((n * size, model), bf16), pltpu.VMEM((n * size, hid), f32)],
        us=4.0,
    )
    return out[:n], out[n], out[n + 1]


def add_kernel(a_ref, b_ref, out_ref):
    def body(at):
        out_ref[at, :] = (a_ref[at, :].astype(f32) + b_ref[at, :].astype(f32)).astype(bf16)

    by_rows(a_ref.shape[0], 192, body)


def add(a, b):
    return kernel_call(add_kernel, [(a.shape, bf16)], (a, b), mib=4, us=1.0)[0]


def places(core_ref, halves, n, size):
    if halves == 1:
        return [pl.ds(i * size, size) for i in range(n)]
    core, half = core_ref[0], n // 2 * size
    own = [pl.ds(pl.multiple_of(core * half + i * size, size), size) for i in range(n // 2)]
    return own + [pl.ds(pl.multiple_of((1 - core) * half + i * size, size), size) for i in range(n // 2)]


def project_kernel(halves, n, core_ref, *refs):
    ns, w_ref, outs = refs[:n], refs[n], refs[n + 1 :]
    size = ns[0].shape[0]
    for i, to in enumerate(places(core_ref, halves, n, size)):
        x = ns[i][...]
        for j in range(3):
            outs[j][to, :] = nn(x, w_ref[j]).astype(bf16)
        outs[3][to, :] = x
    if len(outs) > 4:
        channels = outs[0].shape[1]
        outs[4][:, 0:channels] = outs[1][...]
        outs[4][:, channels : 2 * channels] = outs[2][...]


def project(core, halves, ns, w, pair=False):
    n, size, model, channels = len(ns), ns[0].shape[0], ns[0].shape[1], w.shape[2]
    return kernel_call(
        functools.partial(project_kernel, halves, n),
        [((n * size, channels), bf16)] * 3
        + [((n * size, model), bf16)]
        + [((n * size, 2 * channels), bf16)] * pair,
        (*ns, w),
        scalars=(core,),
        us=3.0,
    )


def out_kernel(halves, n, index, state, core_ref, y_ref, w_ref, *refs):
    if state:
        sin_ref = refs[4]
        parts, yb_ref = refs[5 : 5 + n], refs[5 + n]
        qr = rising(*refs[:4])
        yb_ref[...] = (y_ref[...] + nt(qr, expand(sin_ref[...]).astype(bf16))).astype(bf16)
    else:
        parts, yb_ref = refs[:n], y_ref
    size = parts[0].shape[0]
    for i, to in enumerate(places(core_ref, halves, n, size)):
        parts[i][...] = nt(yb_ref[to, :], w_ref[index]).astype(bf16)


def project_out(core, halves, n, y, w, index, state=()):
    size, model = y.shape[0] // n, w.shape[1]
    outs = [((size, model), bf16)] * n
    if state:
        outs.append((y.shape, bf16))
    return kernel_call(
        functools.partial(out_kernel, halves, n, index, bool(state)),
        outs,
        (y, w, *state),
        scalars=(core,),
        us=2.0,
    )


def out_back_kernel(halves, n, index, state, core_ref, *refs):
    gs, w_ref = refs[:n], refs[n]
    refs = refs[n + 1 :]
    if state:
        rising_refs = refs[:4]
        refs = refs[4:]
    dy_ref, ordered_ref = refs[0], refs[1]
    size = gs[0].shape[0]
    for i, to in enumerate(places(core_ref, halves, n, size)):
        g = gs[i][...]
        dy_ref[to, :] = nn(g, w_ref[index]).astype(bf16)
        ordered_ref[to, :] = g
    if state:
        refs[2][...] = compact(tn(dy_ref[...], rising(*rising_refs)))


def out_back(core, halves, gs, w, index, state=()):
    n, size, model, channels = len(gs), gs[0].shape[0], gs[0].shape[1], w.shape[2]
    outs = [((n * size, channels), bf16), ((n * size, model), bf16)]
    if state:
        outs.append(((HEAD_DIM, channels), bf16))
    return kernel_call(
        functools.partial(out_back_kernel, halves, n, index, bool(state)),
        outs,
        (*gs, w, *state),
        scalars=(core,),
        us=2.0,
    )


def project_back_kernel(halves, n, kind, count, core_ref, dq_ref, *refs):
    others = refs[:count]
    w_ref, n_ref, gain_ref = refs[count : count + 3]
    outs = refs[count + 3 :]
    parts, cat_ref, gsum_ref = outs[:n], outs[n], outs[n + 1]
    rows, channels = dq_ref.shape
    cat_ref[:, 0:channels] = dq_ref[...]
    if kind == "halo":
        dk_ref, dv_ref, extra_ref = others
        cut = rows - extra_ref.shape[0]
        cat_ref[0:cut, channels : 2 * channels] = dk_ref[0:cut, :].astype(bf16)
        cat_ref[cut:rows, channels : 2 * channels] = (
            dk_ref[cut:rows, :] + extra_ref[...].astype(f32)
        ).astype(bf16)
        cat_ref[:, 2 * channels : 3 * channels] = dv_ref[...].astype(bf16)
    else:
        total = others[0][...].astype(f32)
        for other in others[1:]:
            total = total + other[...].astype(f32)
        cat_ref[:, channels : 3 * channels] = total.astype(bf16)
    size = parts[0].shape[0]
    gsum_ref[...] = jnp.zeros(gsum_ref.shape, f32)
    for i, to in enumerate(places(core_ref, halves, n, size)):
        part = sum(nt(cat_ref[to, j * channels : (j + 1) * channels], w_ref[j]) for j in range(3))
        parts[i][...] = part.astype(bf16)
        gsum_ref[...] += jnp.sum(part * n_ref[to, :].astype(f32), axis=0, keepdims=True)
    gsum_ref[...] = gsum_ref[...] / gain_ref[...]


def project_back(core, halves, n, kind, dq, others, w, normed, gain):
    rows, channels = dq.shape
    size, model = rows // n, normed.shape[1]
    out = kernel_call(
        functools.partial(project_back_kernel, halves, n, kind, len(others)),
        [((size, model), bf16)] * n + [((rows, 3 * channels), bf16), ((1, model), f32)],
        (dq, *others, w, normed, gain.reshape(1, -1)),
        scalars=(core,),
        us=3.0,
    )
    return out[:n], out[n], out[n + 1]


def at_rows(value, start, count):
    return lax.dynamic_slice_in_dim(value, start, count, 0)


def tie(*values):
    return lax.optimization_barrier(values)


class Rows:
    halves = 1
    chunks = 1
    grad_type = f32

    def __init__(self):
        self.blocks = lax.axis_size("ctx")
        self.place = lax.axis_index("ctx")
        self.core = self.place

    def enter(self, rows):
        return rows

    def leave_start(self, rows):
        return rows

    def leave_end(self, rows, there):
        return rows

    def spread(self, rows):
        return [rows]

    def half_sum(self, parts):
        return parts[0]

    def total(self, value):
        return [lax.psum(value, "tp")]

    def local(self, value):
        return value

    def assemble(self, share):
        return lax.all_gather(share, "fsdp", axis=1, tiled=True)

    def setup(self, ids, taps_n, channels):
        row = ids
        ids = ids[0]
        n, rows = self.blocks, ids.shape[0]
        halo = lax.ppermute(ids[rows - taps_n :].astype(bf16), "ctx", [(i, i + 1) for i in range(n - 1)])
        ext = jnp.concatenate([halo.astype(jnp.int32), ids])
        at = jnp.arange(ext.shape[0], dtype=jnp.int32)
        same = ext[:, None] == ext[None, :]
        age = jnp.sum((same & (at[None, :] < at[:, None])).astype(jnp.int32), axis=1)
        rem = jnp.sum((same & (at[None, :] > at[:, None])).astype(jnp.int32), axis=1)
        age, rem = [jnp.broadcast_to(v[:, None], (ext.shape[0], channels)) for v in (age, rem)]
        key_ids = lax.all_gather(ids.astype(bf16), "ctx", axis=0, tiled=True).astype(jnp.int32)
        count = rows // CHUNK
        high = self.place * count + jnp.arange(count, dtype=jnp.int32)
        firsts = ids[::CHUNK]
        low = jnp.sum((key_ids[None, :] < firsts[:, None]).astype(jnp.int32), axis=1) // CHUNK
        limits = jnp.stack([low, high, high])
        entry = ext[taps_n - 1].reshape(1, 1)
        return row, ids[:, None], entry, age, rem, (limits, ids[:, None], row, key_ids[:, None], key_ids[None])

    def from_previous(self, value):
        n = self.blocks
        return lax.ppermute(value, "ctx", [(i, i + 1) for i in range(n - 1)])

    def to_previous(self, value):
        n = self.blocks
        return lax.ppermute(value, "ctx", [(i + 1, i) for i in range(n - 1)])

    def state_before(self, factor, state):
        factors = lax.all_gather(factor.astype(bf16), "ctx").astype(f32)
        states = lax.all_gather(state, "ctx")

        def one(hop, held):
            return states[hop].astype(f32) + factors[hop] * held

        held = lax.fori_loop(0, self.place, one, jnp.zeros(state.shape, f32))
        return held.astype(bf16)

    def grad_after(self, factor, dstate):
        factors = lax.all_gather(factor.astype(bf16), "ctx").astype(f32)
        states = lax.all_gather(dstate, "ctx")

        def one(hop, held):
            at = self.blocks - 1 - hop
            return states[at].astype(f32) + factors[at] * held

        held = lax.fori_loop(0, self.blocks - 1 - self.place, one, jnp.zeros(dstate.shape, f32))
        return held.astype(bf16)

    def attend(self, setup, q, kv):
        limits, col, _, _, key_tiles = setup
        kv = lax.all_gather(kv, "ctx", axis=0, tiled=True)
        return attend(limits, q, kv, col, key_tiles), kv

    def attend_back(self, setup, kept, q, kv, grad, mixed, stats, wait):
        limits, _, tiles, key_col, _ = setup
        dq, dkv = attend_back(limits, q, kept, grad, mixed, stats, tiles, key_col, bf16, bf16)
        return dq, [lax.psum_scatter(dkv, "ctx", scatter_dimension=0, tiled=True)], wait

    def scatter(self, value):
        return [lax.psum_scatter(value, "fsdp", scatter_dimension=0, tiled=True)]

    def scattered(self, parts):
        return parts[0]

    def to_owner(self, value):
        return lax.psum(value, "ctx")

    def owned(self, value, got):
        return got

    def over_places(self, value):
        return lax.psum(value, ("ctx", "tp"))


class Pairs(Rows):
    halves = 2
    chunks = 1
    grad_type = bf16

    def __init__(self):
        self.blocks = 2
        self.core = lax.axis_index("ctx")
        self.chip = lax.axis_index("tp")
        self.place = self.chip // 2
        self.home = self.core == self.place

    def send(self, value, pairs):
        number = [(4 * c + t, 4 * d + u) for (c, t), (d, u) in pairs]
        return lax.ppermute(value, ("ctx", "tp"), number)

    def swap(self, value):
        return lax.ppermute(value, "ctx", [(0, 1), (1, 0)])

    def neighbour(self, value):
        return lax.ppermute(value, "tp", [(0, 1), (1, 0), (2, 3), (3, 2)])

    def across(self, value):
        return lax.ppermute(value, "tp", [(0, 2), (2, 0), (1, 3), (3, 1)])

    def from_home_core(self, value):
        return self.send(value, [((t // 2, t), (1 - t // 2, t)) for t in range(4)])

    def enter(self, rows):
        half = rows.shape[0] // 2
        got = self.from_home_core(at_rows(rows, (1 - self.core) * half, half))
        return jnp.where(self.home, at_rows(rows, self.core * half, half), got)

    def setup(self, ids, taps_n, channels):
        other = self.swap(ids)
        own = jnp.where(self.home, ids, other)
        first = jnp.where(self.core == 0, ids, other)
        before = jnp.where(self.place == 1, first, 0)
        col, before_col, entry, age, rem, own_limits, prev_limits = setup_ids(own, before, taps_n, channels)
        return own, col, entry, age, rem, (own_limits, prev_limits, col, before_col, own, before)

    def in_order(self, own, other):
        first = self.core == 0
        return jnp.concatenate([jnp.where(first, own, other), jnp.where(first, other, own)])

    def leave_start(self, rows):
        return self.across(rows)

    def leave_end(self, rows, there):
        got = self.swap(jnp.where(self.home, there, rows))
        return self.in_order(jnp.where(self.home, rows, there), got)

    def spread(self, rows):
        return [rows, self.swap(rows)]

    def half_sum(self, parts):
        return add(parts[0], self.swap(parts[1]))

    def total(self, value):
        return [value, self.neighbour(value)]

    def local(self, value):
        got = self.send(
            value, [((c, 2 * c + e), (c, 2 - 2 * c + e)) for c in range(2) for e in range(2)]
        )
        return jnp.where(self.home, value, got)

    def around(self, value):
        return [lax.ppermute(value, "fsdp", [(i, i ^ k) for i in range(4)]) for k in (1, 2, 3)]

    def assemble(self, share):
        place, size = lax.axis_index("fsdp"), share.shape[1]
        whole = jnp.zeros((share.shape[0], 4 * size, share.shape[2]), share.dtype)
        for k, part in enumerate([share] + self.around(share)):
            whole = lax.dynamic_update_slice_in_dim(whole, part, (place ^ k) * size, 1)
        return whole

    def from_previous(self, value):
        return self.send(value, [((c, t), (c, t + 2)) for c in range(2) for t in range(2)])

    def to_previous(self, value):
        return self.send(value, [((c, t + 2), (c, t)) for c in range(2) for t in range(2)])

    def state_before(self, factor, state):
        return self.from_previous(state)

    def grad_after(self, factor, dstate):
        return self.to_previous(dstate)

    def attend(self, setup, q, kv):
        own_limits, prev_limits, col, _, tiles, prev_tiles = setup
        before = self.from_previous(kv)
        held = attend(own_limits, q, kv, col, tiles, finish=False)
        return attend(prev_limits, q, before, col, prev_tiles, held), before

    def attend_back(self, setup, before, q, kv, grad, mixed, stats, wait):
        own_limits, prev_limits, col, prev_col, tiles, _ = setup
        dq, dkv_prev = attend_back(prev_limits, q, before, grad, mixed, stats, tiles, prev_col, f32, bf16)
        got = self.to_previous(dkv_prev)
        dq, *wait = tie(dq, *wait)
        dq, dkv = attend_back(own_limits, q, kv, grad, mixed, stats, tiles, col, bf16, f32, (dq,))
        return dq, [dkv, got], wait

    def scatter(self, value):
        place = lax.axis_index("fsdp")
        size = value.shape[0] // 4
        parts = [at_rows(value, place * size, size)]
        for k in (1, 2, 3):
            part = at_rows(value, (place ^ k) * size, size)
            parts.append(lax.ppermute(part, "fsdp", [(i, i ^ k) for i in range(4)]))
        return parts

    def scattered(self, parts):
        return sum(part.astype(f32) for part in parts).astype(bf16)

    def to_owner(self, value):
        return self.send(
            value, [((c, 2 - 2 * c + e), (c, 2 * c + e)) for c in range(2) for e in range(2)]
        )

    def owned(self, value, got):
        value = (value.astype(f32) + got.astype(f32)).astype(bf16)
        return jnp.where(self.home, value, self.from_home_core(value))

    def over_places(self, value):
        for step in (self.swap, self.neighbour, self.across):
            value = (value.astype(f32) + step(value).astype(f32)).astype(bf16)
        return value


def dot_tn(a, b):
    return jnp.einsum("tf,td->fd", a, b, preferred_element_type=f32).astype(bf16)


def feed_shares(reduced):
    width = reduced.shape[1] // 2
    return reduced[:, :width].astype(f32), reduced[:, width:].T.astype(f32)


def mixer_shares(reduced, channels):
    parts = [reduced[:, j * channels : (j + 1) * channels].astype(f32) for j in range(3)]
    return jnp.stack(parts), reduced[:, 3 * channels : 4 * channels].T.astype(f32)


def run(plan, inputs, cotangent, segments, gains, last_gain, in_weight, h3_out, attn_out, up_weight, down_weight, shift_taps, decay_rate):
    halves, chunks = plan.halves, plan.chunks
    pieces = halves * chunks
    slots = lax.axis_size("fsdp")
    hid = up_weight.shape[2]
    channels = h3_out.shape[0]
    taps_n = shift_taps.shape[0]
    share = h3_out.shape[1]
    core = plan.core.astype(jnp.int32).reshape(1)

    def split(value):
        size = value.shape[0] // chunks
        return [value[i * size : (i + 1) * size] for i in range(chunks)]

    def by_piece(spreads):
        return [s[i] for i in range(halves) for s in spreads]

    def by_chunk(parts):
        return [[parts[i * chunks + j] for i in range(halves)] for j in range(chunks)]

    def joined(spreads):
        return jnp.concatenate([piece for s in spreads for piece in s])

    def norms(xs, adds, gain):
        out = [norm(x, a, gain) for x, a in zip(xs, adds)]
        return [o[0] for o in out], [plan.spread(o[1]) for o in out]

    def norm_backs(xs, grads, adds, gain):
        out = [norm_back(x, g, a, gain) for x, g, a in zip(xs, grads, adds)]
        return [o[0] for o in out], [plan.spread(o[1]) for o in out]

    def totals(parts, *others):
        sums = [plan.half_sum(p) for p in parts]
        sums[-1], *others = tie(sums[-1], *others)
        adds = [plan.total(v) for v in sums]
        return (adds, *others) if others else adds

    def with_sums(adds, *others):
        adds[-1][-1], *others = tie(adds[-1][-1], *others)
        return others

    weights0 = plan.local(jnp.concatenate([in_weight[0], h3_out.T[None]]))
    xs = split(plan.enter(inputs[0]))
    seg_row, seg_col, entry, age, rem, setup = plan.setup(segments + 1, taps_n, channels)
    rows = seg_row.shape[1]
    small = jnp.concatenate([shift_taps, decay_rate.reshape(1, -1)])
    feed = [jnp.concatenate([up_weight[i], down_weight[i].T], axis=1) for i in range(2)]
    mix = jnp.concatenate([in_weight[1], attn_out.T[None]])
    x0, n0s = norms(xs, [[]] * chunks, gains[0])
    weights0, small, feed[0] = tie(weights0, small, feed[0])
    weights0 = plan.assemble(weights0)
    feed[0], mix = tie(plan.local(feed[0]), mix)
    small, mix = plan.local(small), plan.local(mix)
    weights0, age, rem = tie(weights0, age, rem)

    q0, k0, v0, n0 = project(core, halves, by_piece(n0s), weights0)
    k0, small = tie(k0, small)
    halo = plan.from_previous(k0[rows - taps_n :])
    halo, feed[0], feed[1] = tie(halo, feed[0], feed[1])
    feed0 = lax.all_gather(feed[0], "fsdp", axis=0, tiled=True)
    feed[1] = plan.local(feed[1])
    taps, rate_row = small[:taps_n], small[taps_n:]
    factor = jnp.exp(-rate_row * rows) * (entry == seg_row[:, rows - 1 :]).astype(f32)
    ks, state_end, y0, saved = h3_forward(k0, halo, q0, v0, taps, rate_row, age, seg_col, seg_row)
    state_in = plan.state_before(factor, state_end)
    state_in, mix = tie(state_in, mix)
    mix1 = lax.all_gather(mix, "fsdp", axis=1, tiled=True)
    *parts, y0 = project_out(core, halves, pieces, y0, weights0, 3, (q0, rate_row, seg_col, entry, state_in))
    adds = totals(by_chunk(parts))
    (feed0,) = with_sums(adds, feed0)
    x1, m0s = norms(x0, adds, gains[1])
    out = [feed_forward(m, feed0, hid) for m in m0s]
    parts, r0, slope0 = [[o[i] for o in out] for i in range(3)]
    x2, n2s = norms(x1, totals(parts), gains[2])

    n2s[0][0], g_in, feed[1] = tie(n2s[0][0], cotangent[0], feed[1])
    feed1 = lax.all_gather(feed[1], "fsdp", axis=0, tiled=True)
    gs = split(plan.enter(g_in))
    flat = [p for g in gs for p in plan.spread(g)]
    mix1, *flat = tie(mix1, *flat)
    g_ins = [flat[halves * i : halves * (i + 1)] for i in range(chunks)]

    q2, _, _, n2, kv2 = project(core, halves, by_piece(n2s), mix1, True)
    (mixed, stats, mixed_bf), kept = plan.attend(setup, q2, kv2)
    parts = project_out(core, halves, pieces, mixed_bf, mix1, 3)
    x3, m1s = norms(x2, totals(by_chunk(parts)), last_gain)

    out = [feed_mid(m, g, feed1, hid, last_gain) for m, g in zip(m1s, g_ins)]
    parts, r1, du1, gain3 = [[o[i] for o in out] for i in range(4)]
    adds, r1, du1, m1s, g_ins = totals(parts, r1, du1, m1s, g_ins)
    size = r1[0].shape[0] // halves
    last = [
        [
            jnp.einsum(
                "tf,df->td", r[i * size : (i + 1) * size], feed1[:, hid:], preferred_element_type=f32
            ).astype(bf16)
            for i in range(halves)
        ]
        for r in r1
    ]
    feed1_grad = jnp.concatenate(
        [
            dot_tn(joined(m1s), jnp.concatenate(du1)),
            dot_tn(joined(g_ins), jnp.concatenate(r1)),
        ],
        axis=1,
    )
    feed1_grad, *flat = with_sums(adds, feed1_grad, *[p for s in last for p in s])
    feed1_parts = plan.scatter(feed1_grad)
    last = totals([flat[halves * i : halves * (i + 1)] for i in range(chunks)])
    grads, gbs = norm_backs(x3, gs, adds, last_gain)
    dmixed, grad_bf1 = out_back(core, halves, by_piece(gbs), mix1, 3)
    flat = [a for adds in last for a in adds]
    dq, dkv, flat = plan.attend_back(setup, kept, q2, kv2, dmixed, mixed, stats, flat)
    dkv[0], *feed1_parts = tie(dkv[0], *feed1_parts)
    feed1_grad = plan.scattered(feed1_parts)
    count = len(flat) // chunks
    x4 = []
    for i in range(chunks):
        x4.append(x3[i] + sum(a.astype(f32) for a in flat[count * i : count * (i + 1)]))
    x4 = jnp.concatenate(x4).astype(bf16)
    dkv[-1], feed1_grad, x4 = tie(dkv[-1], feed1_grad, x4)
    parts, cat1, gain2 = project_back(core, halves, pieces, "sum", dq, dkv, mix1, n2, gains[2])
    adds, cat1, n2 = totals(by_chunk(parts), cat1, n2)
    mix1_grad = jnp.concatenate([dot_tn(n2, cat1), dot_tn(grad_bf1, mixed_bf)], axis=1)
    mix1_grad, feed1_grad, x4 = with_sums(adds, mix1_grad, feed1_grad, x4)
    x4_there = plan.leave_start(x4)
    mix1_parts = plan.scatter(mix1_grad)
    grads, gbs = norm_backs(x2, grads, adds, gains[2])

    out = [feed_back(m, g, s, feed0, hid, gains[1]) for m, g, s in zip(m0s, gbs, slope0)]
    parts, du0, gain1 = [[o[i] for o in out] for i in range(3)]
    adds, m0s, du0, gbs, r0 = totals(parts, m0s, du0, gbs, r0)
    feed0_grad = jnp.concatenate(
        [
            dot_tn(joined(m0s), jnp.concatenate(du0)),
            dot_tn(joined(gbs), jnp.concatenate(r0)),
        ],
        axis=1,
    )
    feed0_grad, x4_there, *mix1_parts = with_sums(adds, feed0_grad, x4_there, *mix1_parts)
    feed0_parts = plan.scatter(feed0_grad)
    grads, gbs = norm_backs(x1, grads, adds, gains[1])
    mix1_grad = plan.scattered(mix1_parts)
    dy, grad_bf0, dstate = out_back(
        core, halves, by_piece(gbs), weights0, 3, (q0, rate_row, seg_col, entry)
    )
    dstate_end = plan.grad_after(factor, dstate)
    dstate_end, feed1_grad, mix1_grad = tie(dstate_end, feed1_grad, mix1_grad)
    feed1_got, mix1_got = plan.to_owner(feed1_grad), plan.to_owner(mix1_grad)
    output = plan.leave_end(x4, x4_there)
    dq, dk, dhalo, dv, dtaps, drate = h3_back_call(
        q0, ks, v0, dy, saved, dstate_end, rate_row, seg_col, seg_row, entry, k0, halo, taps, age, rem, state_in
    )
    halo_grad = plan.to_previous(dhalo)
    dq, feed1_got, mix1_got, output, *feed0_parts = tie(dq, feed1_got, mix1_got, output, *feed0_parts)
    feed0_grad = plan.scattered(feed0_parts)
    feed0_got = plan.to_owner(feed0_grad)
    parts, cat0, gain0 = project_back(
        core, halves, pieces, "halo", dq, (dk, dv, halo_grad), weights0, n0, gains[0]
    )
    adds, cat0, n0, dtaps = totals(by_chunk(parts), cat0, n0, dtaps)

    mix0 = jnp.concatenate([dot_tn(n0, cat0), dot_tn(grad_bf0, y0)], axis=1)
    mix0 = mix0.reshape(slots, share, 4 * channels)
    taps_each = taps_n // slots
    small = jnp.concatenate(
        [
            dtaps.reshape(slots, taps_each, channels),
            jnp.pad(
                drate.reshape(-1, slots, HEAD_DIM // slots).transpose(1, 0, 2).reshape(slots, 1, -1),
                ((0, 0), (0, 0), (0, channels - channels // slots)),
            ),
            jnp.concatenate([gain0, sum(gain1), gain2, sum(gain3)]).reshape(4, slots, share).transpose(1, 0, 2),
        ],
        axis=1,
    ).astype(bf16)
    small = jnp.pad(small, ((0, 0), (0, (-small.shape[1]) % 32), (0, 3 * channels)))
    height = share + small.shape[1]
    mix0_parts = plan.scatter(jnp.concatenate([mix0, small], axis=1).reshape(slots * height, 4 * channels))
    grads = [
        norm_back(x, g, a, gains[0])[0].astype(plan.grad_type) for x, g, a in zip(x0, grads, adds)
    ]
    mix0 = plan.scattered(mix0_parts)
    mix0_got = plan.to_owner(mix0)
    grads[-1], feed1_got, mix1_got, feed0_got, gain_rows = tie(
        grads[-1], feed1_got, mix1_got, feed0_got, mix0[share + taps_each + 1 : share + taps_each + 5, :channels]
    )
    there = [plan.leave_start(g) for g in grads]
    gain_rows = plan.over_places(gain_rows).astype(f32)
    feed1 = plan.owned(feed1_grad, feed1_got)
    mix1 = plan.owned(mix1_grad, mix1_got)
    feed0 = plan.owned(feed0_grad, feed0_got)
    mix0 = plan.owned(mix0, mix0_got)
    input_grad = plan.leave_end(jnp.concatenate(grads), jnp.concatenate(there)).astype(f32)
    small = mix0[share:, :channels]
    in0_grad, out0_grad = mixer_shares(mix0[:share], channels)
    dtaps = small[:taps_each].astype(f32)
    drate = small[taps_each, : channels // slots].astype(f32).reshape(-1, HEAD_DIM // slots)
    up0_grad, down0_grad = feed_shares(feed0)
    up1_grad, down1_grad = feed_shares(feed1)
    in1_grad, out1_grad = mixer_shares(mix1, channels)
    return (
        output[None],
        input_grad[None],
        gain_rows[:3],
        gain_rows[3],
        jnp.stack([in0_grad, in1_grad]),
        out0_grad,
        out1_grad,
        jnp.stack([up0_grad, up1_grad]),
        jnp.stack([down0_grad, down1_grad]),
        dtaps,
        drate,
    )


def shards(*arguments):
    paired = lax.axis_size("ctx") == 2 and lax.axis_size("tp") == 4 and lax.axis_size("fsdp") == 4
    return run(Pairs() if paired else Rows(), *arguments)


def solution(mesh):
    placed = (
        P("fsdp", "ctx", None),
        P("fsdp", "ctx", None),
        P("fsdp", "ctx"),
        P(),
        P(),
        P(None, None, "fsdp", "tp"),
        P("tp", "fsdp"),
        P("tp", "fsdp"),
        P(None, "fsdp", "tp"),
        P(None, "tp", "fsdp"),
        P(None, "tp"),
        P("tp", None),
    )
    return jax.shard_map(
        shards,
        mesh=mesh,
        in_specs=placed,
        out_specs=(
            P("fsdp", "ctx", None),
            P("fsdp", "ctx", None),
            P(None, "fsdp"),
            P("fsdp"),
            P(None, None, "fsdp", "tp"),
            P("tp", "fsdp"),
            P("tp", "fsdp"),
            P(None, "fsdp", "tp"),
            P(None, "tp", "fsdp"),
            P("fsdp", "tp"),
            P("tp", "fsdp"),
        ),
        check_vma=False,
    )
```

```python
import functools

import jax
import jax.numpy as jnp
from jax import lax
from jax.experimental import pallas as pl
from jax.experimental.pallas import tpu as pltpu
from jax.sharding import PartitionSpec as P

HEAD_DIM = 64
epsilon = 1e-05
masked_low = -1e30
bf16 = jnp.bfloat16
f32 = jnp.float32
scale = HEAD_DIM ** (-0.5)
CHUNK = 256


def nn(a, b):
    return lax.dot_general(a, b, (((1,), (0,)), ((), ())), preferred_element_type=f32)


def nt(a, b):
    return lax.dot_general(a, b, (((1,), (1,)), ((), ())), preferred_element_type=f32)


def tn(a, b):
    return lax.dot_general(a, b, (((0,), (0,)), ((), ())), preferred_element_type=f32)


def head_masks(rows, channels):
    lane = lax.broadcasted_iota(jnp.int32, (rows, channels), 1)
    return [(lane >= HEAD_DIM * h) & (lane < HEAD_DIM * (h + 1)) for h in range(channels // HEAD_DIM)]


def same_head(channels):
    row = lax.broadcasted_iota(jnp.int32, (channels, channels), 0) // HEAD_DIM
    lane = lax.broadcasted_iota(jnp.int32, (channels, channels), 1) // HEAD_DIM
    return row == lane


def compact(state):
    channels = state.shape[1]
    state = jnp.where(same_head(channels), state, 0.0)
    parts = [state[HEAD_DIM * h : HEAD_DIM * (h + 1), :] for h in range(channels // HEAD_DIM)]
    return sum(parts[1:], parts[0]).astype(bf16)


def expand(small):
    channels = small.shape[1]
    tall = jnp.concatenate([small.astype(f32)] * (channels // HEAD_DIM), axis=0)
    return jnp.where(same_head(channels), tall, 0.0)


def params(mib):
    return pltpu.CompilerParams(vmem_limit_bytes=mib * 1024 * 1024)


def kernel_call(kernel, outs, arrays, scalars=(), scratch=(), mib=12, us=2.0):
    vm = pl.BlockSpec(memory_space=pltpu.VMEM)
    sm = pl.BlockSpec(memory_space=pltpu.SMEM)
    return pl.pallas_call(
        kernel,
        out_shape=[jax.ShapeDtypeStruct(s, d) for s, d in outs],
        in_specs=[sm] * len(scalars) + [vm] * len(arrays),
        out_specs=[vm] * len(outs),
        scratch_shapes=list(scratch),
        compiler_params=params(mib),
        cost_estimate=pl.CostEstimate(flops=int(us * 1e9), bytes_accessed=1000, transcendentals=0),
    )(*scalars, *arrays)


def column_of(row):
    return jnp.broadcast_to(row.astype(f32), (8, row.shape[1])).T[:, 0:1].astype(jnp.int32)


def setup_kernel(taps_n, ids_ref, before_ref, col_ref, before_col_ref, entry_ref, age_ref, rem_ref, own_ref, prev_ref):
    rows = ids_ref.shape[1]
    channels = age_ref.shape[1]
    count = rows // CHUNK
    own, before = ids_ref[...], before_ref[...]
    col_ref[...] = column_of(own)
    before_col_ref[...] = column_of(before)
    entry_ref[...] = before_col_ref[rows - 1 : rows, :]
    lane = lax.broadcasted_iota(jnp.int32, (64, rows), 1)
    row = lax.broadcasted_iota(jnp.int32, (64, rows), 0)
    halo_lane = lane >= rows - taps_n

    def fill(ids, at, start):
        in_own = ids == own
        in_halo = (ids == before) & halo_lane
        both = (in_own & (lane < row + start)).astype(f32) + (in_halo & (lane - rows < row + start)).astype(f32)
        after = (in_own & (lane > row + start)).astype(f32) + (in_halo & (lane - rows > row + start)).astype(f32)
        age = jnp.sum(both, axis=1, keepdims=True).astype(jnp.int32)
        rem = jnp.sum(after, axis=1, keepdims=True).astype(jnp.int32)
        age_ref[at, :] = jnp.broadcast_to(age, (64, channels))
        rem_ref[at, :] = jnp.broadcast_to(rem, (64, channels))

    fill(before_col_ref[rows - 64 : rows, :], pl.ds(0, 64), -64)

    def block(b, carry):
        start = pl.multiple_of(b * 64, 64)
        fill(col_ref[pl.ds(start, 64), :], pl.ds(start + 64, 64), start)
        return carry

    lax.fori_loop(0, rows // 64, block, 0)
    for b in range(count):
        first = own[:, b * CHUNK : b * CHUNK + 1]
        low = jnp.sum((before < first).astype(f32)) + jnp.sum((own < first).astype(f32))
        low = low.astype(jnp.int32) // CHUNK
        own_ref[0, b] = jnp.maximum(low - count, 0)
        own_ref[1, b] = b
        own_ref[2, b] = b
        prev_ref[0, b] = low
        prev_ref[1, b] = count - 1
        prev_ref[2, b] = count + b


def setup_ids(ids, before, taps_n, channels):
    rows = ids.shape[1]
    count = rows // CHUNK
    vm, sm = pl.BlockSpec(memory_space=pltpu.VMEM), pl.BlockSpec(memory_space=pltpu.SMEM)
    shapes = [(rows, 1), (rows, 1), (1, 1), (rows + taps_n, channels), (rows + taps_n, channels), (3, count), (3, count)]
    return pl.pallas_call(
        functools.partial(setup_kernel, taps_n),
        out_shape=[jax.ShapeDtypeStruct(s, jnp.int32) for s in shapes],
        in_specs=[vm] * 2,
        out_specs=[vm] * 5 + [sm] * 2,
        compiler_params=params(8),
        cost_estimate=pl.CostEstimate(flops=int(2e9), bytes_accessed=1000, transcendentals=0),
    )(ids, before)


def tail_and_rise(rate, rows):
    pos = lax.broadcasted_iota(jnp.int32, (rows, rate.shape[1]), 0).astype(f32)
    return jnp.exp(-rate * (rows - 1.0 - pos)), jnp.exp(-rate * (pos + 1.0))


def rising(q_ref, rate_ref, segc_ref, entry_ref):
    rows = q_ref.shape[0]
    rise = tail_and_rise(rate_ref[...], rows)[1]
    rise = rise * ((segc_ref[...] == entry_ref[...]).astype(f32) * scale)
    return (q_ref[...].astype(f32) * rise).astype(bf16)


def rolled_down(ext_ref, age_ref, copies, rows):
    for r in range(8):
        copies[r, 8:rows, :] = jnp.where(age_ref[8:rows, :] >= r, ext_ref[8 - r : rows - r, :], 0.0)


def lane_tiles(channels):
    return [(low, min(low + 128, channels)) for low in range(0, channels, 128)]


def filtered(copies, taps_ref, reach_ref, reach_at, first, step, groups, size, low, high):
    reach = reach_ref[reach_at, low:high]
    base = first if step > 0 else first + step * (groups - 1)
    parts = [None] * groups
    for r in range(8):
        window = copies[r, pl.ds(base, size + 8 * (groups - 1)), low:high]
        for m in range(groups):
            at = 8 * m if step > 0 else 8 * (groups - 1 - m)
            term = window[at : at + size] * taps_ref[8 * m + r : 8 * m + r + 1, low:high]
            parts[m] = term if parts[m] is None else parts[m] + term
    total = parts[0]
    for m in range(1, groups):
        total = total + jnp.where(reach >= 8 * m, parts[m], 0.0)
    return total


def decay_factors(rate_row, rows):
    pos = lax.broadcasted_iota(jnp.int32, (rows, rate_row.shape[1]), 0).astype(f32)
    mid = 0.5 * rows
    q_fac = jnp.exp(-rate_row * (pos - mid))
    k_fac = jnp.exp(rate_row * (pos - mid))
    rise = jnp.exp(-rate_row * (pos + 1.0))
    tail = jnp.exp(-rate_row * (rows - 1.0 - pos))
    whole = jnp.exp(-rate_row * rows)
    return pos, mid, q_fac, k_fac, rise, tail, whole


def h3_kernel(
    taps_n,
    key_ref,
    halo_ref,
    q_ref,
    v_ref,
    taps_ref,
    rate_ref,
    age_ref,
    segc_ref,
    segr_ref,
    ks_ref,
    st_ref,
    y_ref,
    save_ref,
    ext,
    copies,
):
    rows, channels = key_ref.shape
    ext[0:taps_n, :] = halo_ref[...].astype(f32)
    ext[taps_n : taps_n + rows, :] = key_ref[...].astype(f32)
    rolled_down(ext, age_ref, copies, rows + taps_n)

    def block(b, carry):
        start = pl.multiple_of(b * 64, 64)
        for low, high in lane_tiles(channels):
            ks_ref[pl.ds(start, 64), low:high] = filtered(
                copies, taps_ref, age_ref, pl.ds(start + taps_n, 64), start + taps_n, -8, taps_n // 8, 64, low, high
            )
        return carry

    lax.fori_loop(0, rows // 64, block, 0)

    blocks = rows // CHUNK
    _, _, q_fac, k_fac, rise, tail, whole = decay_factors(rate_ref[...], CHUNK)
    heads = head_masks(CHUNK, channels)
    block_diag = same_head(channels)
    causal = lax.broadcasted_iota(jnp.int32, (CHUNK, CHUNK), 0) >= lax.broadcasted_iota(
        jnp.int32, (CHUNK, CHUNK), 1
    )
    state = jnp.zeros((channels, channels), f32)
    for b in range(blocks):
        sl = slice(b * CHUNK, (b + 1) * CHUNK)
        seg_c = segc_ref[sl, :]
        seg_r = segr_ref[:, sl]
        last = segc_ref[(b + 1) * CHUNK - 1 : (b + 1) * CHUNK, :]
        final = (seg_c == last).astype(f32)
        q = q_ref[sl, :].astype(f32) * scale
        k = ks_ref[sl, :]
        v = v_ref[sl, :]
        qf = (q * q_fac).astype(bf16)
        kf = (k * k_fac).astype(bf16)
        kt = (k * (tail * final)).astype(bf16)
        allowed = causal & (seg_c == seg_r)
        save_ref[b, :, :] = state
        y = jnp.zeros((CHUNK, channels), f32)
        if b > 0:
            before = segc_ref[b * CHUNK - 1 : b * CHUNK, :]
            qr = (q * (rise * (seg_c == before).astype(f32))).astype(bf16)
            y = nt(qr, state.astype(bf16))
            state = state * (whole * (last == before).astype(f32))
        for hm in heads:
            scores = nt(jnp.where(hm, qf, jnp.zeros_like(qf)), kf)
            scores = jnp.where(allowed, scores, 0.0).astype(bf16)
            y = y + jnp.where(hm, nn(scores, v), 0.0)
        y_ref[sl, :] = y
        state = state + jnp.where(block_diag, tn(v, kt), 0.0)
    st_ref[...] = compact(state)


def h3_forward(key, halo, q, v, taps, rate_row, age, seg_col, seg_row):
    rows, channels = q.shape
    taps_n = taps.shape[0]
    return kernel_call(
        functools.partial(h3_kernel, taps_n),
        [
            ((rows, channels), f32),
            ((HEAD_DIM, channels), bf16),
            ((rows, channels), f32),
            ((rows // CHUNK, channels, channels), f32),
        ],
        (key, halo, q, v, taps, rate_row, age, seg_col, seg_row),
        scratch=[pltpu.VMEM((rows + taps_n, channels), f32), pltpu.VMEM((8, rows + taps_n, channels), f32)],
        mib=20,
        us=10.0,
    )


def h3_back_kernel(
    taps_n,
    q_ref,
    ks_ref,
    v_ref,
    dy_ref,
    save_ref,
    dst_ref,
    rate_ref,
    segc_ref,
    segr_ref,
    entry_ref,
    key_ref,
    halo_ref,
    taps_ref,
    age_ref,
    rem_ref,
    sin_ref,
    dq_ref,
    dk_ref,
    dhalo_ref,
    dv_ref,
    dtaps_ref,
    drate_ref,
    ext,
    copies,
    dext,
    dcopies,
    tap_acc,
):
    rows, channels = q_ref.shape
    blocks = rows // CHUNK
    pos, mid, q_fac, k_fac, rise, tail, whole = decay_factors(rate_ref[...], CHUNK)
    heads = head_masks(CHUNK, channels)
    block_diag = same_head(channels)
    row = lax.broadcasted_iota(jnp.int32, (CHUNK, CHUNK), 0)
    lane = lax.broadcasted_iota(jnp.int32, (CHUNK, CHUNK), 1)
    dstate = expand(dst_ref[...])
    drate = jnp.zeros((1, channels), f32)
    dext[0:taps_n, :] = jnp.zeros((taps_n, channels), f32)
    dext[rows + taps_n : rows + 2 * taps_n, :] = jnp.zeros((taps_n, channels), f32)
    whole_keeps = []
    for b in range(blocks):
        before = entry_ref[...] if b == 0 else segc_ref[b * CHUNK - 1 : b * CHUNK, :]
        last = segc_ref[(b + 1) * CHUNK - 1 : (b + 1) * CHUNK, :]
        whole_keeps.append(whole * (last == before).astype(f32))
    state_in = expand(sin_ref[...])
    prefix = [jnp.ones_like(whole)]
    for b in range(blocks - 1):
        prefix.append(prefix[-1] * whole_keeps[b])
    for b in reversed(range(blocks)):
        sl = slice(b * CHUNK, (b + 1) * CHUNK)
        seg_c = segc_ref[sl, :]
        seg_r = segr_ref[:, sl]
        before = entry_ref[...] if b == 0 else segc_ref[b * CHUNK - 1 : b * CHUNK, :]
        last = segc_ref[(b + 1) * CHUNK - 1 : (b + 1) * CHUNK, :]
        carried = (seg_c == before).astype(f32)
        final = (seg_c == last).astype(f32)
        q = q_ref[sl, :].astype(f32) * scale
        k = ks_ref[sl, :]
        v = v_ref[sl, :]
        dy = dy_ref[sl, :]
        qf = (q * q_fac).astype(bf16)
        kf = (k * k_fac).astype(bf16)
        rise_c = rise * carried
        tail_c = tail * final
        qr = (q * rise_c).astype(bf16)
        kt = (k * tail_c).astype(bf16)
        same = seg_c == seg_r
        low_mask = (row >= lane) & same
        up_mask = (row <= lane) & same
        state = save_ref[b, :, :] + state_in * prefix[b]
        dstate_b = dstate.astype(bf16)
        dqf = jnp.zeros((CHUNK, channels), f32)
        dkf = jnp.zeros((CHUNK, channels), f32)
        dv = nt(kt, dstate_b)
        zero = jnp.zeros_like(qf)
        for hm in heads:
            kh = jnp.where(hm, kf, zero)
            vh = jnp.where(hm, v, zero)
            scores_t = jnp.where(up_mask, nt(kh, qf), 0.0).astype(bf16)
            dv = dv + jnp.where(hm, nn(scores_t, dy), 0.0)
            dsc = jnp.where(low_mask, nt(dy, vh), 0.0).astype(bf16)
            dsc_t = jnp.where(up_mask, nt(vh, dy), 0.0).astype(bf16)
            dqf = dqf + nn(dsc, kh)
            dkf = dkf + jnp.where(hm, nn(dsc_t, qf), 0.0)
        dqr = nn(dy, state.astype(bf16))
        dkt = nn(v, dstate_b)
        dq_ref[sl, :] = ((dqf * q_fac + dqr * rise_c) * scale).astype(bf16)
        dv_ref[sl, :] = dv.astype(bf16)
        dext[taps_n + b * CHUNK : taps_n + (b + 1) * CHUNK, :] = dkf * k_fac + dkt * tail_c
        part = (pos - mid) * (qf.astype(f32) * dqf - kf.astype(f32) * dkf)
        part = part + (pos + 1.0) * (qr.astype(f32) * dqr)
        part = part + (CHUNK - 1.0 - pos) * (kt.astype(f32) * dkt)
        drate = drate + jnp.sum(part, axis=0, keepdims=True)
        held = dstate * whole_keeps[b]
        drate = drate + CHUNK * jnp.sum(state * held, axis=0, keepdims=True)
        dstate = held + jnp.where(block_diag, tn(dy, qr), 0.0)
    drate_ref[...] = -drate

    total = rows + taps_n
    ext[0:taps_n, :] = halo_ref[...].astype(f32)
    ext[taps_n:total, :] = key_ref[...].astype(f32)
    rolled_down(ext, age_ref, copies, total)
    for r in range(8):
        dcopies[r, 0:total, :] = jnp.where(rem_ref[...] >= r, dext[r : total + r, :], 0.0)
        dcopies[r, total : total + taps_n, :] = jnp.zeros((taps_n, channels), f32)
    tap_acc[...] = jnp.zeros(tap_acc.shape, f32)

    def gathered(start, low, high):
        return filtered(
            dcopies, taps_ref, rem_ref, pl.ds(start, 64), start, 8, taps_n // 8, 64, low, high
        )

    def block(b, carry):
        start = pl.multiple_of(b * 64, 64)
        for low, high in lane_tiles(channels):
            dk_ref[pl.ds(start, 64), low:high] = gathered(start + taps_n, low, high)
        return carry

    lax.fori_loop(0, rows // 64, block, 0)
    for low, high in lane_tiles(channels):
        dhalo_ref[:, low:high] = gathered(0, low, high).astype(bf16)

    def tap_block(b, carry):
        start = pl.multiple_of(b * 64, 64)
        age = age_ref[pl.ds(start + taps_n, 64), :]
        grad = dext[pl.ds(start + taps_n, 64), :]
        for m in range(taps_n // 8):
            held = jnp.where(age >= 8 * m, grad, 0.0)
            for r in range(8):
                term = copies[r, pl.ds(start + taps_n - 8 * m, 64), :] * held
                tap_acc[8 * m + r, :, :] += jnp.sum(term.reshape(8, 8, channels), axis=0)
        return carry

    lax.fori_loop(0, rows // 64, tap_block, 0)
    dtaps_ref[...] = jnp.sum(tap_acc[...], axis=1)


def h3_back_call(q, ks, v, dy, save, dstate, rate_row, seg_col, seg_row, entry, key, halo, taps, age, rem, state_in):
    rows, channels = q.shape
    taps_n = taps.shape[0]
    total = rows + taps_n
    return kernel_call(
        functools.partial(h3_back_kernel, taps_n),
        [
            ((rows, channels), bf16),
            ((rows, channels), f32),
            ((taps_n, channels), bf16),
            ((rows, channels), bf16),
            ((taps_n, channels), f32),
            ((1, channels), f32),
        ],
        (q, ks, v, dy, save, dstate, rate_row, seg_col, seg_row, entry, key, halo, taps, age, rem, state_in),
        scratch=[
            pltpu.VMEM((total, channels), f32),
            pltpu.VMEM((8, total, channels), f32),
            pltpu.VMEM((total + taps_n, channels), f32),
            pltpu.VMEM((8, total + taps_n, channels), f32),
            pltpu.VMEM((taps_n, 8, channels), f32),
        ],
        mib=26,
        us=18.0,
    )


def attend_kernel(resume, finish, lim_ref, q_ref, kv_ref, segc_ref, segr_ref, *refs):
    if resume:
        acc_in, col_in = refs[:2]
        refs = refs[2:]
    rows, channels = q_ref.shape
    n_heads = channels // HEAD_DIM
    heads = head_masks(CHUNK, channels)
    row = lax.broadcasted_iota(jnp.int32, (CHUNK, CHUNK), 0)
    lane = lax.broadcasted_iota(jnp.int32, (CHUNK, CHUNK), 1)
    stat_lane = lax.broadcasted_iota(jnp.int32, (CHUNK, 128), 1)
    for b in range(rows // CHUNK):
        sl = slice(b * CHUNK, (b + 1) * CHUNK)
        low, high, diagonal = lim_ref[0, b], lim_ref[1, b], lim_ref[2, b]
        q = q_ref[sl, :]
        seg_c = segc_ref[sl, :]
        qh = [jnp.where(hm, q, jnp.zeros_like(q)) for hm in heads]

        def step(t, carry):
            at = pl.multiple_of(t * CHUNK, CHUNK)
            keys = kv_ref[pl.ds(at, CHUNK), 0:channels]
            values = kv_ref[pl.ds(at, CHUNK), channels : 2 * channels]
            seg_r = segr_ref[:, pl.ds(at, CHUNK)]
            allowed = (row >= lane + (t - diagonal) * CHUNK) & (seg_c == seg_r)
            new = []
            for h in range(n_heads):
                top, total, acc = carry[h]
                z = jnp.where(allowed, nt(qh[h], keys) * scale, masked_low)
                new_top = jnp.maximum(top, jnp.max(z, axis=1, keepdims=True))
                shrink = jnp.exp(top - new_top)
                e = jnp.where(allowed, jnp.exp(z - new_top), 0.0)
                total = total * shrink + jnp.sum(e, axis=1, keepdims=True)
                acc = acc * shrink + nn(e.astype(bf16), values)
                new.append((new_top, total, acc))
            return tuple(new)

        if resume:
            col = col_in[sl, :]
            held = acc_in[sl, :]
            start = tuple((col[:, h : h + 1], col[:, 8 + h : 9 + h], held) for h in range(n_heads))
        else:
            start = tuple(
                (
                    jnp.full((CHUNK, 1), masked_low, f32),
                    jnp.zeros((CHUNK, 1), f32),
                    jnp.zeros((CHUNK, channels), f32),
                )
                for _ in range(n_heads)
            )
        state = lax.fori_loop(low, high + 1, step, start)
        out = jnp.zeros((CHUNK, channels), f32)
        stats = jnp.zeros((CHUNK, 128), f32)
        for h in range(n_heads):
            top, total, acc = state[h]
            out = jnp.where(heads[h], acc / total if finish else acc, out)
            stats = jnp.where(stat_lane == h, top, stats)
            stats = jnp.where(stat_lane == 8 + h, total, stats)
        refs[0][sl, :] = out
        if finish:
            refs[1][b, :, :] = stats.T[0:16, :]
            refs[2][sl, :] = out.astype(bf16)
        else:
            refs[1][sl, :] = stats


def attend(lim, q, kv, seg_col, seg_tiles, held=(), finish=True):
    rows, channels = q.shape
    if finish:
        outs = [((rows, channels), f32), ((rows // CHUNK, 16, CHUNK), f32), ((rows, channels), bf16)]
    else:
        outs = [((rows, channels), f32), ((rows, 128), f32)]
    return kernel_call(
        functools.partial(attend_kernel, bool(held), finish),
        outs,
        (q, kv, seg_col, seg_tiles, *held),
        scalars=(lim,),
        mib=16 + kv.shape[0] // 512,
        us=5.0,
    )


def attend_back_kernel(
    resume, lim_ref, q_ref, kv_ref, do_ref, o_ref, stat_ref, qseg_ref, kseg_ref, *refs
):
    dq_ref, dkv_ref, acc = refs[-3:]
    rows, channels = q_ref.shape
    n_heads = channels // HEAD_DIM
    heads = head_masks(CHUNK, channels)
    row = lax.broadcasted_iota(jnp.int32, (CHUNK, CHUNK), 0)
    lane = lax.broadcasted_iota(jnp.int32, (CHUNK, CHUNK), 1)
    stat_lane = lax.broadcasted_iota(jnp.int32, (CHUNK, 128), 1)
    acc[...] = jnp.zeros(acc.shape, f32)
    for b in range(rows // CHUNK):
        sl = slice(b * CHUNK, (b + 1) * CHUNK)
        low, high, diagonal = lim_ref[0, b], lim_ref[1, b], lim_ref[2, b]
        q = q_ref[sl, :]
        do = do_ref[sl, :].astype(f32)
        o = o_ref[sl, :]
        seg_q = qseg_ref[:, sl]
        zero = jnp.zeros_like(q)
        qh = [jnp.where(hm, q, zero) for hm in heads]
        cols = jnp.zeros((CHUNK, 128), f32)
        for h in range(n_heads):
            inner = jnp.sum(jnp.where(heads[h], do * o, 0.0), axis=1, keepdims=True)
            cols = jnp.where(stat_lane == h, inner, cols)
        inner_rows = cols.T
        totals = stat_ref[b, 8:16, :]
        inv_cols = jnp.concatenate([1.0 / jnp.maximum(totals, 1e-30), jnp.zeros((120, CHUNK), f32)]).T
        wh = []
        for h in range(n_heads):
            inv = inv_cols[:, h : h + 1]
            wh.append(jnp.where(heads[h], do * inv, 0.0).astype(bf16))

        def step(t, dq):
            at = pl.multiple_of(t * CHUNK, CHUNK)
            keys = kv_ref[pl.ds(at, CHUNK), 0:channels]
            values = kv_ref[pl.ds(at, CHUNK), channels : 2 * channels]
            seg_k = kseg_ref[pl.ds(at, CHUNK), :]
            allowed = (lane >= row + (t - diagonal) * CHUNK) & (seg_k == seg_q)
            dk = jnp.zeros((CHUNK, channels), f32)
            dv = jnp.zeros((CHUNK, channels), f32)
            for h in range(n_heads):
                top = stat_ref[b, h : h + 1, :]
                total = stat_ref[b, 8 + h : 9 + h, :]
                z = jnp.where(allowed, nt(keys, qh[h]) * scale, masked_low)
                e = jnp.where(allowed, jnp.exp(z - top), 0.0)
                dp = nt(values, wh[h])
                dz = (e * (dp - inner_rows[h : h + 1, :] / total)).astype(bf16)
                dk = dk + nn(dz, qh[h])
                dv = dv + nn(e.astype(bf16), wh[h])
                dq = dq + jnp.where(heads[h], tn(dz, keys), 0.0)
            acc[0, pl.ds(at, CHUNK), :] += dk
            acc[1, pl.ds(at, CHUNK), :] += dv
            return dq

        dq = lax.fori_loop(low, high + 1, step, jnp.zeros((CHUNK, channels), f32))
        dq = dq * scale
        if resume:
            dq = dq + refs[0][sl, :]
        dq_ref[sl, :] = dq.astype(dq_ref.dtype)
    dkv_ref[:, 0:channels] = (acc[0] * scale).astype(dkv_ref.dtype)
    dkv_ref[:, channels : 2 * channels] = acc[1].astype(dkv_ref.dtype)


def attend_back(lim, q, kv, do, o, stats, q_tiles, key_col, dq_type, dkv_type, held=()):
    rows, channels = q.shape
    return kernel_call(
        functools.partial(attend_back_kernel, bool(held)),
        [((rows, channels), dq_type), ((kv.shape[0], 2 * channels), dkv_type)],
        (q, kv, do, o, stats, q_tiles, key_col, *held),
        scalars=(lim,),
        scratch=[pltpu.VMEM((2, kv.shape[0], channels), f32)],
        mib=18 + kv.shape[0] // 256,
        us=7.0,
    )


def by_rows(rows, step, body):
    def one(i, carry):
        body(pl.ds(pl.multiple_of(i * step, step), step))
        return carry

    lax.fori_loop(0, rows // step, one, 0)


def norm_kernel(n_add, x_ref, *refs):
    adds, gain_ref, outs = refs[:n_add], refs[n_add], refs[n_add + 1 :]

    def body(at):
        x = x_ref[at, :].astype(f32)
        for a in adds:
            x = x + a[at, :].astype(f32)
        center = jnp.mean(x, axis=1, keepdims=True)
        moved = x - center
        inv = lax.rsqrt(jnp.mean(moved * moved, axis=1, keepdims=True) + epsilon)
        outs[0][at, :] = x
        outs[1][at, :] = (moved * inv * gain_ref[...]).astype(bf16)

    by_rows(x_ref.shape[0], 384, body)


def norm(x, adds, gain):
    shape = x.shape
    return kernel_call(
        functools.partial(norm_kernel, len(adds)),
        [(shape, f32), (shape, bf16)],
        (x, *adds, gain.reshape(1, -1)),
        us=2.0,
    )


def norm_back_kernel(n_add, x_ref, grad_ref, *refs):
    adds, gain_ref, outs = refs[:n_add], refs[n_add], refs[n_add + 1 :]

    def body(at):
        x = x_ref[at, :]
        center = jnp.mean(x, axis=1, keepdims=True)
        moved = x - center
        inv = lax.rsqrt(jnp.mean(moved * moved, axis=1, keepdims=True) + epsilon)
        unit = moved * inv
        d = adds[0][at, :].astype(f32)
        for a in adds[1:]:
            d = d + a[at, :].astype(f32)
        d = d * gain_ref[...]
        mean_d = jnp.mean(d, axis=1, keepdims=True)
        mean_du = jnp.mean(d * unit, axis=1, keepdims=True)
        grad = grad_ref[at, :].astype(f32) + inv * (d - mean_d - unit * mean_du)
        outs[0][at, :] = grad
        outs[1][at, :] = grad.astype(bf16)

    by_rows(x_ref.shape[0], 384, body)


def norm_back(x, grad, adds, gain):
    shape = x.shape
    return kernel_call(
        functools.partial(norm_back_kernel, len(adds)),
        [(shape, f32), (shape, bf16)],
        (x, grad, *adds, gain.reshape(1, -1)),
        us=2.0,
    )


def gelu_both(u):
    inner = 0.7978845608028654 * (u + 0.044715 * (u * u * u))
    t = jnp.tanh(inner)
    half = 0.5 * (1.0 + t)
    slope = half + 0.5 * u * (1.0 - t * t) * (0.7978845608028654 * (1.0 + 0.134145 * (u * u)))
    return u * half, slope


def gather_rows(refs, to):
    size = refs[0].shape[0]
    for i, ref in enumerate(refs):
        to[i * size : (i + 1) * size, :] = ref[...]


def feed_forward_kernel(n, hid, *refs):
    ms, w_ref = refs[:n], refs[n]
    parts, r_ref, slope_ref, rows, up = refs[n + 1 : 2 * n + 1], *refs[2 * n + 1 :]
    size = ms[0].shape[0]
    gather_rows(ms, rows)
    up[...] = nn(rows[...], w_ref[:, 0:hid])

    def body(at):
        r, slope = gelu_both(up[at, :])
        r_ref[at, :] = r.astype(bf16)
        slope_ref[at, :] = slope.astype(bf16)

    by_rows(n * size, 32, body)
    up[...] = nt(r_ref[...], w_ref[:, hid : 2 * hid])
    for i in range(n):
        parts[i][...] = up[i * size : (i + 1) * size, :].astype(bf16)


def feed_forward(ms, w, hid):
    n, size, model = len(ms), ms[0].shape[0], ms[0].shape[1]
    out = kernel_call(
        functools.partial(feed_forward_kernel, n, hid),
        [((size, model), bf16)] * n + [((n * size, hid), bf16)] * 2,
        (*ms, w),
        scratch=[pltpu.VMEM((n * size, model), bf16), pltpu.VMEM((n * size, hid), f32)],
        us=5.0,
    )
    return out[:n], out[n], out[n + 1]


def feed_mid_kernel(n, hid, *refs):
    ms, gs, w_ref, gain_ref = refs[:n], refs[n : 2 * n], refs[2 * n], refs[2 * n + 1]
    outs = refs[2 * n + 2 :]
    parts, r_ref, du_ref, gsum_ref, rows, up, dr = outs[:n], *outs[n:]
    size = ms[0].shape[0]
    gather_rows(ms, rows)
    up[...] = nn(rows[...], w_ref[:, 0:hid])
    gather_rows(gs, rows)
    dr[...] = nn(rows[...], w_ref[:, hid : 2 * hid])

    def body(at):
        r, slope = gelu_both(up[at, :])
        r_ref[at, :] = r.astype(bf16)
        du_ref[at, :] = (dr[at, :] * slope).astype(bf16)

    by_rows(n * size, 32, body)
    finish_back(ms, du_ref, w_ref, gain_ref, parts, gsum_ref, up, hid)


def finish_back(ms, du_ref, w_ref, gain_ref, parts, gsum_ref, part, hid):
    size = ms[0].shape[0]
    part[...] = nt(du_ref[...], w_ref[:, 0:hid])
    gsum = jnp.zeros(gsum_ref.shape, f32)
    for i, m in enumerate(ms):
        own = part[i * size : (i + 1) * size, :]
        parts[i][...] = own.astype(bf16)
        gsum = gsum + jnp.sum(own * m[...].astype(f32), axis=0, keepdims=True)
    gsum_ref[...] = gsum / gain_ref[...]


def feed_mid(ms, gs, w, hid, gain):
    n, size, model = len(ms), ms[0].shape[0], ms[0].shape[1]
    out = kernel_call(
        functools.partial(feed_mid_kernel, n, hid),
        [((size, model), bf16)] * n + [((n * size, hid), bf16)] * 2 + [((1, model), f32)],
        (*ms, *gs, w, gain.reshape(1, -1)),
        scratch=[pltpu.VMEM((n * size, model), bf16)] + [pltpu.VMEM((n * size, hid), f32)] * 2,
        mib=16,
        us=6.0,
    )
    return out[:n], out[n], out[n + 1], out[n + 2]


def feed_back_kernel(n, hid, *refs):
    ms, gs, slope_ref, w_ref, gain_ref = refs[:n], refs[n : 2 * n], refs[2 * n], refs[2 * n + 1], refs[2 * n + 2]
    outs = refs[2 * n + 3 :]
    parts, du_ref, gsum_ref, rows, dr = outs[:n], *outs[n:]
    gather_rows(gs, rows)
    dr[...] = nn(rows[...], w_ref[:, hid : 2 * hid])

    def body(at):
        du_ref[at, :] = (dr[at, :] * slope_ref[at, :].astype(f32)).astype(bf16)

    by_rows(dr.shape[0], 32, body)
    finish_back(ms, du_ref, w_ref, gain_ref, parts, gsum_ref, dr, hid)


def feed_back(ms, gs, slope, w, hid, gain):
    n, size, model = len(ms), ms[0].shape[0], ms[0].shape[1]
    out = kernel_call(
        functools.partial(feed_back_kernel, n, hid),
        [((size, model), bf16)] * n + [((n * size, hid), bf16), ((1, model), f32)],
        (*ms, *gs, slope, w, gain.reshape(1, -1)),
        scratch=[pltpu.VMEM((n * size, model), bf16), pltpu.VMEM((n * size, hid), f32)],
        us=4.0,
    )
    return out[:n], out[n], out[n + 1]


def add_kernel(a_ref, b_ref, out_ref):
    def body(at):
        out_ref[at, :] = (a_ref[at, :].astype(f32) + b_ref[at, :].astype(f32)).astype(bf16)

    by_rows(a_ref.shape[0], 192, body)


def add(a, b):
    return kernel_call(add_kernel, [(a.shape, bf16)], (a, b), mib=4, us=1.0)[0]


def places(core_ref, halves, n, size):
    if halves == 1:
        return [pl.ds(i * size, size) for i in range(n)]
    core, half = core_ref[0], n // 2 * size
    own = [pl.ds(pl.multiple_of(core * half + i * size, size), size) for i in range(n // 2)]
    return own + [pl.ds(pl.multiple_of((1 - core) * half + i * size, size), size) for i in range(n // 2)]


def project_kernel(halves, n, core_ref, *refs):
    ns, w_ref, outs = refs[:n], refs[n], refs[n + 1 :]
    size = ns[0].shape[0]
    for i, to in enumerate(places(core_ref, halves, n, size)):
        x = ns[i][...]
        for j in range(3):
            outs[j][to, :] = nn(x, w_ref[j]).astype(bf16)
        outs[3][to, :] = x
    if len(outs) > 4:
        channels = outs[0].shape[1]
        outs[4][:, 0:channels] = outs[1][...]
        outs[4][:, channels : 2 * channels] = outs[2][...]


def project(core, halves, ns, w, pair=False):
    n, size, model, channels = len(ns), ns[0].shape[0], ns[0].shape[1], w.shape[2]
    return kernel_call(
        functools.partial(project_kernel, halves, n),
        [((n * size, channels), bf16)] * 3
        + [((n * size, model), bf16)]
        + [((n * size, 2 * channels), bf16)] * pair,
        (*ns, w),
        scalars=(core,),
        us=3.0,
    )


def out_kernel(halves, n, index, state, core_ref, y_ref, w_ref, *refs):
    if state:
        sin_ref = refs[4]
        parts, yb_ref = refs[5 : 5 + n], refs[5 + n]
        qr = rising(*refs[:4])
        yb_ref[...] = (y_ref[...] + nt(qr, expand(sin_ref[...]).astype(bf16))).astype(bf16)
    else:
        parts, yb_ref = refs[:n], y_ref
    size = parts[0].shape[0]
    for i, to in enumerate(places(core_ref, halves, n, size)):
        parts[i][...] = nt(yb_ref[to, :], w_ref[index]).astype(bf16)


def project_out(core, halves, n, y, w, index, state=()):
    size, model = y.shape[0] // n, w.shape[1]
    outs = [((size, model), bf16)] * n
    if state:
        outs.append((y.shape, bf16))
    return kernel_call(
        functools.partial(out_kernel, halves, n, index, bool(state)),
        outs,
        (y, w, *state),
        scalars=(core,),
        us=2.0,
    )


def out_back_kernel(halves, n, index, state, core_ref, *refs):
    gs, w_ref = refs[:n], refs[n]
    refs = refs[n + 1 :]
    if state:
        rising_refs = refs[:4]
        refs = refs[4:]
    dy_ref, ordered_ref = refs[0], refs[1]
    size = gs[0].shape[0]
    for i, to in enumerate(places(core_ref, halves, n, size)):
        g = gs[i][...]
        dy_ref[to, :] = nn(g, w_ref[index]).astype(bf16)
        ordered_ref[to, :] = g
    if state:
        refs[2][...] = compact(tn(dy_ref[...], rising(*rising_refs)))


def out_back(core, halves, gs, w, index, state=()):
    n, size, model, channels = len(gs), gs[0].shape[0], gs[0].shape[1], w.shape[2]
    outs = [((n * size, channels), bf16), ((n * size, model), bf16)]
    if state:
        outs.append(((HEAD_DIM, channels), bf16))
    return kernel_call(
        functools.partial(out_back_kernel, halves, n, index, bool(state)),
        outs,
        (*gs, w, *state),
        scalars=(core,),
        us=2.0,
    )


def project_back_kernel(halves, n, kind, count, core_ref, dq_ref, *refs):
    others = refs[:count]
    w_ref, n_ref, gain_ref = refs[count : count + 3]
    outs = refs[count + 3 :]
    parts, cat_ref, gsum_ref = outs[:n], outs[n], outs[n + 1]
    rows, channels = dq_ref.shape
    cat_ref[:, 0:channels] = dq_ref[...]
    if kind == "halo":
        dk_ref, dv_ref, extra_ref = others
        cut = rows - extra_ref.shape[0]
        cat_ref[0:cut, channels : 2 * channels] = dk_ref[0:cut, :].astype(bf16)
        cat_ref[cut:rows, channels : 2 * channels] = (
            dk_ref[cut:rows, :] + extra_ref[...].astype(f32)
        ).astype(bf16)
        cat_ref[:, 2 * channels : 3 * channels] = dv_ref[...].astype(bf16)
    else:
        total = others[0][...].astype(f32)
        for other in others[1:]:
            total = total + other[...].astype(f32)
        cat_ref[:, channels : 3 * channels] = total.astype(bf16)
    size = parts[0].shape[0]
    gsum_ref[...] = jnp.zeros(gsum_ref.shape, f32)
    for i, to in enumerate(places(core_ref, halves, n, size)):
        part = sum(nt(cat_ref[to, j * channels : (j + 1) * channels], w_ref[j]) for j in range(3))
        parts[i][...] = part.astype(bf16)
        gsum_ref[...] += jnp.sum(part * n_ref[to, :].astype(f32), axis=0, keepdims=True)
    gsum_ref[...] = gsum_ref[...] / gain_ref[...]


def project_back(core, halves, n, kind, dq, others, w, normed, gain):
    rows, channels = dq.shape
    size, model = rows // n, normed.shape[1]
    out = kernel_call(
        functools.partial(project_back_kernel, halves, n, kind, len(others)),
        [((size, model), bf16)] * n + [((rows, 3 * channels), bf16), ((1, model), f32)],
        (dq, *others, w, normed, gain.reshape(1, -1)),
        scalars=(core,),
        us=3.0,
    )
    return out[:n], out[n], out[n + 1]


def at_rows(value, start, count):
    return lax.dynamic_slice_in_dim(value, start, count, 0)


def tie(*values):
    return lax.optimization_barrier(values)


class Rows:
    halves = 1
    chunks = 1
    grad_type = f32

    def __init__(self):
        self.blocks = lax.axis_size("ctx")
        self.place = lax.axis_index("ctx")
        self.core = self.place

    def enter(self, rows):
        return rows

    def leave_start(self, rows):
        return rows

    def leave_end(self, rows, there):
        return rows

    def spread(self, rows):
        return [rows]

    def half_sum(self, parts):
        return parts[0]

    def total(self, value):
        return [lax.psum(value, "tp")]

    def local(self, value):
        return value

    def assemble(self, share):
        return lax.all_gather(share, "fsdp", axis=1, tiled=True)

    def setup(self, ids, taps_n, channels):
        row = ids
        ids = ids[0]
        n, rows = self.blocks, ids.shape[0]
        halo = lax.ppermute(ids[rows - taps_n :].astype(bf16), "ctx", [(i, i + 1) for i in range(n - 1)])
        ext = jnp.concatenate([halo.astype(jnp.int32), ids])
        at = jnp.arange(ext.shape[0], dtype=jnp.int32)
        same = ext[:, None] == ext[None, :]
        age = jnp.sum((same & (at[None, :] < at[:, None])).astype(jnp.int32), axis=1)
        rem = jnp.sum((same & (at[None, :] > at[:, None])).astype(jnp.int32), axis=1)
        age, rem = [jnp.broadcast_to(v[:, None], (ext.shape[0], channels)) for v in (age, rem)]
        key_ids = lax.all_gather(ids.astype(bf16), "ctx", axis=0, tiled=True).astype(jnp.int32)
        count = rows // CHUNK
        high = self.place * count + jnp.arange(count, dtype=jnp.int32)
        firsts = ids[::CHUNK]
        low = jnp.sum((key_ids[None, :] < firsts[:, None]).astype(jnp.int32), axis=1) // CHUNK
        limits = jnp.stack([low, high, high])
        entry = ext[taps_n - 1].reshape(1, 1)
        return row, ids[:, None], entry, age, rem, (limits, ids[:, None], row, key_ids[:, None], key_ids[None])

    def from_previous(self, value):
        n = self.blocks
        return lax.ppermute(value, "ctx", [(i, i + 1) for i in range(n - 1)])

    def to_previous(self, value):
        n = self.blocks
        return lax.ppermute(value, "ctx", [(i + 1, i) for i in range(n - 1)])

    def state_before(self, factor, state):
        factors = lax.all_gather(factor.astype(bf16), "ctx").astype(f32)
        states = lax.all_gather(state, "ctx")

        def one(hop, held):
            return states[hop].astype(f32) + factors[hop] * held

        held = lax.fori_loop(0, self.place, one, jnp.zeros(state.shape, f32))
        return held.astype(bf16)

    def grad_after(self, factor, dstate):
        factors = lax.all_gather(factor.astype(bf16), "ctx").astype(f32)
        states = lax.all_gather(dstate, "ctx")

        def one(hop, held):
            at = self.blocks - 1 - hop
            return states[at].astype(f32) + factors[at] * held

        held = lax.fori_loop(0, self.blocks - 1 - self.place, one, jnp.zeros(dstate.shape, f32))
        return held.astype(bf16)

    def attend(self, setup, q, kv):
        limits, col, _, _, key_tiles = setup
        kv = lax.all_gather(kv, "ctx", axis=0, tiled=True)
        return attend(limits, q, kv, col, key_tiles), kv

    def attend_back(self, setup, kept, q, kv, grad, mixed, stats, wait):
        limits, _, tiles, key_col, _ = setup
        dq, dkv = attend_back(limits, q, kept, grad, mixed, stats, tiles, key_col, bf16, bf16)
        return dq, [lax.psum_scatter(dkv, "ctx", scatter_dimension=0, tiled=True)], wait

    def scatter(self, value):
        return [lax.psum_scatter(value, "fsdp", scatter_dimension=0, tiled=True)]

    def scattered(self, parts):
        return parts[0]

    def to_owner(self, value):
        return lax.psum(value, "ctx")

    def owned(self, value, got):
        return got

    def over_places(self, value):
        return lax.psum(value, ("ctx", "tp"))


class Pairs(Rows):
    halves = 2
    chunks = 1
    grad_type = bf16

    def __init__(self):
        self.blocks = 2
        self.core = lax.axis_index("ctx")
        self.chip = lax.axis_index("tp")
        self.place = self.chip // 2
        self.home = self.core == self.place

    def send(self, value, pairs):
        number = [(4 * c + t, 4 * d + u) for (c, t), (d, u) in pairs]
        return lax.ppermute(value, ("ctx", "tp"), number)

    def swap(self, value):
        return lax.ppermute(value, "ctx", [(0, 1), (1, 0)])

    def neighbour(self, value):
        return lax.ppermute(value, "tp", [(0, 1), (1, 0), (2, 3), (3, 2)])

    def across(self, value):
        return lax.ppermute(value, "tp", [(0, 2), (2, 0), (1, 3), (3, 1)])

    def from_home_core(self, value):
        return self.send(value, [((t // 2, t), (1 - t // 2, t)) for t in range(4)])

    def enter(self, rows):
        half = rows.shape[0] // 2
        got = self.from_home_core(at_rows(rows, (1 - self.core) * half, half))
        return jnp.where(self.home, at_rows(rows, self.core * half, half), got)

    def setup(self, ids, taps_n, channels):
        other = self.swap(ids)
        own = jnp.where(self.home, ids, other)
        first = jnp.where(self.core == 0, ids, other)
        before = jnp.where(self.place == 1, first, 0)
        col, before_col, entry, age, rem, own_limits, prev_limits = setup_ids(own, before, taps_n, channels)
        return own, col, entry, age, rem, (own_limits, prev_limits, col, before_col, own, before)

    def in_order(self, own, other):
        first = self.core == 0
        return jnp.concatenate([jnp.where(first, own, other), jnp.where(first, other, own)])

    def leave_start(self, rows):
        return self.across(rows)

    def leave_end(self, rows, there):
        got = self.swap(jnp.where(self.home, there, rows))
        return self.in_order(jnp.where(self.home, rows, there), got)

    def spread(self, rows):
        return [rows, self.swap(rows)]

    def half_sum(self, parts):
        return add(parts[0], self.swap(parts[1]))

    def total(self, value):
        return [value, self.neighbour(value)]

    def local(self, value):
        got = self.send(
            value, [((c, 2 * c + e), (c, 2 - 2 * c + e)) for c in range(2) for e in range(2)]
        )
        return jnp.where(self.home, value, got)

    def around(self, value):
        return [lax.ppermute(value, "fsdp", [(i, i ^ k) for i in range(4)]) for k in (1, 2, 3)]

    def assemble(self, share):
        place, size = lax.axis_index("fsdp"), share.shape[1]
        whole = jnp.zeros((share.shape[0], 4 * size, share.shape[2]), share.dtype)
        for k, part in enumerate([share] + self.around(share)):
            whole = lax.dynamic_update_slice_in_dim(whole, part, (place ^ k) * size, 1)
        return whole

    def from_previous(self, value):
        return self.send(value, [((c, t), (c, t + 2)) for c in range(2) for t in range(2)])

    def to_previous(self, value):
        return self.send(value, [((c, t + 2), (c, t)) for c in range(2) for t in range(2)])

    def state_before(self, factor, state):
        return self.from_previous(state)

    def grad_after(self, factor, dstate):
        return self.to_previous(dstate)

    def attend(self, setup, q, kv):
        own_limits, prev_limits, col, _, tiles, prev_tiles = setup
        before = self.from_previous(kv)
        held = attend(own_limits, q, kv, col, tiles, finish=False)
        return attend(prev_limits, q, before, col, prev_tiles, held), before

    def attend_back(self, setup, before, q, kv, grad, mixed, stats, wait):
        own_limits, prev_limits, col, prev_col, tiles, _ = setup
        dq, dkv_prev = attend_back(prev_limits, q, before, grad, mixed, stats, tiles, prev_col, f32, bf16)
        got = self.to_previous(dkv_prev)
        dq, *wait = tie(dq, *wait)
        dq, dkv = attend_back(own_limits, q, kv, grad, mixed, stats, tiles, col, bf16, f32, (dq,))
        return dq, [dkv, got], wait

    def scatter(self, value):
        place = lax.axis_index("fsdp")
        size = value.shape[0] // 4
        parts = [at_rows(value, place * size, size)]
        for k in (1, 2, 3):
            part = at_rows(value, (place ^ k) * size, size)
            parts.append(lax.ppermute(part, "fsdp", [(i, i ^ k) for i in range(4)]))
        return parts

    def scattered(self, parts):
        return sum(part.astype(f32) for part in parts).astype(bf16)

    def to_owner(self, value):
        return self.send(
            value, [((c, 2 - 2 * c + e), (c, 2 * c + e)) for c in range(2) for e in range(2)]
        )

    def owned(self, value, got):
        value = (value.astype(f32) + got.astype(f32)).astype(bf16)
        return jnp.where(self.home, value, self.from_home_core(value))

    def over_places(self, value):
        for step in (self.swap, self.neighbour, self.across):
            value = (value.astype(f32) + step(value).astype(f32)).astype(bf16)
        return value


def dot_tn(a, b):
    return jnp.einsum("tf,td->fd", a, b, preferred_element_type=f32).astype(bf16)


def feed_shares(reduced):
    width = reduced.shape[1] // 2
    return reduced[:, :width].astype(f32), reduced[:, width:].T.astype(f32)


def mixer_shares(reduced, channels):
    parts = [reduced[:, j * channels : (j + 1) * channels].astype(f32) for j in range(3)]
    return jnp.stack(parts), reduced[:, 3 * channels : 4 * channels].T.astype(f32)


def run(plan, inputs, cotangent, segments, gains, last_gain, in_weight, h3_out, attn_out, up_weight, down_weight, shift_taps, decay_rate):
    halves, chunks = plan.halves, plan.chunks
    pieces = halves * chunks
    slots = lax.axis_size("fsdp")
    hid = up_weight.shape[2]
    channels = h3_out.shape[0]
    taps_n = shift_taps.shape[0]
    share = h3_out.shape[1]
    core = plan.core.astype(jnp.int32).reshape(1)

    def split(value):
        size = value.shape[0] // chunks
        return [value[i * size : (i + 1) * size] for i in range(chunks)]

    def by_piece(spreads):
        return [s[i] for i in range(halves) for s in spreads]

    def by_chunk(parts):
        return [[parts[i * chunks + j] for i in range(halves)] for j in range(chunks)]

    def joined(spreads):
        return jnp.concatenate([piece for s in spreads for piece in s])

    def norms(xs, adds, gain):
        out = [norm(x, a, gain) for x, a in zip(xs, adds)]
        return [o[0] for o in out], [plan.spread(o[1]) for o in out]

    def norm_backs(xs, grads, adds, gain):
        out = [norm_back(x, g, a, gain) for x, g, a in zip(xs, grads, adds)]
        return [o[0] for o in out], [plan.spread(o[1]) for o in out]

    def totals(parts, *others):
        sums = [plan.half_sum(p) for p in parts]
        sums[-1], *others = tie(sums[-1], *others)
        adds = [plan.total(v) for v in sums]
        return (adds, *others) if others else adds

    def with_sums(adds, *others):
        adds[-1][-1], *others = tie(adds[-1][-1], *others)
        return others

    weights0 = plan.local(jnp.concatenate([in_weight[0], h3_out.T[None]]))
    xs = split(plan.enter(inputs[0]))
    seg_row, seg_col, entry, age, rem, setup = plan.setup(segments + 1, taps_n, channels)
    rows = seg_row.shape[1]
    small = jnp.concatenate([shift_taps, decay_rate.reshape(1, -1)])
    feed = [jnp.concatenate([up_weight[i], down_weight[i].T], axis=1) for i in range(2)]
    mix = jnp.concatenate([in_weight[1], attn_out.T[None]])
    x0, n0s = norms(xs, [[]] * chunks, gains[0])
    weights0, small, feed[0] = tie(weights0, small, feed[0])
    weights0 = plan.assemble(weights0)
    feed[0], mix = tie(plan.local(feed[0]), mix)
    small, mix = plan.local(small), plan.local(mix)
    weights0, age, rem = tie(weights0, age, rem)

    q0, k0, v0, n0 = project(core, halves, by_piece(n0s), weights0)
    k0, small = tie(k0, small)
    halo = plan.from_previous(k0[rows - taps_n :])
    halo, feed[0], feed[1] = tie(halo, feed[0], feed[1])
    feed0 = lax.all_gather(feed[0], "fsdp", axis=0, tiled=True)
    feed[1] = plan.local(feed[1])
    taps, rate_row = small[:taps_n], small[taps_n:]
    factor = jnp.exp(-rate_row * rows) * (entry == seg_row[:, rows - 1 :]).astype(f32)
    ks, state_end, y0, saved = h3_forward(k0, halo, q0, v0, taps, rate_row, age, seg_col, seg_row)
    state_in = plan.state_before(factor, state_end)
    state_in, mix = tie(state_in, mix)
    mix1 = lax.all_gather(mix, "fsdp", axis=1, tiled=True)
    *parts, y0 = project_out(core, halves, pieces, y0, weights0, 3, (q0, rate_row, seg_col, entry, state_in))
    adds = totals(by_chunk(parts))
    (feed0,) = with_sums(adds, feed0)
    x1, m0s = norms(x0, adds, gains[1])
    out = [feed_forward(m, feed0, hid) for m in m0s]
    parts, r0, slope0 = [[o[i] for o in out] for i in range(3)]
    x2, n2s = norms(x1, totals(parts), gains[2])

    n2s[0][0], g_in, feed[1] = tie(n2s[0][0], cotangent[0], feed[1])
    feed1 = lax.all_gather(feed[1], "fsdp", axis=0, tiled=True)
    gs = split(plan.enter(g_in))
    flat = [p for g in gs for p in plan.spread(g)]
    mix1, *flat = tie(mix1, *flat)
    g_ins = [flat[halves * i : halves * (i + 1)] for i in range(chunks)]

    q2, _, _, n2, kv2 = project(core, halves, by_piece(n2s), mix1, True)
    (mixed, stats, mixed_bf), kept = plan.attend(setup, q2, kv2)
    parts = project_out(core, halves, pieces, mixed_bf, mix1, 3)
    x3, m1s = norms(x2, totals(by_chunk(parts)), last_gain)

    out = [feed_mid(m, g, feed1, hid, last_gain) for m, g in zip(m1s, g_ins)]
    parts, r1, du1, gain3 = [[o[i] for o in out] for i in range(4)]
    adds, r1, du1, m1s, g_ins = totals(parts, r1, du1, m1s, g_ins)
    size = r1[0].shape[0] // halves
    last = [
        [
            jnp.einsum(
                "tf,df->td", r[i * size : (i + 1) * size], feed1[:, hid:], preferred_element_type=f32
            ).astype(bf16)
            for i in range(halves)
        ]
        for r in r1
    ]
    feed1_grad = jnp.concatenate(
        [
            dot_tn(joined(m1s), jnp.concatenate(du1)),
            dot_tn(joined(g_ins), jnp.concatenate(r1)),
        ],
        axis=1,
    )
    feed1_grad, *flat = with_sums(adds, feed1_grad, *[p for s in last for p in s])
    feed1_parts = plan.scatter(feed1_grad)
    last = totals([flat[halves * i : halves * (i + 1)] for i in range(chunks)])
    grads, gbs = norm_backs(x3, gs, adds, last_gain)
    dmixed, grad_bf1 = out_back(core, halves, by_piece(gbs), mix1, 3)
    flat = [a for adds in last for a in adds]
    dq, dkv, flat = plan.attend_back(setup, kept, q2, kv2, dmixed, mixed, stats, flat)
    dkv[0], *feed1_parts = tie(dkv[0], *feed1_parts)
    feed1_grad = plan.scattered(feed1_parts)
    count = len(flat) // chunks
    x4 = []
    for i in range(chunks):
        x4.append(x3[i] + sum(a.astype(f32) for a in flat[count * i : count * (i + 1)]))
    x4 = jnp.concatenate(x4).astype(bf16)
    dkv[-1], feed1_grad, x4 = tie(dkv[-1], feed1_grad, x4)
    parts, cat1, gain2 = project_back(core, halves, pieces, "sum", dq, dkv, mix1, n2, gains[2])
    adds, cat1, n2 = totals(by_chunk(parts), cat1, n2)
    mix1_grad = jnp.concatenate([dot_tn(n2, cat1), dot_tn(grad_bf1, mixed_bf)], axis=1)
    mix1_grad, feed1_grad, x4 = with_sums(adds, mix1_grad, feed1_grad, x4)
    x4_there = plan.leave_start(x4)
    mix1_parts = plan.scatter(mix1_grad)
    grads, gbs = norm_backs(x2, grads, adds, gains[2])

    out = [feed_back(m, g, s, feed0, hid, gains[1]) for m, g, s in zip(m0s, gbs, slope0)]
    parts, du0, gain1 = [[o[i] for o in out] for i in range(3)]
    adds, m0s, du0, gbs, r0 = totals(parts, m0s, du0, gbs, r0)
    feed0_grad = jnp.concatenate(
        [
            dot_tn(joined(m0s), jnp.concatenate(du0)),
            dot_tn(joined(gbs), jnp.concatenate(r0)),
        ],
        axis=1,
    )
    feed0_grad, x4_there, *mix1_parts = with_sums(adds, feed0_grad, x4_there, *mix1_parts)
    feed0_parts = plan.scatter(feed0_grad)
    grads, gbs = norm_backs(x1, grads, adds, gains[1])
    mix1_grad = plan.scattered(mix1_parts)
    dy, grad_bf0, dstate = out_back(
        core, halves, by_piece(gbs), weights0, 3, (q0, rate_row, seg_col, entry)
    )
    dstate_end = plan.grad_after(factor, dstate)
    dstate_end, feed1_grad, mix1_grad = tie(dstate_end, feed1_grad, mix1_grad)
    feed1_got, mix1_got = plan.to_owner(feed1_grad), plan.to_owner(mix1_grad)
    output = plan.leave_end(x4, x4_there)
    dq, dk, dhalo, dv, dtaps, drate = h3_back_call(
        q0, ks, v0, dy, saved, dstate_end, rate_row, seg_col, seg_row, entry, k0, halo, taps, age, rem, state_in
    )
    halo_grad = plan.to_previous(dhalo)
    dq, feed1_got, mix1_got, output, *feed0_parts = tie(dq, feed1_got, mix1_got, output, *feed0_parts)
    feed0_grad = plan.scattered(feed0_parts)
    feed0_got = plan.to_owner(feed0_grad)
    parts, cat0, gain0 = project_back(
        core, halves, pieces, "halo", dq, (dk, dv, halo_grad), weights0, n0, gains[0]
    )
    adds, cat0, n0, dtaps = totals(by_chunk(parts), cat0, n0, dtaps)

    mix0 = jnp.concatenate([dot_tn(n0, cat0), dot_tn(grad_bf0, y0)], axis=1)
    mix0 = mix0.reshape(slots, share, 4 * channels)
    taps_each = taps_n // slots
    small = jnp.concatenate(
        [
            dtaps.reshape(slots, taps_each, channels),
            jnp.pad(
                drate.reshape(-1, slots, HEAD_DIM // slots).transpose(1, 0, 2).reshape(slots, 1, -1),
                ((0, 0), (0, 0), (0, channels - channels // slots)),
            ),
            jnp.concatenate([gain0, sum(gain1), gain2, sum(gain3)]).reshape(4, slots, share).transpose(1, 0, 2),
        ],
        axis=1,
    ).astype(bf16)
    small = jnp.pad(small, ((0, 0), (0, (-small.shape[1]) % 32), (0, 3 * channels)))
    height = share + small.shape[1]
    mix0_parts = plan.scatter(jnp.concatenate([mix0, small], axis=1).reshape(slots * height, 4 * channels))
    grads = [
        norm_back(x, g, a, gains[0])[0].astype(plan.grad_type) for x, g, a in zip(x0, grads, adds)
    ]
    mix0 = plan.scattered(mix0_parts)
    mix0_got = plan.to_owner(mix0)
    grads[-1], feed1_got, mix1_got, feed0_got, gain_rows = tie(
        grads[-1], feed1_got, mix1_got, feed0_got, mix0[share + taps_each + 1 : share + taps_each + 5, :channels]
    )
    there = [plan.leave_start(g) for g in grads]
    gain_rows = plan.over_places(gain_rows).astype(f32)
    feed1 = plan.owned(feed1_grad, feed1_got)
    mix1 = plan.owned(mix1_grad, mix1_got)
    feed0 = plan.owned(feed0_grad, feed0_got)
    mix0 = plan.owned(mix0, mix0_got)
    input_grad = plan.leave_end(jnp.concatenate(grads), jnp.concatenate(there)).astype(f32)
    small = mix0[share:, :channels]
    in0_grad, out0_grad = mixer_shares(mix0[:share], channels)
    dtaps = small[:taps_each].astype(f32)
    drate = small[taps_each, : channels // slots].astype(f32).reshape(-1, HEAD_DIM // slots)
    up0_grad, down0_grad = feed_shares(feed0)
    up1_grad, down1_grad = feed_shares(feed1)
    in1_grad, out1_grad = mixer_shares(mix1, channels)
    return (
        output[None],
        input_grad[None],
        gain_rows[:3],
        gain_rows[3],
        jnp.stack([in0_grad, in1_grad]),
        out0_grad,
        out1_grad,
        jnp.stack([up0_grad, up1_grad]),
        jnp.stack([down0_grad, down1_grad]),
        dtaps,
        drate,
    )


def shards(*arguments):
    paired = lax.axis_size("ctx") == 2 and lax.axis_size("tp") == 4 and lax.axis_size("fsdp") == 4
    return run(Pairs() if paired else Rows(), *arguments)


def solution(mesh):
    placed = (
        P("fsdp", "ctx", None),
        P("fsdp", "ctx", None),
        P("fsdp", "ctx"),
        P(),
        P(),
        P(None, None, "fsdp", "tp"),
        P("tp", "fsdp"),
        P("tp", "fsdp"),
        P(None, "fsdp", "tp"),
        P(None, "tp", "fsdp"),
        P(None, "tp"),
        P("tp", None),
    )
    return jax.shard_map(
        shards,
        mesh=mesh,
        in_specs=placed,
        out_specs=(
            P("fsdp", "ctx", None),
            P("fsdp", "ctx", None),
            P(None, "fsdp"),
            P("fsdp"),
            P(None, None, "fsdp", "tp"),
            P("tp", "fsdp"),
            P("tp", "fsdp"),
            P(None, "fsdp", "tp"),
            P(None, "tp", "fsdp"),
            P("fsdp", "tp"),
            P("tp", "fsdp"),
        ),
        check_vma=False,
    )
```
